256 devices in a mesh: sample: 8 (over x, core), space: 32 (over y, z).
Axes of the slice: x: 4, y: 4, z: 8, core: 2. Of those that a mesh axis runs over, the one named last changes fastest.
Arguments:
- load_field: float32 [3, 128, 64, 128], P(None, 'space'), may hold values from -6 to 6
- density: float32 [128, 64, 128], P('space'), may hold values from 0.3 to 1
- mode_panels: bfloat16 [256, 32, 512], P('sample', 'space'), may hold values from -5 to 5
- mode_weight: float32 [256], replicated, may hold values from 0.01 to 0.12
- mode_germs: float32 [8, 256], replicated, may hold values from -5 to 5
Outputs:
- displacement: float32 [8, 3, 128, 64, 128], P('sample', None, 'space')
- gradient: float32 [128, 64, 128], P('space', 'sample')
- compliance: float32 [8], P('sample')
The draws below stay inside these ranges and needn't reach their ends.
All inputs are finite; a program needn't handle non-finite values.
Results may differ from the reference program's by a relative error of at most 0.00068.
Values sent between devices are 32-bit elements; how exact they have to be, the bound alone decides.
No kernel may reach another device: no remote copies, remote signals or barrier semaphores. Data moves between devices by JAX's collectives and lax.ppermute only.
A program may use at most 64 MiB of HBM per device.

```python
import math
import jax
import jax.numpy as jnp
import numpy as np
from jax import lax

NX = 64
NY = 128
MODES = 256
ITERS = 2
SAMPLES = 8
NZ = 128
CNX = 16
CNY = 32
CNZ = 32
CCELL = 512


def draw_load_field(key, part):
    key = jax.random.fold_in(key, 11)
    key_noise, key_comp = jax.random.split(key)
    z_pos = (jnp.arange(NZ).astype(jnp.float32) + 0.5) / NZ
    x_pos = (jnp.arange(NX).astype(jnp.float32) + 0.5) / NX
    y_pos = (jnp.arange(NY).astype(jnp.float32) + 0.5) / NY
    lower_half = jnp.arange(NZ) < NZ // 2
    comp_scale = jax.random.uniform(key_comp, (3,), jnp.float32, 0.6, 1.0) * jnp.array([1.0, -1.0, 1.0], jnp.float32)
    noise = jax.random.truncated_normal(key_noise, -4.0, 4.0, (3, NZ, NX, NY), jnp.float32)
    envelope = jnp.maximum(jnp.sin(2.0 * math.pi * z_pos), 0.0)
    plane = jnp.sin(math.pi * x_pos)[:, None] * jnp.sin(math.pi * y_pos)[None, :]
    rough_scale = jnp.where(lower_half, 0.4, 1.0)
    amplitude = 3.5
    smooth = amplitude * comp_scale[:, None, None, None] * envelope[None, :, None, None] * plane[None, None]
    total = smooth + rough_scale[None, :, None, None] * noise
    return jnp.clip(total, -6.0, 6.0).astype(jnp.float32)


def shard_levels(stream_key, dims, cuts, smallest, largest):
    factor_of, own = 1.0, jax.random.fold_in(stream_key, 6)
    for axis_at, blocks in cuts:
        steps = jnp.exp(jax.random.uniform(jax.random.fold_in(own, axis_at), (blocks,), jnp.float32, smallest / len(cuts), largest / len(cuts)))
        factor_of = factor_of * jnp.repeat(steps, dims[axis_at] // blocks).reshape([-1 if axis == axis_at else 1 for axis in range(len(dims))])
    return factor_of


def centred(rng, dims, deviation, bound, shards=(), held_as=jnp.bfloat16):
    level = shard_levels(rng, dims, shards, -0.22, 0.18) if shards else 1.0
    result = jax.random.normal(rng, dims, jnp.float32) * deviation * level
    return jnp.minimum(jnp.maximum(result, -bound), bound).astype(held_as)


def setup_inputs(seed: int = 0) -> dict:
    splits = jax.random.split(jax.random.key(seed), 6)
    load_field = draw_load_field(jax.random.fold_in(splits[5], 71), 0)
    density = jnp.clip(0.3 + 0.7 * jax.random.uniform(splits[1], (NZ, NX, NY), jnp.float32) ** shard_levels(splits[1], (NZ, NX, NY), ((0, 32),), -0.2, 0.2), 0.3, 1.0)
    mode_panels = centred(splits[2], (MODES, CNZ, CCELL), 1.0, 5.0, ((0, 8), (1, 32)))
    mode_weight = jnp.clip(jnp.exp(jax.random.uniform(splits[3], (MODES,), jnp.float32, math.log(0.01), math.log(0.12))), 0.01, 0.12)
    mode_germs = centred(splits[4], (SAMPLES, MODES), 1.0, 5.0, (), jnp.float32)
    return {"load_field": load_field, "density": density, "mode_panels": mode_panels, "mode_weight": mode_weight, "mode_germs": mode_germs}


highest_precision = lax.Precision.HIGHEST

def stiffness_table():
    poisson = 0.3
    lame_first = poisson / ((1.0 + poisson) * (1.0 - 2.0 * poisson))
    shear_modulus = 1.0 / (2.0 * (1.0 + poisson))
    moduli = np.zeros((6, 6))
    moduli[:3, :3] = lame_first
    for direction in range(3):
        moduli[direction, direction] += 2.0 * shear_modulus
        moduli[3 + direction, 3 + direction] = shear_modulus
    points = (0.5 - 0.5 / math.sqrt(3.0), 0.5 + 0.5 / math.sqrt(3.0))
    shear_pairs = ((0, 1), (1, 2), (0, 2))
    matrix = np.zeros((24, 24))
    for gauss_one in points:
        for gauss_two in points:
            for gauss_three in points:
                location = (gauss_one, gauss_two, gauss_three)
                strain = np.zeros((6, 24))
                for corner in range(8):
                    corner_bits = (corner >> 2 & 1, corner >> 1 & 1, corner & 1)
                    values = [location[direction] if corner_bits[direction] else 1.0 - location[direction] for direction in range(3)]
                    slopes = []
                    for direction in range(3):
                        slope_value = 1.0 if corner_bits[direction] else -1.0
                        for others in range(3):
                            if others != direction:
                                slope_value = slope_value * values[others]
                        slopes.append(slope_value)
                    for direction in range(3):
                        strain[direction, 3 * corner + direction] = slopes[direction]
                    for pair_index in range(3):
                        left_axis, right_axis = shear_pairs[pair_index]
                        strain[3 + pair_index, 3 * corner + left_axis] = slopes[right_axis]
                        strain[3 + pair_index, 3 * corner + right_axis] = slopes[left_axis]
                matrix = matrix + strain.T @ moduli @ strain / 8.0
    return matrix

def corner_offsets():
    return [(corner >> 2 & 1, corner >> 1 & 1, corner & 1) for corner in range(8)]

def hat_weights(fine_count, coarse_count, offset):
    fine_pos = (jnp.arange(fine_count).astype(jnp.float32) + 0.5) / 4.0 - 0.5 + offset
    coarse_pos = jnp.arange(coarse_count).astype(jnp.float32)
    return jnp.maximum(0.0, 1.0 - jnp.abs(fine_pos[:, None] - coarse_pos[None, :]))

def upsample(coarse_grid, weight_z, weight_x, weight_y):
    along_y = jnp.einsum('cde,ye->cdy', coarse_grid, weight_y, precision=highest_precision)
    along_x = jnp.einsum('cdy,xd->cxy', along_y, weight_x, precision=highest_precision)
    return jnp.einsum('cxy,zc->zxy', along_x, weight_z, precision=highest_precision)

def diagonal_of(elastic_ext, matrix_diag, depth_count):
    rows_x = elastic_ext.shape[1]
    cols_y = elastic_ext.shape[2]
    padded = jnp.pad(elastic_ext, ((0, 0), (1, 0), (1, 0)))
    summed = jnp.zeros((3, depth_count, rows_x, cols_y), jnp.float32)
    for corner, (shift_z, shift_x, shift_y) in enumerate(corner_offsets()):
        window = padded[1 - shift_z:1 - shift_z + depth_count, 1 - shift_x:1 - shift_x + rows_x, 1 - shift_y:1 - shift_y + cols_y]
        summed = summed + matrix_diag[corner][:, None, None, None] * window[None]
    return summed

def corner_pieces(nodal):
    depth_count, rows_x, cols_y = (nodal.shape[1], nodal.shape[2], nodal.shape[3])
    padded = jnp.pad(nodal, ((0, 0), (1, 1), (0, 1), (0, 1)))
    return [padded[:, shift_z:shift_z + depth_count + 1, shift_x:shift_x + rows_x, shift_y:shift_y + cols_y] for shift_z, shift_x, shift_y in corner_offsets()]

def apply_operator(nodal, elastic, matrix):
    depth_count, rows_x, cols_y = elastic.shape
    pieces = corner_pieces(nodal)
    elastic_ext = jnp.pad(elastic, ((1, 0), (0, 0), (0, 0)))
    summed = jnp.zeros(nodal.shape, jnp.float32)
    offsets = corner_offsets()
    for target in range(8):
        forces = jnp.zeros(pieces[0].shape, jnp.float32)
        for source in range(8):
            block = matrix[3 * target:3 * target + 3, 3 * source:3 * source + 3]
            forces = forces + jnp.einsum('ij,jzxy->izxy', block, pieces[source], precision=highest_precision)
        forces = forces * elastic_ext[None]
        padded_force = jnp.pad(forces, ((0, 0), (0, 0), (1, 0), (1, 0)))
        shift_z, shift_x, shift_y = offsets[target]
        summed = summed + padded_force[:, 1 - shift_z:1 - shift_z + depth_count, 1 - shift_x:1 - shift_x + rows_x, 1 - shift_y:1 - shift_y + cols_y]
    return summed

def element_energy(nodal, matrix):
    pieces = [piece[:, 1:] for piece in corner_pieces(nodal)]
    energy = jnp.zeros(pieces[0].shape[1:], jnp.float32)
    for target in range(8):
        forces = jnp.zeros(pieces[0].shape, jnp.float32)
        for source in range(8):
            block = matrix[3 * target:3 * target + 3, 3 * source:3 * source + 3]
            forces = forces + jnp.einsum('ij,jzxy->izxy', block, pieces[source], precision=highest_precision)
        energy = energy + lax.optimization_barrier(jnp.sum(pieces[target] * forces, axis=0))
    return energy

def reference(load_field, density, mode_panels, mode_weight, mode_germs):
    matrix = jnp.asarray(stiffness_table(), jnp.float32)
    matrix_diag = jnp.diagonal(matrix).reshape(8, 3)
    coefficients = (mode_weight[None, :] * mode_germs).astype(jnp.bfloat16)
    coarse_field = jnp.dot(coefficients, mode_panels.reshape(MODES, -1), preferred_element_type=jnp.float32)
    coarse_field = coarse_field.reshape(SAMPLES, CNZ, CNX, CNY)
    weight_z = hat_weights(NZ, CNZ, 0.0)
    weight_x = hat_weights(NX, CNX, 0.0)
    weight_y = hat_weights(NY, CNY, 0.0)

    def one_sample(coarse_grid):
        log_field = upsample(coarse_grid, weight_z, weight_x, weight_y)
        elastic = jnp.exp(log_field) * (0.001 + density ** 3)
        jacobi_diag = diagonal_of(jnp.pad(elastic, ((1, 0), (0, 0), (0, 0))), matrix_diag, NZ)
        displacement = jnp.zeros_like(load_field)
        residual = load_field
        precond_res = residual / jacobi_diag
        direction = precond_res
        precond_dot = jnp.sum(residual * precond_res)
        for iteration in range(ITERS):
            image_vec = apply_operator(direction, elastic, matrix)
            step_length = precond_dot / jnp.sum(direction * image_vec)
            displacement = displacement + step_length * direction
            residual = residual - step_length * image_vec
            precond_res = residual / jacobi_diag
            next_dot = jnp.sum(residual * precond_res)
            direction = precond_res + next_dot / precond_dot * direction
            precond_dot = next_dot
        compliance = jnp.sum(load_field * displacement)
        energy = element_energy(displacement, matrix)
        return (displacement, jnp.exp(log_field) * energy, compliance)
    displacement, sample_terms, compliance = lax.map(one_sample, coarse_field)
    gradient = -(3.0 / SAMPLES) * density ** 2 * lax.optimization_barrier(jnp.sum(sample_terms, axis=0))
    return (displacement, gradient, compliance)
```

```python
import itertools

import jax
import jax.numpy as jnp
import numpy as np
from jax import lax
from jax.experimental import pallas as pl
from jax.experimental.pallas import tpu as pltpu
from jax.sharding import PartitionSpec as P

BOTH = ("sample", "space")
POISSON = 0.3
LAME = POISSON / ((1.0 + POISSON) * (1.0 - 2.0 * POISSON))
SHEAR = 1.0 / (2.0 * (1.0 + POISSON))
DIAGONAL = (LAME + 2.0 * SHEAR) / 9.0 + 2.0 * SHEAR / 9.0
MODES = tuple(itertools.product((0, 1), repeat=3))
VMEM_LIMIT = 48 * 1024 * 1024


def vmem_spec():
    return pl.BlockSpec(memory_space=pltpu.VMEM)


def f32(*shape):
    return jax.ShapeDtypeStruct(shape, jnp.float32)


def split3(value):
    high = value.astype(jnp.bfloat16)
    rest = value - high.astype(jnp.float32)
    mid = rest.astype(jnp.bfloat16)
    low = (rest - mid.astype(jnp.float32)).astype(jnp.bfloat16)
    return high, mid, low


def dot32(left, right):
    return jnp.dot(left, right, preferred_element_type=jnp.float32)


def weight_tables(depth, rows, cols):
    def hat(positions, cells):
        return np.maximum(0.0, 1.0 - np.abs(positions[:, None] - cells[None, :]))

    along_x = hat((np.arange(rows) + 0.5) / 4.0 - 0.5, np.arange(rows // 4))
    along_y = hat((np.arange(cols) + 0.5) / 4.0 - 0.5, np.arange(cols // 4))
    along_z = hat((np.arange(depth + 4) - 2 + 0.5) / 4.0 - 0.5, np.arange(-1, 2))
    spread_y = np.tile(along_y.T, (rows // 4, 1))
    spread_zx = np.einsum("pc,xd->pxcd", along_z, along_x).reshape((depth + 4) * rows, -1)
    return spread_y.astype(jnp.bfloat16), spread_zx.astype(jnp.bfloat16)


def first_kernel(
    weight_ref, germs_ref, panels_ref, density_ref, load_ref,
    keep_ref, send1_ref, send2_ref, send3_ref, up_ref, down_ref,
):
    sample = lax.axis_index("sample")
    chip, core = sample // 2, sample % 2
    own_modes = panels_ref.shape[0]
    modes = germs_ref.shape[1]
    coefficients = (weight_ref[...] * germs_ref[...]).astype(jnp.bfloat16)
    mode_at = lax.broadcasted_iota(jnp.int32, (modes, own_modes), 0)
    slot_at = lax.broadcasted_iota(jnp.int32, (modes, own_modes), 1)
    pick = jnp.where(mode_at == slot_at + sample * own_modes, 1.0, 0.0).astype(jnp.bfloat16)
    own_coeff = dot32(coefficients, pick).astype(jnp.bfloat16)
    partial = dot32(own_coeff, panels_ref[...])
    row_at = lax.broadcasted_iota(jnp.int32, partial.shape, 0)
    for step, out_ref in enumerate((keep_ref, send1_ref, send2_ref, send3_ref)):
        target = (chip + step) % 4
        for place in range(2):
            row = 2 * target + (core if place == 0 else 1 - core)
            out_ref[place : place + 1] = jnp.sum(
                jnp.where(row_at == row, partial, 0.0), axis=0, keepdims=True
            )
    up_ref[0:2] = density_ref[2:4]
    down_ref[0:2] = density_ref[0:2]
    for comp in range(3):
        up_ref[2 + comp] = load_ref[comp, 3]
        down_ref[2 + 2 * comp : 4 + 2 * comp] = load_ref[comp, 0:2]


def shift_ahead(value, axis, mask):
    return jnp.where(mask, 0.0, pltpu.roll(value, value.shape[axis] - 1, axis))


def shift_back(value, axis, mask):
    return jnp.where(mask, 0.0, pltpu.roll(value, 1, axis))


def spread_plane(value, last_row, last_col):
    ahead = shift_ahead(value, 1, last_col)
    by_y = (value + ahead, ahead - value)
    aheads = [shift_ahead(part, 0, last_row) for part in by_y]
    sums = [part + other for part, other in zip(by_y, aheads)]
    diffs = [other - part for part, other in zip(by_y, aheads)]
    return sums + diffs


def element_modes(lower, upper):
    hat = {}
    for comp in range(3):
        for mode_x, mode_y in itertools.product((0, 1), repeat=2):
            at = 4 * comp + 2 * mode_x + mode_y
            if mode_x or mode_y:
                hat[comp, (0, mode_x, mode_y)] = lower[at] + upper[at]
            hat[comp, (1, mode_x, mode_y)] = upper[at] - lower[at]
    return hat


def modal_forces(hat):
    forces = {}
    for comp in range(3):
        for mode in MODES:
            count = sum(mode)
            if not count:
                continue
            own = (LAME + 2.0 * SHEAR) * mode[comp] + SHEAR * (count - mode[comp])
            value = (own / (16.0 * 3.0 ** (count - 1))) * hat[comp, mode]
            for other in range(3):
                if other == comp or mode[comp] + mode[other] != 1:
                    continue
                third = 3 - comp - other
                swapped = list(mode)
                swapped[comp], swapped[other] = mode[other], mode[comp]
                factor = (LAME if mode[comp] else SHEAR) / (16.0 * 3.0 ** mode[third])
                value = value + factor * hat[other, tuple(swapped)]
            forces[comp, mode] = value
    return forces


def modal_product(left, right):
    total = None
    for key, value in right.items():
        term = left[key] * value
        total = term if total is None else total + term
    return total


def fold(plane):
    return jnp.sum(plane.reshape(-1, 8, plane.shape[-1]), axis=0)


def middle_kernel(
    sums_ref, here_ref, low_other_ref, high_other_ref, low_same_ref, high_same_ref,
    density_ref, load_ref, below_ref, above_ref, spread_y_ref, spread_zx_ref,
    z_ref, y_ref, quad_ref, dots_ref,
    elastic, fields, fields_y, forces_at, inverse,
):
    slab = lax.axis_index("space")
    slabs = lax.axis_size("space")
    depth, rows, cols = density_ref.shape
    row_at = lax.broadcasted_iota(jnp.int32, (rows, cols), 0)
    col_at = lax.broadcasted_iota(jnp.int32, (rows, cols), 1)
    first_row, last_row = row_at == 0, row_at == rows - 1
    first_col, last_col = col_at == 0, col_at == cols - 1

    planes = (
        low_other_ref[...] + low_same_ref[...],
        sums_ref[0:1] + here_ref[...],
        high_other_ref[...] + high_same_ref[...],
    )
    cells = planes[0].shape[1]
    coarse_x, coarse_y = rows // 4, cols // 4
    cell_at = lax.broadcasted_iota(jnp.int32, (coarse_x, cells), 1)
    line_at = lax.broadcasted_iota(jnp.int32, (coarse_x, cells), 0)
    on_line = cell_at // coarse_y == line_at
    lines = jnp.concatenate(
        [jnp.where(on_line, jnp.broadcast_to(plane, on_line.shape), 0.0) for plane in planes], axis=0
    )
    spread_y = spread_y_ref[...]
    high, mid, low = (dot32(part, spread_y) for part in split3(lines))
    along_y = high + (mid + low)
    spread_zx = spread_zx_ref[...]
    high, mid, low = (dot32(spread_zx, part) for part in split3(along_y))
    growth = jnp.exp(high + (mid + low)).reshape(depth + 4, rows, cols)

    for place in range(depth + 4):
        if place < 2:
            dense = below_ref[place]
        elif place < depth + 2:
            dense = density_ref[place - 2]
        else:
            dense = above_ref[place - depth - 2]
        modulus = growth[place] * (0.001 + dense * dense * dense)
        if place < 2:
            modulus = jnp.where(slab > 0, modulus, 0.0)
        if place >= depth + 2:
            modulus = jnp.where(slab < slabs - 1, modulus, 0.0)
        elastic[place] = modulus

    before = None
    dot_load = jnp.zeros((8, cols), jnp.float32)
    for place in range(depth + 4):
        modulus = elastic[place]
        along = modulus + shift_back(modulus, 1, first_col)
        along = along + shift_back(along, 0, first_row)
        if place:
            diagonal = DIAGONAL * (along + before)
            if place == 1:
                diagonal = jnp.where(slab > 0, diagonal, 1.0)
            if place == depth + 3:
                diagonal = jnp.where(slab < slabs - 1, diagonal, 1.0)
            inverse_here = 1.0 / diagonal
            if 2 <= place <= depth + 2:
                inverse[place - 2] = inverse_here
            for comp in range(3):
                if place < 2:
                    load = below_ref[2 + comp]
                elif place < depth + 2:
                    load = load_ref[comp, place - 2]
                else:
                    load = above_ref[2 + 2 * comp + place - depth - 2]
                start = load * inverse_here
                if 2 <= place < depth + 2:
                    z_ref[comp, place - 2] = start
                    dot_load = dot_load + fold(load * start)
                for at, part in enumerate(spread_plane(start, last_row, last_col)):
                    fields[place - 1, 4 * comp + at] = part
        before = along

    def first_product(chunk, dot_zz):
        span = pl.ds(pl.multiple_of(chunk * 8, 8), 8)
        lower = [fields[0, at, span] for at in range(12)]
        carried = None
        for place in range(1, depth + 3):
            upper = [fields[place, at, span] for at in range(12)]
            hat = element_modes(lower, upper)
            forces = modal_forces(hat)
            modulus = elastic[place, span]
            if 2 <= place < depth + 2:
                energy = modal_product(hat, forces)
                quad_ref[0, place - 2, span] = energy
                dot_zz = dot_zz + modulus * energy
            forces = {key: value * modulus for key, value in forces.items()}
            passed = []
            for comp in range(3):
                for mode_x, mode_y in itertools.product((0, 1), repeat=2):
                    at = 4 * comp + 2 * mode_x + mode_y
                    rise = forces[comp, (1, mode_x, mode_y)]
                    if mode_x or mode_y:
                        level = forces[comp, (0, mode_x, mode_y)]
                        near, far = level - rise, level + rise
                    else:
                        near, far = -rise, rise
                    if carried is not None:
                        forces_at[place - 2, at, span] = near + carried[at]
                    passed.append(far)
            carried = passed
            lower = upper
        return dot_zz

    zeros = jnp.zeros((8, cols), jnp.float32)
    dot_zz = lax.fori_loop(0, rows // 8, first_product, zeros)

    for place in range(depth + 1):
        scale = inverse[place]
        if place == depth:
            scale = jnp.where(slab < slabs - 1, scale, 0.0)
        for comp in range(3):
            along = []
            for mode_y in range(2):
                level = forces_at[place, 4 * comp + mode_y]
                rise = forces_at[place, 4 * comp + 2 + mode_y]
                along.append((level - rise) + shift_back(level + rise, 0, first_row))
            image = (along[0] - along[1]) + shift_back(along[0] + along[1], 1, first_col)
            image = image * scale
            if place < depth:
                y_ref[comp, place] = image
            for at, part in enumerate(spread_plane(image, last_row, last_col)):
                fields_y[place, 4 * comp + at] = part

    def second_product(chunk, dots):
        dot_zy, dot_yy = dots
        span = pl.ds(pl.multiple_of(chunk * 8, 8), 8)
        lower = [fields_y[0, at, span] for at in range(12)]
        lower_z = [fields[1, at, span] for at in range(12)]
        for place in range(depth):
            upper = [fields_y[place + 1, at, span] for at in range(12)]
            upper_z = [fields[place + 2, at, span] for at in range(12)]
            hat = element_modes(lower, upper)
            forces = modal_forces(hat)
            modulus = elastic[place + 2, span]
            energy_yy = modal_product(hat, forces)
            energy_zy = modal_product(element_modes(lower_z, upper_z), forces)
            dot_zy = dot_zy + modulus * energy_zy
            dot_yy = dot_yy + modulus * energy_yy
            dense = density_ref[place, span]
            factor = -(3.0 / 8.0) * dense * dense
            factor = factor * modulus / (0.001 + dense * dense * dense)
            quad_ref[0, place, span] = factor * quad_ref[0, place, span]
            quad_ref[1, place, span] = (2.0 * factor) * energy_zy
            quad_ref[2, place, span] = factor * energy_yy
            lower, lower_z = upper, upper_z
        return dot_zy, dot_yy

    dot_zy, dot_yy = lax.fori_loop(0, rows // 8, second_product, (zeros, zeros))
    for at, part in enumerate((dot_load, dot_zz, dot_zy, dot_yy)):
        dots_ref[at : at + 1] = jnp.sum(part, axis=0, keepdims=True)


def last_kernel(
    dots_ref, other_dots_ref, z_ref, y_ref, quad_ref,
    displacement_ref, compliance_ref, keep_ref, send1_ref, send2_ref, send3_ref,
):
    chip = lax.axis_index("sample") // 2
    dots = jnp.sum(dots_ref[...] + other_dots_ref[...], axis=1, keepdims=True)
    dot_load, dot_zz, dot_zy, dot_yy = (dots[at : at + 1] for at in range(4))
    first = dot_zz / dot_load
    second = dot_zy / dot_load
    third = dot_yy / dot_load
    under = third * first - second * second
    along_z = (third - first * second) / under
    along_y = (first * first - second) / under
    compliance_ref[0] = (dot_load * (along_z + along_y * first))[0, 0]
    for comp in range(3):
        for place in range(z_ref.shape[1]):
            displacement_ref[0, comp, place] = along_z * z_ref[comp, place] + along_y * y_ref[comp, place]
    squares = (along_z * along_z, along_z * along_y, along_y * along_y)
    share = quad_ref.shape[2] // 4
    for step, out_ref in enumerate((keep_ref, send1_ref, send2_ref, send3_ref)):
        span = pl.ds(pl.multiple_of((chip + step) % 4 * share, share), share)
        for place in range(z_ref.shape[1]):
            out_ref[place] = sum(squares[at] * quad_ref[at, place, span] for at in range(3))


def call(kernel, outs, scratch=(), out_specs=None):
    return pl.pallas_call(
        kernel,
        out_shape=outs,
        out_specs=out_specs if out_specs is not None else [vmem_spec()] * len(outs),
        scratch_shapes=scratch,
        compiler_params=pltpu.CompilerParams(vmem_limit_bytes=VMEM_LIMIT),
    )


def ring_sum(value, offsets, period, base):
    total = value
    parts = []
    for offset in offsets:
        pairs = []
        for source in range(lax.axis_size("space")):
            block = source // period * period
            pairs.append((source, block + (source - block + offset) % period))
        parts.append(lax.ppermute(value, "space", pairs))
    for part in parts:
        total = total + part
    return total


def per_device(load_field, density, mode_panels, mode_weight, mode_germs):
    depth, rows, cols = density.shape
    slabs = lax.axis_size("space")
    samples = lax.axis_size("sample")
    own_modes = mode_panels.shape[0]
    cells = mode_panels.shape[2]
    spread_y, spread_zx = weight_tables(depth, rows, cols)

    keep, send1, send2, send3, going_up, going_down = call(
        first_kernel,
        [f32(2, cells)] * 4 + [f32(5, rows, cols), f32(8, rows, cols)],
    )(
        mode_weight.reshape(1, -1),
        mode_germs,
        mode_panels.reshape(own_modes, cells),
        density,
        load_field,
    )

    def along_chips(value, offset):
        return lax.ppermute(
            value, "sample", [(at, (at + 2 * offset) % samples) for at in range(samples)]
        )

    def neighbour(value, flip, step):
        pairs = []
        for sample in range(samples):
            for slab in range(slabs):
                if 0 <= slab + step < slabs:
                    target = sample ^ 1 if flip else sample
                    pairs.append((sample * slabs + slab, target * slabs + slab + step))
        return lax.ppermute(value, BOTH, pairs)

    got = [along_chips(value, step + 1) for step, value in enumerate((send1, send2, send3))]
    below = neighbour(going_up, False, 1)
    above = neighbour(going_down, False, -1)
    sums = keep + got[0] + got[1] + got[2]
    same, other = sums[0:1], sums[1:2]
    here = neighbour(other, True, 0)
    low_other, high_other = neighbour(other, True, 1), neighbour(other, True, -1)
    low_same, high_same = neighbour(same, False, 1), neighbour(same, False, -1)

    z_vec, y_vec, quads, dots = call(
        middle_kernel,
        [
            f32(3, depth, rows, cols),
            f32(3, depth, rows, cols),
            f32(3, depth, rows, cols),
            f32(4, cols),
        ],
        scratch=[
            pltpu.VMEM((depth + 4, rows, cols), jnp.float32),
            pltpu.VMEM((depth + 3, 12, rows, cols), jnp.float32),
            pltpu.VMEM((depth + 1, 12, rows, cols), jnp.float32),
            pltpu.VMEM((depth + 1, 12, rows, cols), jnp.float32),
            pltpu.VMEM((depth + 1, rows, cols), jnp.float32),
        ],
    )(
        sums, here, low_other, high_other, low_same, high_same,
        density, load_field, below, above, spread_y, spread_zx,
    )

    dots = ring_sum(dots, (8, 16, 24), 32, 0)
    dots = ring_sum(dots, (2, 4, 6), 8, 0)
    other_dots = lax.ppermute(dots, "space", [(at, at ^ 1) for at in range(slabs)])

    share = rows // 4
    displacement, compliance, keep, send1, send2, send3 = call(
        last_kernel,
        [f32(1, 3, depth, rows, cols), f32(1)] + [f32(depth, share, cols)] * 4,
        out_specs=[vmem_spec(), pl.BlockSpec(memory_space=pltpu.SMEM)] + [vmem_spec()] * 4,
    )(dots, other_dots, z_vec, y_vec, quads)

    got = [along_chips(value, step + 1) for step, value in enumerate((send1, send2, send3))]
    total = keep + got[0] + got[1] + got[2]
    halves = total.reshape(depth, 2, share // 2, cols)
    core = lax.axis_index("sample") % 2
    own = lax.dynamic_index_in_dim(halves, core, 1, keepdims=False)
    away = lax.dynamic_index_in_dim(halves, 1 - core, 1, keepdims=False)
    gradient = own + neighbour(away, True, 0)
    return displacement, gradient, compliance


def solution(mesh):
    placed = (
        P(None, "space", None, None),
        P("space", None, None),
        P("sample", "space", None),
        P(),
        P(),
    )
    return jax.shard_map(
        per_device,
        mesh=mesh,
        in_specs=placed,
        out_specs=(P("sample", None, "space", None, None), P("space", "sample", None), P("sample")),
        check_vma=False,
    )
```

```python
import itertools

import jax
import jax.numpy as jnp
import numpy as np
from jax import lax
from jax.experimental import pallas as pl
from jax.experimental.pallas import tpu as pltpu
from jax.sharding import PartitionSpec as P

POISSON = 0.3
LAME = POISSON / ((1.0 + POISSON) * (1.0 - 2.0 * POISSON))
SHEAR = 1.0 / (2.0 * (1.0 + POISSON))
DIAGONAL = (LAME + 2.0 * SHEAR) / 9.0 + 2.0 * SHEAR / 9.0
MODES = tuple(itertools.product((0, 1), repeat=3))
VMEM_LIMIT = 48 * 1024 * 1024


def vmem_spec():
    return pl.BlockSpec(memory_space=pltpu.VMEM)


def f32(*shape):
    return jax.ShapeDtypeStruct(shape, jnp.float32)


def split3(value):
    high = value.astype(jnp.bfloat16)
    rest = value - high.astype(jnp.float32)
    mid = rest.astype(jnp.bfloat16)
    low = (rest - mid.astype(jnp.float32)).astype(jnp.bfloat16)
    return high, mid, low


def dot32(left, right):
    return jnp.dot(left, right, preferred_element_type=jnp.float32)


def weight_tables(depth, rows, cols):
    def hat(positions, cells):
        return np.maximum(0.0, 1.0 - np.abs(positions[:, None] - cells[None, :]))

    along_x = hat((np.arange(rows) + 0.5) / 4.0 - 0.5, np.arange(rows // 4))
    along_y = hat((np.arange(cols) + 0.5) / 4.0 - 0.5, np.arange(cols // 4))
    along_z = hat((np.arange(depth + 4) - 2 + 0.5) / 4.0 - 0.5, np.arange(-1, 2))
    spread_y = np.tile(along_y.T, (4, 1))
    spread_zx = np.einsum("pc,xd->pxcd", along_z, along_x).reshape((depth + 4) * rows, -1)
    return spread_y.astype(jnp.bfloat16), spread_zx.astype(jnp.bfloat16)


def first_kernel(weight_hbm, germs_hbm, panels_hbm, partial_ref, weight, germs, panels, sems):
    sample = lax.axis_index("sample")
    copies = [
        pltpu.make_async_copy(source, target, sems.at[at])
        for at, (source, target) in enumerate(
            ((weight_hbm, weight), (germs_hbm, germs), (panels_hbm, panels))
        )
    ]
    for copy in copies:
        copy.start()
    own_modes = panels.shape[0]
    modes = germs.shape[1]
    mode_at = lax.broadcasted_iota(jnp.int32, (modes, own_modes), 0)
    slot_at = lax.broadcasted_iota(jnp.int32, (modes, own_modes), 1)
    pick = jnp.where(mode_at == slot_at + sample * own_modes, 1.0, 0.0).astype(jnp.bfloat16)
    for copy in copies:
        copy.wait()
    coefficients = (weight[...] * germs[...]).astype(jnp.bfloat16)
    own_coeff = dot32(coefficients, pick).astype(jnp.bfloat16)
    partial = dot32(own_coeff, panels[...])
    for at in range(partial_ref.shape[1]):
        partial_ref[:, at] = partial[:, at * 128 : (at + 1) * 128]


def pack_kernel(parts_ref, density_ref, load_ref, sums_ref, pair_ref, next_ref):
    slab = lax.axis_index("space")
    planes = (pair_ref.shape[0] - 8) // density_ref.shape[1]
    rows = density_ref.shape[1]
    depth = density_ref.shape[0]
    cells = parts_ref.shape[1]
    sums = jnp.sum(parts_ref[...], axis=0)
    sums_ref[...] = sums

    def fill(up_ref, down_ref):
        up = [density_ref[depth - 2], density_ref[depth - 1]]
        up += [load_ref[comp, depth - 1] for comp in range(3)]
        down = [density_ref[0], density_ref[1]]
        down += [load_ref[comp, place] for comp in range(3) for place in range(2)]
        for ref, parts in ((up_ref, up), (down_ref, down)):
            for at in range(planes):
                ref[at * rows : (at + 1) * rows] = parts[at] if at < len(parts) else jnp.zeros_like(up[0])
            ref[planes * rows : planes * rows + cells] = sums
            ref[planes * rows + cells :] = jnp.zeros((8 - cells, sums.shape[1]), jnp.float32)

    @pl.when(slab % 2 == 0)
    def _():
        fill(pair_ref, next_ref)

    @pl.when(slab % 2 == 1)
    def _():
        fill(next_ref, pair_ref)


def shift_ahead(value, axis, mask):
    return jnp.where(mask, 0.0, pltpu.roll(value, value.shape[axis] - 1, axis))


def shift_back(value, axis, mask):
    return jnp.where(mask, 0.0, pltpu.roll(value, 1, axis))


def spread_plane(value, last_row, last_col):
    ahead = shift_ahead(value, 1, last_col)
    by_y = (value + ahead, ahead - value)
    aheads = [shift_ahead(part, 0, last_row) for part in by_y]
    sums = [part + other for part, other in zip(by_y, aheads)]
    diffs = [other - part for part, other in zip(by_y, aheads)]
    return sums + diffs


def element_modes(lower, upper):
    hat = {}
    for comp in range(3):
        for mode_x, mode_y in itertools.product((0, 1), repeat=2):
            at = 4 * comp + 2 * mode_x + mode_y
            if mode_x or mode_y:
                hat[comp, (0, mode_x, mode_y)] = lower[at] + upper[at]
            hat[comp, (1, mode_x, mode_y)] = upper[at] - lower[at]
    return hat


def modal_forces(hat):
    forces = {}
    for comp in range(3):
        for mode in MODES:
            count = sum(mode)
            if not count:
                continue
            own = (LAME + 2.0 * SHEAR) * mode[comp] + SHEAR * (count - mode[comp])
            value = (own / (16.0 * 3.0 ** (count - 1))) * hat[comp, mode]
            for other in range(3):
                if other == comp or mode[comp] + mode[other] != 1:
                    continue
                third = 3 - comp - other
                swapped = list(mode)
                swapped[comp], swapped[other] = mode[other], mode[comp]
                factor = (LAME if mode[comp] else SHEAR) / (16.0 * 3.0 ** mode[third])
                value = value + factor * hat[other, tuple(swapped)]
            forces[comp, mode] = value
    return forces


def modal_product(left, right):
    total = None
    for key, value in right.items():
        term = left[key] * value
        total = term if total is None else total + term
    return total


def fold(plane):
    return jnp.sum(plane.reshape(-1, 8, plane.shape[-1]), axis=0)


def middle_kernel(
    sums_ref, density_ref, load_ref, pair_ref, next_ref, spread_y_ref, spread_zx_ref,
    z_ref, y_ref, quad_ref, dots_ref,
    elastic, fields, fields_y, forces_at, inverse,
):
    slab = lax.axis_index("space")
    slabs = lax.axis_size("space")
    even = slab % 2 == 0
    depth, rows, cols = density_ref.shape
    row_at = lax.broadcasted_iota(jnp.int32, (rows, cols), 0)
    col_at = lax.broadcasted_iota(jnp.int32, (rows, cols), 1)
    first_row, last_row = row_at == 0, row_at == rows - 1
    first_col, last_col = col_at == 0, col_at == cols - 1
    cells = sums_ref.shape[0]
    extra = pl.ds(pair_ref.shape[0] - 8, cells)

    def from_below(span):
        return jnp.where(even, next_ref[span], pair_ref[span])

    def from_above(span):
        return jnp.where(even, pair_ref[span], next_ref[span])

    def plane(place):
        return pl.ds(place * rows, rows)

    coarse_x, coarse_y = rows // 4, cols // 4
    fold_x = coarse_x // cells
    line_at = lax.broadcasted_iota(jnp.int32, (coarse_x, cols), 0)
    cell_at = lax.broadcasted_iota(jnp.int32, (coarse_x, cols), 1)
    on_line = cell_at // coarse_y == line_at % fold_x
    lines = []
    for coarse in (from_below(extra), sums_ref[...], from_above(extra)):
        tall = jnp.zeros((coarse_x, cols), jnp.float32)
        for at in range(cells):
            tall = jnp.where(line_at // fold_x == at, coarse[at : at + 1], tall)
        lines.append(jnp.where(on_line, tall, 0.0))
    lines = jnp.concatenate(lines, axis=0)
    spread_y = spread_y_ref[...]
    high, mid, low = (dot32(part, spread_y) for part in split3(lines))
    along_y = high + (mid + low)
    spread_zx = spread_zx_ref[...]
    high, mid, low = (dot32(spread_zx, part) for part in split3(along_y))
    growth = jnp.exp(high + (mid + low)).reshape(depth + 4, rows, cols)

    for place in range(depth + 4):
        if place < 2:
            dense = from_below(plane(place))
        elif place < depth + 2:
            dense = density_ref[place - 2]
        else:
            dense = from_above(plane(place - depth - 2))
        modulus = growth[place] * (0.001 + dense * dense * dense)
        if place < 2:
            modulus = jnp.where(slab > 0, modulus, 0.0)
        if place >= depth + 2:
            modulus = jnp.where(slab < slabs - 1, modulus, 0.0)
        elastic[place] = modulus

    before = None
    dot_load = jnp.zeros((8, cols), jnp.float32)
    for place in range(depth + 4):
        modulus = elastic[place]
        along = modulus + shift_back(modulus, 1, first_col)
        along = along + shift_back(along, 0, first_row)
        if place:
            diagonal = DIAGONAL * (along + before)
            if place == 1:
                diagonal = jnp.where(slab > 0, diagonal, 1.0)
            if place == depth + 3:
                diagonal = jnp.where(slab < slabs - 1, diagonal, 1.0)
            inverse_here = 1.0 / diagonal
            if 2 <= place <= depth + 2:
                inverse[place - 2] = inverse_here
            for comp in range(3):
                if place < 2:
                    load = from_below(plane(2 + comp))
                elif place < depth + 2:
                    load = load_ref[comp, place - 2]
                else:
                    load = from_above(plane(2 + 2 * comp + place - depth - 2))
                start = load * inverse_here
                if 2 <= place < depth + 2:
                    z_ref[comp, place - 2] = start
                    dot_load = dot_load + fold(load * start)
                for at, part in enumerate(spread_plane(start, last_row, last_col)):
                    fields[place - 1, 4 * comp + at] = part
        before = along

    def first_product(chunk, dot_zz):
        span = pl.ds(pl.multiple_of(chunk * 8, 8), 8)
        lower = [fields[0, at, span] for at in range(12)]
        carried = None
        for place in range(1, depth + 3):
            upper = [fields[place, at, span] for at in range(12)]
            hat = element_modes(lower, upper)
            forces = modal_forces(hat)
            modulus = elastic[place, span]
            if 2 <= place < depth + 2:
                energy = modal_product(hat, forces)
                quad_ref[0, place - 2, span] = energy
                dot_zz = dot_zz + modulus * energy
            forces = {key: value * modulus for key, value in forces.items()}
            passed = []
            for comp in range(3):
                for mode_x, mode_y in itertools.product((0, 1), repeat=2):
                    at = 4 * comp + 2 * mode_x + mode_y
                    rise = forces[comp, (1, mode_x, mode_y)]
                    if mode_x or mode_y:
                        level = forces[comp, (0, mode_x, mode_y)]
                        near, far = level - rise, level + rise
                    else:
                        near, far = -rise, rise
                    if carried is not None:
                        forces_at[place - 2, at, span] = near + carried[at]
                    passed.append(far)
            carried = passed
            lower = upper
        return dot_zz

    zeros = jnp.zeros((8, cols), jnp.float32)
    dot_zz = lax.fori_loop(0, rows // 8, first_product, zeros)

    for place in range(depth + 1):
        scale = inverse[place]
        if place == depth:
            scale = jnp.where(slab < slabs - 1, scale, 0.0)
        for comp in range(3):
            along = []
            for mode_y in range(2):
                level = forces_at[place, 4 * comp + mode_y]
                rise = forces_at[place, 4 * comp + 2 + mode_y]
                along.append((level - rise) + shift_back(level + rise, 0, first_row))
            image = (along[0] - along[1]) + shift_back(along[0] + along[1], 1, first_col)
            image = image * scale
            if place < depth:
                y_ref[comp, place] = image
            for at, part in enumerate(spread_plane(image, last_row, last_col)):
                fields_y[place, 4 * comp + at] = part

    def second_product(chunk, dots):
        dot_zy, dot_yy = dots
        span = pl.ds(pl.multiple_of(chunk * 8, 8), 8)
        lower = [fields_y[0, at, span] for at in range(12)]
        lower_z = [fields[1, at, span] for at in range(12)]
        for place in range(depth):
            upper = [fields_y[place + 1, at, span] for at in range(12)]
            upper_z = [fields[place + 2, at, span] for at in range(12)]
            hat = element_modes(lower, upper)
            forces = modal_forces(hat)
            modulus = elastic[place + 2, span]
            energy_yy = modal_product(hat, forces)
            energy_zy = modal_product(element_modes(lower_z, upper_z), forces)
            dot_zy = dot_zy + modulus * energy_zy
            dot_yy = dot_yy + modulus * energy_yy
            dense = density_ref[place, span]
            factor = -(3.0 / 8.0) * dense * dense
            factor = factor * modulus / (0.001 + dense * dense * dense)
            quad_ref[0, place, span] = factor * quad_ref[0, place, span]
            quad_ref[1, place, span] = (2.0 * factor) * energy_zy
            quad_ref[2, place, span] = factor * energy_yy
            lower, lower_z = upper, upper_z
        return dot_zy, dot_yy

    dot_zy, dot_yy = lax.fori_loop(0, rows // 8, second_product, (zeros, zeros))
    lane_at = lax.broadcasted_iota(jnp.int32, (1, cols), 1)
    packed = jnp.zeros((1, cols), jnp.float32)
    for at, part in enumerate((dot_load, dot_zz, dot_zy, dot_yy)):
        packed = jnp.where(lane_at == at, jnp.sum(part, keepdims=True), packed)
    dots_ref[...] = jnp.broadcast_to(packed, dots_ref.shape)


def last_kernel(dots_ref, z_ref, y_ref, quad_ref, displacement_ref, compliance_ref, terms_ref):
    dots = jnp.sum(dots_ref[...], axis=0, keepdims=True)
    lane_at = lax.broadcasted_iota(jnp.int32, dots.shape, 1)
    dot_load, dot_zz, dot_zy, dot_yy = (
        jnp.sum(jnp.where(lane_at == at, dots, 0.0), axis=1, keepdims=True) for at in range(4)
    )
    first = dot_zz / dot_load
    second = dot_zy / dot_load
    third = dot_yy / dot_load
    under = third * first - second * second
    along_z = (third - first * second) / under
    along_y = (first * first - second) / under
    compliance_ref[0] = (dot_load * (along_z + along_y * first))[0, 0]
    for comp in range(3):
        for place in range(z_ref.shape[1]):
            displacement_ref[0, comp, place] = along_z * z_ref[comp, place] + along_y * y_ref[comp, place]
    squares = (along_z * along_z, along_z * along_y, along_y * along_y)
    samples, depth, share = terms_ref.shape[:3]
    for sample in range(samples):
        span = pl.ds(sample * share, share)
        for place in range(depth):
            terms_ref[sample, place] = sum(squares[at] * quad_ref[at, place, span] for at in range(3))


def call(kernel, outs, inputs, scratch=(), in_memory=pltpu.VMEM, out_specs=None):
    return pl.pallas_call(
        kernel,
        out_shape=outs,
        in_specs=[pl.BlockSpec(memory_space=in_memory)] * inputs,
        out_specs=out_specs if out_specs is not None else [vmem_spec()] * len(outs),
        scratch_shapes=scratch,
        compiler_params=pltpu.CompilerParams(vmem_limit_bytes=VMEM_LIMIT),
    )


def per_device(load_field, density, mode_panels, mode_weight, mode_germs):
    depth, rows, cols = density.shape
    slabs = lax.axis_size("space")
    samples = lax.axis_size("sample")
    own_modes, _, cells = mode_panels.shape
    spread_y, spread_zx = weight_tables(depth, rows, cols)

    (partial,) = call(
        first_kernel,
        [f32(samples, cells // 128, 128)],
        inputs=3,
        scratch=[
            pltpu.VMEM((1, mode_weight.shape[0]), jnp.float32),
            pltpu.VMEM(mode_germs.shape, jnp.float32),
            pltpu.VMEM((own_modes, cells), jnp.bfloat16),
            pltpu.SemaphoreType.DMA((3,)),
        ],
        in_memory=pl.ANY,
    )(mode_weight.reshape(1, -1), mode_germs, mode_panels.reshape(own_modes, cells))
    parts = lax.all_to_all(partial, "sample", 0, 0, tiled=True)

    message = f32(8 * rows + 8, cols)
    sums, pair_out, next_out = call(pack_kernel, [f32(cells // 128, 128), message, message], inputs=3)(
        parts, density, load_field
    )
    pairs = [(at, at ^ 1) for at in range(slabs)]
    nexts = [(at, at + 1) for at in range(1, slabs - 1, 2)]
    nexts += [(target, source) for source, target in nexts]
    pair_in = lax.ppermute(pair_out, "space", pairs)
    next_in = lax.ppermute(next_out, "space", nexts)

    z_vec, y_vec, quads, dots = call(
        middle_kernel,
        [f32(3, depth, rows, cols)] * 3 + [f32(slabs, cols)],
        inputs=7,
        scratch=[
            pltpu.VMEM((depth + 4, rows, cols), jnp.float32),
            pltpu.VMEM((depth + 3, 12, rows, cols), jnp.float32),
            pltpu.VMEM((depth + 1, 12, rows, cols), jnp.float32),
            pltpu.VMEM((depth + 1, 12, rows, cols), jnp.float32),
            pltpu.VMEM((depth + 1, rows, cols), jnp.float32),
        ],
    )(sums, density, load_field, pair_in, next_in, spread_y, spread_zx)
    dots = lax.all_to_all(dots, "space", 0, 0, tiled=True)

    displacement, compliance, terms = call(
        last_kernel,
        [f32(1, 3, depth, rows, cols), f32(1), f32(samples, depth, rows // samples, cols)],
        inputs=4,
        out_specs=[vmem_spec(), pl.BlockSpec(memory_space=pltpu.SMEM), vmem_spec()],
    )(dots, z_vec, y_vec, quads)
    terms = lax.all_to_all(terms, "sample", 0, 0, tiled=True)
    return displacement, jnp.sum(terms, axis=0), compliance


def solution(mesh):
    placed = (
        P(None, "space", None, None),
        P("space", None, None),
        P("sample", "space", None),
        P(),
        P(),
    )
    return jax.shard_map(
        per_device,
        mesh=mesh,
        in_specs=placed,
        out_specs=(P("sample", None, "space", None, None), P("space", "sample", None), P("sample")),
        check_vma=False,
    )
```

```python
import itertools

import jax
import jax.numpy as jnp
import numpy as np
from jax import lax
from jax.experimental import pallas as pl
from jax.experimental.pallas import tpu as pltpu
from jax.sharding import PartitionSpec as P

POISSON = 0.3
LAME = POISSON / ((1.0 + POISSON) * (1.0 - 2.0 * POISSON))
SHEAR = 1.0 / (2.0 * (1.0 + POISSON))
DIAGONAL = (LAME + 2.0 * SHEAR) / 9.0 + 2.0 * SHEAR / 9.0
RATIO = LAME / SHEAR
UNIT = SHEAR / 16.0
VMEM_LIMIT = 48 * 1024 * 1024


def vmem_spec():
    return pl.BlockSpec(memory_space=pltpu.VMEM)


def f32(*shape):
    return jax.ShapeDtypeStruct(shape, jnp.float32)


def split3(value):
    high = value.astype(jnp.bfloat16)
    rest = value - high.astype(jnp.float32)
    mid = rest.astype(jnp.bfloat16)
    low = (rest - mid.astype(jnp.float32)).astype(jnp.bfloat16)
    return high, mid, low


def dot32(left, right):
    return jnp.dot(left, right, preferred_element_type=jnp.float32)


def weight_tables(depth, rows, cols):
    def hat(positions, cells):
        return np.maximum(0.0, 1.0 - np.abs(positions[:, None] - cells[None, :]))

    along_x = hat((np.arange(rows) + 0.5) / 4.0 - 0.5, np.arange(rows // 4))
    along_y = hat((np.arange(cols) + 0.5) / 4.0 - 0.5, np.arange(cols // 4))
    along_z = hat((np.arange(depth + 4) - 2 + 0.5) / 4.0 - 0.5, np.arange(-1, 2))
    spread_y = np.tile(along_y.T, (4, 1))
    spread_zx = np.einsum("pc,xd->pxcd", along_z, along_x).reshape((depth + 4) * rows, -1)
    return spread_y.astype(jnp.bfloat16), spread_zx.astype(jnp.bfloat16)


def first_kernel(
    weight_hbm, germs_hbm, panels_hbm, density_hbm, load_hbm,
    partial_ref, density_ref, load_ref,
    weight, germs, panels, sems,
):
    sample = lax.axis_index("sample")
    copies = [
        pltpu.make_async_copy(source, target, sems.at[at])
        for at, (source, target) in enumerate(
            (
                (weight_hbm, weight),
                (germs_hbm, germs),
                (panels_hbm, panels),
                (density_hbm, density_ref),
                (load_hbm, load_ref),
            )
        )
    ]
    for copy in copies:
        copy.start()
    own_modes = panels.shape[0]
    modes = germs.shape[1]
    mode_at = lax.broadcasted_iota(jnp.int32, (modes, own_modes), 0)
    slot_at = lax.broadcasted_iota(jnp.int32, (modes, own_modes), 1)
    pick = jnp.where(mode_at == slot_at + sample * own_modes, 1.0, 0.0).astype(jnp.bfloat16)
    for copy in copies[:3]:
        copy.wait()
    coefficients = (weight[...] * germs[...]).astype(jnp.bfloat16)
    own_coeff = dot32(coefficients, pick).astype(jnp.bfloat16)
    partial = dot32(own_coeff, panels[...])
    for at in range(partial_ref.shape[1]):
        partial_ref[:, at] = partial[:, at * 128 : (at + 1) * 128]
    for copy in copies[3:]:
        copy.wait()


def pack_kernel(parts_ref, density_ref, load_ref, sums_ref, pair_ref, next_ref):
    slab = lax.axis_index("space")
    planes = (pair_ref.shape[0] - 8) // density_ref.shape[1]
    rows = density_ref.shape[1]
    depth = density_ref.shape[0]
    cells = parts_ref.shape[1]
    sums = jnp.sum(parts_ref[...], axis=0)
    sums_ref[...] = sums

    def fill(up_ref, down_ref):
        up = [density_ref[depth - 2], density_ref[depth - 1]]
        up += [load_ref[comp, depth - 1] for comp in range(3)]
        down = [density_ref[0], density_ref[1]]
        down += [load_ref[comp, place] for comp in range(3) for place in range(2)]
        for ref, parts in ((up_ref, up), (down_ref, down)):
            for at in range(planes):
                ref[at * rows : (at + 1) * rows] = parts[at] if at < len(parts) else jnp.zeros_like(up[0])
            ref[planes * rows : planes * rows + cells] = sums
            ref[planes * rows + cells :] = jnp.zeros((8 - cells, sums.shape[1]), jnp.float32)

    @pl.when(slab % 2 == 0)
    def _():
        fill(pair_ref, next_ref)

    @pl.when(slab % 2 == 1)
    def _():
        fill(next_ref, pair_ref)


def shift_ahead(value, axis, mask):
    return jnp.where(mask, 0.0, pltpu.roll(value, value.shape[axis] - 1, axis))


def shift_back(value, axis, mask):
    return jnp.where(mask, 0.0, pltpu.roll(value, 1, axis))


def store_along_y(target, place, comp, value, last_col):
    ahead = shift_ahead(value, 1, last_col)
    target[place, 2 * comp, 0 : value.shape[0]] = value + ahead
    target[place, 2 * comp + 1, 0 : value.shape[0]] = ahead - value


def load_spread(source, place, chunk):
    parts = []
    for comp in range(3):
        here = [source[place, 2 * comp + mode, pl.ds(chunk * 8, 8)] for mode in range(2)]
        ahead = [source[place, 2 * comp + mode, pl.ds(chunk * 8 + 1, 8)] for mode in range(2)]
        parts += [one + two for one, two in zip(here, ahead)]
        parts += [two - one for one, two in zip(here, ahead)]
    return parts


def element_modes(lower, upper):
    hat = {}
    for comp in range(3):
        for mode_x, mode_y in itertools.product((0, 1), repeat=2):
            at = 4 * comp + 2 * mode_x + mode_y
            if mode_x or mode_y:
                hat[comp, (0, mode_x, mode_y)] = lower[at] + upper[at]
            hat[comp, (1, mode_x, mode_y)] = upper[at] - lower[at]
    return hat


def mode(*axes):
    return tuple(int(axis in axes) for axis in range(3))


def modal_parts(hat):
    shear = {
        (one, two): hat[one, mode(two)] + hat[two, mode(one)] for one, two in ((0, 1), (0, 2), (1, 2))
    }
    trace = hat[0, mode(0)] + hat[1, mode(1)] + hat[2, mode(2)]
    twist = [hat[axis, mode(*(other for other in range(3) if other != axis))] for axis in range(3)]
    bends = {}
    for across in range(3):
        one, two = (axis for axis in range(3) if axis != across)
        bends[across] = (one, two, hat[one, mode(one, across)] + hat[two, mode(two, across)])
    return shear, trace, twist, bends


def modal_forces(hat, weight):
    shear, trace, twist, bends = modal_parts(hat)
    forces = {}
    for (one, two), value in shear.items():
        forces[one, mode(two)] = forces[two, mode(one)] = value * weight
    level = RATIO * trace
    for axis in range(3):
        forces[axis, mode(axis)] = (2.0 * hat[axis, mode(axis)] + level) * weight
    third = (1.0 / 3.0) * weight
    both = twist[0] + twist[1] + twist[2]
    for axis in range(3):
        place = mode(*(other for other in range(3) if other != axis))
        forces[axis, place] = (twist[axis] + both) * third
    for across, (one, two, total) in bends.items():
        extra = (RATIO / 3.0) * total
        for axis in (one, two):
            place = mode(axis, across)
            forces[axis, place] = (hat[axis, place] + extra) * weight
    last = ((RATIO + 4.0) / 9.0) * weight
    for axis in range(3):
        forces[axis, (1, 1, 1)] = hat[axis, (1, 1, 1)] * last
    return forces


def total_of(values):
    values = list(values)
    while len(values) > 1:
        paired = [one + two for one, two in zip(values[::2], values[1::2])]
        values = paired + ([values[-1]] if len(values) % 2 else [])
    return values[0]


def modal_product(left, right):
    return total_of(left[key] * value for key, value in right.items())


def modal_energy(hat):
    shear, trace, twist, bends = modal_parts(hat)

    def squares(values):
        return total_of(value * value for value in values)

    both = twist[0] + twist[1] + twist[2]
    whole = list(shear.values())
    for across, (one, two, _) in bends.items():
        whole += [hat[one, mode(one, across)], hat[two, mode(two, across)]]
    return total_of(
        [
            squares(whole),
            2.0 * squares(hat[axis, mode(axis)] for axis in range(3)),
            RATIO * (trace * trace),
            (1.0 / 3.0) * squares(twist + [both]),
            (RATIO / 3.0) * squares(total for _, _, total in bends.values()),
            ((RATIO + 4.0) / 9.0) * squares(hat[axis, (1, 1, 1)] for axis in range(3)),
        ]
    )


def fold(plane):
    return jnp.sum(plane.reshape(-1, 8, plane.shape[-1]), axis=0)


def middle_kernel(
    sums_ref, density_ref, load_ref, pair_ref, next_ref, spread_y_ref, spread_zx_ref,
    z_ref, y_ref, growth_ref, dots_ref,
    elastic, dense_all, loads, around, inverse, fields, fields_y, near_at, far_at,
):
    slab = lax.axis_index("space")
    slabs = lax.axis_size("space")
    even = slab % 2 == 0
    depth, rows, cols = density_ref.shape
    row_at = lax.broadcasted_iota(jnp.int32, (rows, cols), 0)
    col_at = lax.broadcasted_iota(jnp.int32, (rows, cols), 1)
    first_row = row_at == 0
    first_col, last_col = col_at == 0, col_at == cols - 1
    cells = sums_ref.shape[0]
    extra = pl.ds(pair_ref.shape[0] - 8, cells)

    def from_below(span):
        return jnp.where(even, next_ref[span], pair_ref[span])

    def from_above(span):
        return jnp.where(even, pair_ref[span], next_ref[span])

    def plane(place):
        return pl.ds(place * rows, rows)

    coarse_x, coarse_y = rows // 4, cols // 4
    fold_x = coarse_x // cells
    line_at = lax.broadcasted_iota(jnp.int32, (coarse_x, cols), 0)
    cell_at = lax.broadcasted_iota(jnp.int32, (coarse_x, cols), 1)
    on_line = cell_at // coarse_y == line_at % fold_x
    lines = []
    for coarse in (from_below(extra), sums_ref[...], from_above(extra)):
        tall = jnp.zeros((coarse_x, cols), jnp.float32)
        for at in range(cells):
            tall = jnp.where(line_at // fold_x == at, coarse[at : at + 1], tall)
        lines.append(jnp.where(on_line, tall, 0.0))
    lines = jnp.concatenate(lines, axis=0)
    spread_y = spread_y_ref[...]
    high, mid, low = (dot32(part, spread_y) for part in split3(lines))
    along_y = high + (mid + low)
    spread_zx = spread_zx_ref[...]
    high, mid, low = (dot32(spread_zx, part) for part in split3(along_y))
    growth_ref[...] = jnp.exp(high + (mid + low)).reshape(depth + 4, rows, cols)

    for place in range(2):
        dense_all[place] = from_below(plane(place))
        dense_all[place + depth + 2] = from_above(plane(place))
    dense_all[2 : depth + 2] = density_ref[...]
    for comp in range(3):
        loads[comp, 1] = from_below(plane(2 + comp))
        loads[comp, 2 : depth + 2] = load_ref[comp]
        for place in range(2):
            loads[comp, place + depth + 2] = from_above(plane(2 + 2 * comp + place))
    zero_rows = jnp.zeros((8, cols), jnp.float32)
    for target, first in ((fields, rows), (fields_y, rows), (far_at, 0)):
        for place, at in itertools.product(range(target.shape[0]), range(6)):
            target[place, at, first : first + 8] = zero_rows

    def stiffen(place, carry):
        dense = dense_all[place]
        missing = ((slab == 0) & (place < 2)) | ((slab == slabs - 1) & (place >= depth + 2))
        scale = jnp.where(missing, 0.0, UNIT)
        modulus = growth_ref[place] * (0.001 + dense * dense * dense) * scale
        elastic[place] = modulus
        along = modulus + shift_back(modulus, 1, first_col)
        around[place] = along + shift_back(along, 0, first_row)
        return carry

    lax.fori_loop(0, depth + 4, stiffen, 0, unroll=True)

    def start(place, carry):
        diagonal = (DIAGONAL / UNIT) * (around[place - 1] + around[place])
        missing = ((slab == 0) & (place == 1)) | ((slab == slabs - 1) & (place == depth + 3))
        inverse_here = 1.0 / jnp.where(missing, 1.0, diagonal)
        inverse[place - 1] = inverse_here
        for comp in range(3):
            value = loads[comp, place] * inverse_here
            z_ref[comp, place - 1] = value
            store_along_y(fields, place - 1, comp, value, last_col)
        return carry

    lax.fori_loop(1, depth + 4, start, 0, unroll=True)

    def first_product(chunk, carry):
        lower = load_spread(fields, 0, chunk)
        carried = None
        for place in range(1, depth + 3):
            upper = load_spread(fields, place, chunk)
            forces = modal_forces(element_modes(lower, upper), elastic[place, pl.ds(chunk * 8, 8)])
            passed = []
            for comp in range(3):
                sums = []
                for mode_x, mode_y in itertools.product((0, 1), repeat=2):
                    rise = forces[comp, (1, mode_x, mode_y)]
                    if mode_x or mode_y:
                        level = forces[comp, (0, mode_x, mode_y)]
                        near, far = level - rise, level + rise
                    else:
                        near, far = -rise, rise
                    if carried is not None:
                        sums.append(near + carried[4 * comp + 2 * mode_x + mode_y])
                    passed.append(far)
                if carried is not None:
                    for mode_y in range(2):
                        level, rise = sums[mode_y], sums[2 + mode_y]
                        near_at[place - 2, 2 * comp + mode_y, pl.ds(chunk * 8, 8)] = level - rise
                        far_at[place - 2, 2 * comp + mode_y, pl.ds(chunk * 8 + 8, 8)] = level + rise
            carried = passed
            lower = upper
        return carry

    lax.fori_loop(0, rows // 8, first_product, 0, unroll=True)

    def image_at(place, dots, own):
        dot_load, dot_zz, dot_zy = dots
        scale = inverse[place + 1]
        if not own:
            scale = jnp.where(slab < slabs - 1, scale, 0.0)
        for comp in range(3):
            along = [
                near_at[place, 2 * comp + mode_y] + far_at[place, 2 * comp + mode_y, 7 : rows + 7]
                for mode_y in range(2)
            ]
            image = (along[0] - along[1]) + shift_back(along[0] + along[1], 1, first_col)
            scaled = image * scale
            y_ref[comp, place] = scaled
            if own:
                value = z_ref[comp, place + 1]
                dot_load = dot_load + fold(loads[comp, place + 2] * value)
                dot_zz = dot_zz + fold(value * image)
                dot_zy = dot_zy + fold(scaled * image)
            store_along_y(fields_y, place, comp, scaled, last_col)
        return dot_load, dot_zz, dot_zy

    zeros = jnp.zeros((8, cols), jnp.float32)
    dot_load, dot_zz, dot_zy = lax.fori_loop(
        0, depth, lambda place, dots: image_at(place, dots, True), (zeros,) * 3, unroll=True
    )
    image_at(depth, (zeros,) * 3, False)

    def second_product(chunk, dot_yy):
        lower = load_spread(fields_y, 0, chunk)
        for place in range(depth):
            upper = load_spread(fields_y, place + 1, chunk)
            weight = elastic[place + 2, pl.ds(chunk * 8, 8)]
            dot_yy = dot_yy + weight * modal_energy(element_modes(lower, upper))
            lower = upper
        return dot_yy

    dot_yy = lax.fori_loop(0, rows // 8, second_product, zeros, unroll=True)
    lane_at = lax.broadcasted_iota(jnp.int32, (1, cols), 1)
    packed = jnp.zeros((1, cols), jnp.float32)
    for at, part in enumerate((dot_load, dot_zz, dot_zy, dot_yy)):
        packed = jnp.where(lane_at == at, jnp.sum(part, keepdims=True), packed)
    dots_ref[...] = jnp.broadcast_to(packed, dots_ref.shape)


def energy_kernel(z_ref, y_ref, growth_ref, density_ref, quad_ref, fields, fields_y):
    depth, rows, cols = density_ref.shape
    last_col = lax.broadcasted_iota(jnp.int32, (rows, cols), 1) == cols - 1
    zero_rows = jnp.zeros((8, cols), jnp.float32)

    def spread(place, carry):
        for source, first, target in ((z_ref, 1, fields), (y_ref, 0, fields_y)):
            for comp in range(3):
                store_along_y(target, place, comp, source[comp, place + first], last_col)
            for at in range(6):
                target[place, at, rows : rows + 8] = zero_rows
        return carry

    lax.fori_loop(0, depth + 1, spread, 0)

    def products(chunk, carry):
        span = pl.ds(chunk * 8, 8)
        lower, lower_y = load_spread(fields, 0, chunk), load_spread(fields_y, 0, chunk)
        for place in range(depth):
            upper, upper_y = load_spread(fields, place + 1, chunk), load_spread(fields_y, place + 1, chunk)
            hat, hat_y = element_modes(lower, upper), element_modes(lower_y, upper_y)
            dense = density_ref[place, span]
            weight = (-3.0 / 8.0 * UNIT) * dense * dense * growth_ref[place + 2, span]
            forces = modal_forces(hat, weight)
            quad_ref[0, place, span] = modal_product(hat, forces)
            quad_ref[1, place, span] = 2.0 * modal_product(hat_y, forces)
            quad_ref[2, place, span] = weight * modal_energy(hat_y)
            lower, lower_y = upper, upper_y
        return carry

    lax.fori_loop(0, rows // 8, products, 0)


def solve(dots_ref):
    dots = jnp.sum(dots_ref[...], axis=0, keepdims=True)
    lane_at = lax.broadcasted_iota(jnp.int32, dots.shape, 1)
    dot_load, dot_zz, dot_zy, dot_yy = (
        jnp.sum(jnp.where(lane_at == at, dots, 0.0), axis=1, keepdims=True) for at in range(4)
    )
    first = dot_zz / dot_load
    second = dot_zy / dot_load
    third = dot_yy / dot_load
    under = third * first - second * second
    along_z = (third - first * second) / under
    along_y = (first * first - second) / under
    return dot_load * (along_z + along_y * first), along_z, along_y


def terms_kernel(dots_ref, quad_ref, terms_ref):
    _, along_z, along_y = solve(dots_ref)
    squares = (along_z * along_z, along_z * along_y, along_y * along_y)
    samples, depth, share = terms_ref.shape[:3]
    for sample in range(samples):
        span = pl.ds(sample * share, share)
        for place in range(depth):
            terms_ref[sample, place] = sum(squares[at] * quad_ref[at, place, span] for at in range(3))


def displacement_kernel(dots_ref, z_ref, y_ref, displacement_ref, compliance_ref):
    compliance, along_z, along_y = solve(dots_ref)
    compliance_ref[0] = compliance[0, 0]
    for comp in range(3):
        for place in range(displacement_ref.shape[2]):
            displacement_ref[0, comp, place] = along_z * z_ref[comp, place + 1] + along_y * y_ref[comp, place]


def call(kernel, outs, inputs, scratch=(), in_memory=pltpu.VMEM, out_specs=None):
    return pl.pallas_call(
        kernel,
        out_shape=outs,
        in_specs=[pl.BlockSpec(memory_space=in_memory)] * inputs,
        out_specs=out_specs if out_specs is not None else [vmem_spec()] * len(outs),
        scratch_shapes=scratch,
        compiler_params=pltpu.CompilerParams(vmem_limit_bytes=VMEM_LIMIT),
    )


def per_device(load_field, density, mode_panels, mode_weight, mode_germs):
    depth, rows, cols = density.shape
    slabs = lax.axis_size("space")
    samples = lax.axis_size("sample")
    own_modes, _, cells = mode_panels.shape
    spread_y, spread_zx = weight_tables(depth, rows, cols)

    held_density, held_load = f32(depth, rows, cols), f32(3, depth, rows, cols)
    partial, density, load_field = call(
        first_kernel,
        [f32(samples, cells // 128, 128), held_density, held_load],
        inputs=5,
        scratch=[
            pltpu.VMEM((1, mode_weight.shape[0]), jnp.float32),
            pltpu.VMEM(mode_germs.shape, jnp.float32),
            pltpu.VMEM((own_modes, cells), jnp.bfloat16),
            pltpu.SemaphoreType.DMA((5,)),
        ],
        in_memory=pltpu.HBM,
    )(
        *(
            pltpu.with_memory_space_constraint(value, pltpu.HBM)
            for value in (
                mode_weight.reshape(1, -1),
                mode_germs,
                mode_panels.reshape(own_modes, cells),
                density,
                load_field,
            )
        )
    )
    parts = lax.all_to_all(partial, "sample", 0, 0, tiled=True)

    message = f32(8 * rows + 8, cols)
    sums, pair_out, next_out = call(pack_kernel, [f32(cells // 128, 128), message, message], inputs=3)(
        parts, density, load_field
    )
    pairs = [(at, at ^ 1) for at in range(slabs)]
    nexts = [(at, at + 1) for at in range(1, slabs - 1, 2)]
    nexts += [(target, source) for source, target in nexts]
    pair_in = lax.ppermute(pair_out, "space", pairs)
    next_in = lax.ppermute(next_out, "space", nexts)

    padded = pltpu.VMEM((depth + 1, 6, rows + 8, cols), jnp.float32)
    planes = pltpu.VMEM((depth + 4, rows, cols), jnp.float32)
    z_vec, y_vec, growth, dots = call(
        middle_kernel,
        [
            f32(3, depth + 3, rows, cols),
            f32(3, depth + 1, rows, cols),
            f32(depth + 4, rows, cols),
            f32(slabs, cols),
        ],
        inputs=7,
        scratch=[
            planes,
            planes,
            pltpu.VMEM((3, depth + 4, rows, cols), jnp.float32),
            planes,
            pltpu.VMEM((depth + 3, rows, cols), jnp.float32),
            pltpu.VMEM((depth + 3, 6, rows + 8, cols), jnp.float32),
            padded,
            pltpu.VMEM((depth + 1, 6, rows, cols), jnp.float32),
            padded,
        ],
    )(sums, density, load_field, pair_in, next_in, spread_y, spread_zx)
    dots = lax.all_to_all(dots, "space", 0, 0, tiled=True)
    (quads,) = call(energy_kernel, [f32(3, depth, rows, cols)], inputs=4, scratch=[padded, padded])(
        z_vec, y_vec, growth, density
    )
    (terms,) = call(terms_kernel, [f32(samples, depth, rows // samples, cols)], inputs=2)(dots, quads)
    terms = lax.all_to_all(terms, "sample", 0, 0, tiled=True)
    displacement, compliance = call(
        displacement_kernel,
        [f32(1, 3, depth, rows, cols), f32(1)],
        inputs=3,
        out_specs=[vmem_spec(), pl.BlockSpec(memory_space=pltpu.SMEM)],
    )(dots, z_vec, y_vec)
    return displacement, jnp.sum(terms, axis=0), compliance


def solution(mesh):
    placed = (
        P(None, "space", None, None),
        P("space", None, None),
        P("sample", "space", None),
        P(),
        P(),
    )
    return jax.shard_map(
        per_device,
        mesh=mesh,
        in_specs=placed,
        out_specs=(P("sample", None, "space", None, None), P("space", "sample", None), P("sample")),
        check_vma=False,
    )
```

```python
import itertools

import jax
import jax.numpy as jnp
import numpy as np
from jax import lax
from jax.experimental import pallas as pl
from jax.experimental.pallas import tpu as pltpu
from jax.sharding import PartitionSpec as P

POISSON = 0.3
LAME = POISSON / ((1.0 + POISSON) * (1.0 - 2.0 * POISSON))
SHEAR = 1.0 / (2.0 * (1.0 + POISSON))
DIAGONAL = (LAME + 2.0 * SHEAR) / 9.0 + 2.0 * SHEAR / 9.0
RATIO = LAME / SHEAR
UNIT = SHEAR / 16.0
VMEM_LIMIT = 48 * 1024 * 1024


def vmem_spec():
    return pl.BlockSpec(memory_space=pltpu.VMEM)


def f32(*shape):
    return jax.ShapeDtypeStruct(shape, jnp.float32)


def split3(value):
    high = value.astype(jnp.bfloat16)
    rest = value - high.astype(jnp.float32)
    mid = rest.astype(jnp.bfloat16)
    low = (rest - mid.astype(jnp.float32)).astype(jnp.bfloat16)
    return high, mid, low


def dot32(left, right):
    return jnp.dot(left, right, preferred_element_type=jnp.float32)


def weight_tables(depth, rows, cols):
    def hat(positions, cells):
        return np.maximum(0.0, 1.0 - np.abs(positions[:, None] - cells[None, :]))

    along_x = hat((np.arange(rows) + 0.5) / 4.0 - 0.5, np.arange(rows // 4))
    along_y = hat((np.arange(cols) + 0.5) / 4.0 - 0.5, np.arange(cols // 4))
    along_z = hat((np.arange(depth + 4) - 2 + 0.5) / 4.0 - 0.5, np.arange(-1, 2))
    spread_y = np.tile(along_y.T, (4, 1))
    spread_zx = np.einsum("pc,xd->pxcd", along_z, along_x).reshape((depth + 4) * rows, -1)
    return spread_y.astype(jnp.bfloat16), spread_zx.astype(jnp.bfloat16)


def first_kernel(
    weight_hbm, germs_hbm, panels_hbm, density_hbm, load_hbm,
    partial_ref, density_ref, load_ref,
    weight, germs, panels, sems,
):
    sample = lax.axis_index("sample")
    copies = [
        pltpu.make_async_copy(source, target, sems.at[at])
        for at, (source, target) in enumerate(
            (
                (weight_hbm, weight),
                (germs_hbm, germs),
                (panels_hbm, panels),
                (density_hbm, density_ref),
                (load_hbm, load_ref),
            )
        )
    ]
    for copy in copies:
        copy.start()
    own_modes = panels.shape[0]
    modes = germs.shape[1]
    mode_at = lax.broadcasted_iota(jnp.int32, (modes, own_modes), 0)
    slot_at = lax.broadcasted_iota(jnp.int32, (modes, own_modes), 1)
    pick = jnp.where(mode_at == slot_at + sample * own_modes, 1.0, 0.0).astype(jnp.bfloat16)
    for copy in copies[:3]:
        copy.wait()
    coefficients = (weight[...] * germs[...]).astype(jnp.bfloat16)
    own_coeff = dot32(coefficients, pick).astype(jnp.bfloat16)
    partial = dot32(own_coeff, panels[...])
    for at in range(partial_ref.shape[1]):
        partial_ref[:, at] = partial[:, at * 128 : (at + 1) * 128]
    for copy in copies[3:]:
        copy.wait()


def pack_kernel(parts_ref, density_ref, load_ref, sums_ref, up_ref, down_ref):
    rows = density_ref.shape[1]
    depth = density_ref.shape[0]
    cells = parts_ref.shape[1]
    sums = jnp.sum(parts_ref[...], axis=0)
    sums_ref[...] = sums
    up = [density_ref[depth - 2], density_ref[depth - 1]]
    up += [load_ref[comp, depth - 1] for comp in range(3)]
    down = [density_ref[0], density_ref[1]]
    down += [load_ref[comp, place] for comp in range(3) for place in range(2)]
    for ref, parts in ((up_ref, up), (down_ref, down)):
        for at, part in enumerate(parts):
            ref[at * rows : (at + 1) * rows] = part
        first = len(parts) * rows
        ref[first : first + cells] = sums
        ref[first + cells :] = jnp.zeros((8 - cells, sums.shape[1]), jnp.float32)


def shift_ahead(value, axis, mask):
    return jnp.where(mask, 0.0, pltpu.roll(value, value.shape[axis] - 1, axis))


def shift_back(value, axis, mask):
    return jnp.where(mask, 0.0, pltpu.roll(value, 1, axis))


def store_along_y(target, place, comp, value, last_col):
    ahead = shift_ahead(value, 1, last_col)
    target[place, 2 * comp, 0 : value.shape[0]] = value + ahead
    target[place, 2 * comp + 1, 0 : value.shape[0]] = ahead - value


def load_spread(source, place, chunk):
    parts = []
    for comp in range(3):
        here = [source[place, 2 * comp + mode, pl.ds(chunk * 8, 8)] for mode in range(2)]
        ahead = [source[place, 2 * comp + mode, pl.ds(chunk * 8 + 1, 8)] for mode in range(2)]
        parts += [one + two for one, two in zip(here, ahead)]
        parts += [two - one for one, two in zip(here, ahead)]
    return parts


def element_modes(lower, upper):
    hat = {}
    for comp in range(3):
        for mode_x, mode_y in itertools.product((0, 1), repeat=2):
            at = 4 * comp + 2 * mode_x + mode_y
            if mode_x or mode_y:
                hat[comp, (0, mode_x, mode_y)] = lower[at] + upper[at]
            hat[comp, (1, mode_x, mode_y)] = upper[at] - lower[at]
    return hat


def mode(*axes):
    return tuple(int(axis in axes) for axis in range(3))


def modal_parts(hat):
    shear = {
        (one, two): hat[one, mode(two)] + hat[two, mode(one)] for one, two in ((0, 1), (0, 2), (1, 2))
    }
    trace = hat[0, mode(0)] + hat[1, mode(1)] + hat[2, mode(2)]
    twist = [hat[axis, mode(*(other for other in range(3) if other != axis))] for axis in range(3)]
    bends = {}
    for across in range(3):
        one, two = (axis for axis in range(3) if axis != across)
        bends[across] = (one, two, hat[one, mode(one, across)] + hat[two, mode(two, across)])
    return shear, trace, twist, bends


def modal_forces(hat, weight):
    shear, trace, twist, bends = modal_parts(hat)
    forces = {}
    for (one, two), value in shear.items():
        forces[one, mode(two)] = forces[two, mode(one)] = value * weight
    level = RATIO * trace
    for axis in range(3):
        forces[axis, mode(axis)] = (2.0 * hat[axis, mode(axis)] + level) * weight
    third = (1.0 / 3.0) * weight
    both = twist[0] + twist[1] + twist[2]
    for axis in range(3):
        place = mode(*(other for other in range(3) if other != axis))
        forces[axis, place] = (twist[axis] + both) * third
    for across, (one, two, total) in bends.items():
        extra = (RATIO / 3.0) * total
        for axis in (one, two):
            place = mode(axis, across)
            forces[axis, place] = (hat[axis, place] + extra) * weight
    last = ((RATIO + 4.0) / 9.0) * weight
    for axis in range(3):
        forces[axis, (1, 1, 1)] = hat[axis, (1, 1, 1)] * last
    return forces


def total_of(values):
    values = list(values)
    while len(values) > 1:
        paired = [one + two for one, two in zip(values[::2], values[1::2])]
        values = paired + ([values[-1]] if len(values) % 2 else [])
    return values[0]


def modal_product(left, right):
    return total_of(left[key] * value for key, value in right.items())


def modal_energy(hat):
    shear, trace, twist, bends = modal_parts(hat)

    def squares(values):
        return total_of(value * value for value in values)

    both = twist[0] + twist[1] + twist[2]
    whole = list(shear.values())
    for across, (one, two, _) in bends.items():
        whole += [hat[one, mode(one, across)], hat[two, mode(two, across)]]
    return total_of(
        [
            squares(whole),
            2.0 * squares(hat[axis, mode(axis)] for axis in range(3)),
            RATIO * (trace * trace),
            (1.0 / 3.0) * squares(twist + [both]),
            (RATIO / 3.0) * squares(total for _, _, total in bends.values()),
            ((RATIO + 4.0) / 9.0) * squares(hat[axis, (1, 1, 1)] for axis in range(3)),
        ]
    )


def fold(plane):
    return jnp.sum(plane.reshape(-1, 8, plane.shape[-1]), axis=0)


def middle_kernel(
    sums_ref, density_ref, load_ref, below_ref, above_ref, spread_y_ref, spread_zx_ref,
    z_ref, y_ref, growth_ref, dots_ref,
    elastic, dense_all, loads, around, inverse, fields, fields_y, near_at, far_at,
):
    slab = lax.axis_index("space")
    slabs = lax.axis_size("space")
    depth, rows, cols = density_ref.shape
    row_at = lax.broadcasted_iota(jnp.int32, (rows, cols), 0)
    col_at = lax.broadcasted_iota(jnp.int32, (rows, cols), 1)
    first_row = row_at == 0
    first_col, last_col = col_at == 0, col_at == cols - 1
    cells = sums_ref.shape[0]
    def from_below(span):
        return below_ref[span]

    def from_above(span):
        return above_ref[span]

    def plane(place):
        return pl.ds(place * rows, rows)

    coarse_x, coarse_y = rows // 4, cols // 4
    fold_x = coarse_x // cells
    line_at = lax.broadcasted_iota(jnp.int32, (coarse_x, cols), 0)
    cell_at = lax.broadcasted_iota(jnp.int32, (coarse_x, cols), 1)
    on_line = cell_at // coarse_y == line_at % fold_x
    lines = []
    for coarse in (from_below(pl.ds(5 * rows, cells)), sums_ref[...], from_above(pl.ds(8 * rows, cells))):
        tall = jnp.zeros((coarse_x, cols), jnp.float32)
        for at in range(cells):
            tall = jnp.where(line_at // fold_x == at, coarse[at : at + 1], tall)
        lines.append(jnp.where(on_line, tall, 0.0))
    lines = jnp.concatenate(lines, axis=0)
    spread_y = spread_y_ref[...]
    high, mid, low = (dot32(part, spread_y) for part in split3(lines))
    along_y = high + (mid + low)
    spread_zx = spread_zx_ref[...]
    high, mid, low = (dot32(spread_zx, part) for part in split3(along_y))
    growth_ref[...] = jnp.exp(high + (mid + low)).reshape(depth + 4, rows, cols)

    for place in range(2):
        dense_all[place] = from_below(plane(place))
        dense_all[place + depth + 2] = from_above(plane(place))
    dense_all[2 : depth + 2] = density_ref[...]
    for comp in range(3):
        loads[comp, 1] = from_below(plane(2 + comp))
        loads[comp, 2 : depth + 2] = load_ref[comp]
        for place in range(2):
            loads[comp, place + depth + 2] = from_above(plane(2 + 2 * comp + place))
    zero_rows = jnp.zeros((8, cols), jnp.float32)
    for target, first in ((fields, rows), (fields_y, rows), (far_at, 0)):
        for place, at in itertools.product(range(target.shape[0]), range(6)):
            target[place, at, first : first + 8] = zero_rows

    def stiffen(place, carry):
        dense = dense_all[place]
        missing = ((slab == 0) & (place < 2)) | ((slab == slabs - 1) & (place >= depth + 2))
        scale = jnp.where(missing, 0.0, UNIT)
        modulus = growth_ref[place] * (0.001 + dense * dense * dense) * scale
        elastic[place] = modulus
        along = modulus + shift_back(modulus, 1, first_col)
        around[place] = along + shift_back(along, 0, first_row)
        return carry

    lax.fori_loop(0, depth + 4, stiffen, 0, unroll=True)

    def start(place, carry):
        diagonal = (DIAGONAL / UNIT) * (around[place - 1] + around[place])
        missing = ((slab == 0) & (place == 1)) | ((slab == slabs - 1) & (place == depth + 3))
        inverse_here = 1.0 / jnp.where(missing, 1.0, diagonal)
        inverse[place - 1] = inverse_here
        for comp in range(3):
            value = loads[comp, place] * inverse_here
            z_ref[comp, place - 1] = value
            store_along_y(fields, place - 1, comp, value, last_col)
        return carry

    lax.fori_loop(1, depth + 4, start, 0, unroll=True)

    def first_product(chunk, carry):
        lower = load_spread(fields, 0, chunk)
        carried = None
        for place in range(1, depth + 3):
            upper = load_spread(fields, place, chunk)
            forces = modal_forces(element_modes(lower, upper), elastic[place, pl.ds(chunk * 8, 8)])
            passed = []
            for comp in range(3):
                sums = []
                for mode_x, mode_y in itertools.product((0, 1), repeat=2):
                    rise = forces[comp, (1, mode_x, mode_y)]
                    if mode_x or mode_y:
                        level = forces[comp, (0, mode_x, mode_y)]
                        near, far = level - rise, level + rise
                    else:
                        near, far = -rise, rise
                    if carried is not None:
                        sums.append(near + carried[4 * comp + 2 * mode_x + mode_y])
                    passed.append(far)
                if carried is not None:
                    for mode_y in range(2):
                        level, rise = sums[mode_y], sums[2 + mode_y]
                        near_at[place - 2, 2 * comp + mode_y, pl.ds(chunk * 8, 8)] = level - rise
                        far_at[place - 2, 2 * comp + mode_y, pl.ds(chunk * 8 + 8, 8)] = level + rise
            carried = passed
            lower = upper
        return carry

    lax.fori_loop(0, rows // 8, first_product, 0, unroll=True)

    def image_at(place, dots, own):
        dot_load, dot_zz, dot_zy = dots
        scale = inverse[place + 1]
        if not own:
            scale = jnp.where(slab < slabs - 1, scale, 0.0)
        for comp in range(3):
            along = [
                near_at[place, 2 * comp + mode_y] + far_at[place, 2 * comp + mode_y, 7 : rows + 7]
                for mode_y in range(2)
            ]
            image = (along[0] - along[1]) + shift_back(along[0] + along[1], 1, first_col)
            scaled = image * scale
            y_ref[comp, place] = scaled
            if own:
                value = z_ref[comp, place + 1]
                dot_load = dot_load + fold(loads[comp, place + 2] * value)
                dot_zz = dot_zz + fold(value * image)
                dot_zy = dot_zy + fold(scaled * image)
            store_along_y(fields_y, place, comp, scaled, last_col)
        return dot_load, dot_zz, dot_zy

    zeros = jnp.zeros((8, cols), jnp.float32)
    dot_load, dot_zz, dot_zy = lax.fori_loop(
        0, depth, lambda place, dots: image_at(place, dots, True), (zeros,) * 3, unroll=True
    )
    image_at(depth, (zeros,) * 3, False)

    def second_product(chunk, dot_yy):
        lower = load_spread(fields_y, 0, chunk)
        for place in range(depth):
            upper = load_spread(fields_y, place + 1, chunk)
            weight = elastic[place + 2, pl.ds(chunk * 8, 8)]
            dot_yy = dot_yy + weight * modal_energy(element_modes(lower, upper))
            lower = upper
        return dot_yy

    dot_yy = lax.fori_loop(0, rows // 8, second_product, zeros, unroll=True)
    lane_at = lax.broadcasted_iota(jnp.int32, (1, cols), 1)
    packed = jnp.zeros((1, cols), jnp.float32)
    for at, part in enumerate((dot_load, dot_zz, dot_zy, dot_yy)):
        packed = jnp.where(lane_at == at, jnp.sum(part, keepdims=True), packed)
    dots_ref[...] = jnp.broadcast_to(packed, dots_ref.shape)


def energy_kernel(z_ref, y_ref, growth_ref, density_ref, quad_ref, fields, fields_y):
    depth, rows, cols = density_ref.shape
    last_col = lax.broadcasted_iota(jnp.int32, (rows, cols), 1) == cols - 1
    zero_rows = jnp.zeros((8, cols), jnp.float32)

    def spread(place, carry):
        for source, first, target in ((z_ref, 1, fields), (y_ref, 0, fields_y)):
            for comp in range(3):
                store_along_y(target, place, comp, source[comp, place + first], last_col)
            for at in range(6):
                target[place, at, rows : rows + 8] = zero_rows
        return carry

    lax.fori_loop(0, depth + 1, spread, 0)

    def products(chunk, carry):
        span = pl.ds(chunk * 8, 8)
        lower, lower_y = load_spread(fields, 0, chunk), load_spread(fields_y, 0, chunk)
        for place in range(depth):
            upper, upper_y = load_spread(fields, place + 1, chunk), load_spread(fields_y, place + 1, chunk)
            hat, hat_y = element_modes(lower, upper), element_modes(lower_y, upper_y)
            dense = density_ref[place, span]
            weight = (-3.0 / 8.0 * UNIT) * dense * dense * growth_ref[place + 2, span]
            forces = modal_forces(hat, weight)
            quad_ref[0, place, span] = modal_product(hat, forces)
            quad_ref[1, place, span] = 2.0 * modal_product(hat_y, forces)
            quad_ref[2, place, span] = weight * modal_energy(hat_y)
            lower, lower_y = upper, upper_y
        return carry

    lax.fori_loop(0, rows // 8, products, 0)


def solve(dots_ref):
    dots = jnp.sum(dots_ref[...], axis=0, keepdims=True)
    lane_at = lax.broadcasted_iota(jnp.int32, dots.shape, 1)
    dot_load, dot_zz, dot_zy, dot_yy = (
        jnp.sum(jnp.where(lane_at == at, dots, 0.0), axis=1, keepdims=True) for at in range(4)
    )
    first = dot_zz / dot_load
    second = dot_zy / dot_load
    third = dot_yy / dot_load
    under = third * first - second * second
    along_z = (third - first * second) / under
    along_y = (first * first - second) / under
    return dot_load * (along_z + along_y * first), along_z, along_y


def terms_kernel(dots_ref, quad_ref, terms_ref):
    _, along_z, along_y = solve(dots_ref)
    squares = (along_z * along_z, along_z * along_y, along_y * along_y)
    samples, depth, share = terms_ref.shape[:3]
    for sample in range(samples):
        span = pl.ds(sample * share, share)
        for place in range(depth):
            terms_ref[sample, place] = sum(squares[at] * quad_ref[at, place, span] for at in range(3))


def last_kernel(
    terms_ref, dots_ref, z_ref, y_ref, displacement_ref, gradient_ref, compliance_ref
):
    compliance, along_z, along_y = solve(dots_ref)
    compliance_ref[...] = compliance
    gradient_ref[...] = jnp.sum(terms_ref[...], axis=0)
    for comp in range(3):
        for place in range(displacement_ref.shape[2]):
            displacement_ref[0, comp, place] = along_z * z_ref[comp, place + 1] + along_y * y_ref[comp, place]


def call(kernel, outs, inputs, scratch=(), in_memory=pltpu.VMEM, out_specs=None):
    return pl.pallas_call(
        kernel,
        out_shape=outs,
        in_specs=[pl.BlockSpec(memory_space=in_memory)] * inputs,
        out_specs=out_specs if out_specs is not None else [vmem_spec()] * len(outs),
        scratch_shapes=scratch,
        compiler_params=pltpu.CompilerParams(vmem_limit_bytes=VMEM_LIMIT),
    )


def per_device(load_field, density, mode_panels, mode_weight, mode_germs):
    depth, rows, cols = density.shape
    slabs = lax.axis_size("space")
    samples = lax.axis_size("sample")
    own_modes, _, cells = mode_panels.shape
    spread_y, spread_zx = weight_tables(depth, rows, cols)

    held_density, held_load = f32(depth, rows, cols), f32(3, depth, rows, cols)
    partial, density, load_field = call(
        first_kernel,
        [f32(samples, cells // 128, 128), held_density, held_load],
        inputs=5,
        scratch=[
            pltpu.VMEM((1, mode_weight.shape[0]), jnp.float32),
            pltpu.VMEM(mode_germs.shape, jnp.float32),
            pltpu.VMEM((own_modes, cells), jnp.bfloat16),
            pltpu.SemaphoreType.DMA((5,)),
        ],
        in_memory=pltpu.HBM,
    )(
        *(
            pltpu.with_memory_space_constraint(value, pltpu.HBM)
            for value in (
                mode_weight.reshape(1, -1),
                mode_germs,
                mode_panels.reshape(own_modes, cells),
                density,
                load_field,
            )
        )
    )
    parts = lax.all_to_all(partial, "sample", 0, 0, tiled=True)

    sums, up, down = call(
        pack_kernel,
        [f32(cells // 128, 128), f32(5 * rows + 8, cols), f32(8 * rows + 8, cols)],
        inputs=3,
    )(parts, density, load_field)
    below = lax.ppermute(up, "space", [(at, at + 1) for at in range(slabs - 1)])
    above = lax.ppermute(down, "space", [(at + 1, at) for at in range(slabs - 1)])

    padded = pltpu.VMEM((depth + 1, 6, rows + 8, cols), jnp.float32)
    planes = pltpu.VMEM((depth + 4, rows, cols), jnp.float32)
    z_vec, y_vec, growth, dots = call(
        middle_kernel,
        [
            f32(3, depth + 3, rows, cols),
            f32(3, depth + 1, rows, cols),
            f32(depth + 4, rows, cols),
            f32(slabs, cols),
        ],
        inputs=7,
        scratch=[
            planes,
            planes,
            pltpu.VMEM((3, depth + 4, rows, cols), jnp.float32),
            planes,
            pltpu.VMEM((depth + 3, rows, cols), jnp.float32),
            pltpu.VMEM((depth + 3, 6, rows + 8, cols), jnp.float32),
            padded,
            pltpu.VMEM((depth + 1, 6, rows, cols), jnp.float32),
            padded,
        ],
    )(sums, density, load_field, below, above, spread_y, spread_zx)
    dots = lax.all_to_all(dots, "space", 0, 0, tiled=True)
    (quads,) = call(energy_kernel, [f32(3, depth, rows, cols)], inputs=4, scratch=[padded, padded])(
        z_vec, y_vec, growth, density
    )
    (terms,) = call(terms_kernel, [f32(samples, depth, rows // samples, cols)], inputs=2)(dots, quads)
    terms = lax.all_to_all(terms, "sample", 0, 0, tiled=True)
    displacement, gradient, compliance = call(
        last_kernel,
        [f32(1, 3, depth, rows, cols), f32(depth, rows // samples, cols), f32(1, 1)],
        inputs=4,
    )(terms, dots, z_vec, y_vec)
    return displacement, gradient, compliance.reshape(1)


def solution(mesh):
    placed = (
        P(None, "space", None, None),
        P("space", None, None),
        P("sample", "space", None),
        P(),
        P(),
    )
    return jax.shard_map(
        per_device,
        mesh=mesh,
        in_specs=placed,
        out_specs=(P("sample", None, "space", None, None), P("space", "sample", None), P("sample")),
        check_vma=False,
    )
```

```python
import itertools

import jax
import jax.numpy as jnp
import numpy as np
from jax import lax
from jax.experimental import pallas as pl
from jax.experimental.pallas import tpu as pltpu
from jax.sharding import PartitionSpec as P

POISSON = 0.3
LAME = POISSON / ((1.0 + POISSON) * (1.0 - 2.0 * POISSON))
SHEAR = 1.0 / (2.0 * (1.0 + POISSON))
DIAGONAL = (LAME + 2.0 * SHEAR) / 9.0 + 2.0 * SHEAR / 9.0
RATIO = LAME / SHEAR
UNIT = SHEAR / 16.0
VMEM_LIMIT = 48 * 1024 * 1024


def vmem_spec():
    return pl.BlockSpec(memory_space=pltpu.VMEM)


def f32(*shape):
    return jax.ShapeDtypeStruct(shape, jnp.float32)


def split3(value):
    high = value.astype(jnp.bfloat16)
    rest = value - high.astype(jnp.float32)
    mid = rest.astype(jnp.bfloat16)
    low = (rest - mid.astype(jnp.float32)).astype(jnp.bfloat16)
    return high, mid, low


def dot32(left, right):
    return jnp.dot(left, right, preferred_element_type=jnp.float32)


def weight_tables(depth, rows, cols):
    def hat(positions, cells):
        return np.maximum(0.0, 1.0 - np.abs(positions[:, None] - cells[None, :]))

    along_x = hat((np.arange(rows) + 0.5) / 4.0 - 0.5, np.arange(rows // 4))
    along_y = hat((np.arange(cols) + 0.5) / 4.0 - 0.5, np.arange(cols // 4))
    along_z = hat((np.arange(depth + 4) - 2 + 0.5) / 4.0 - 0.5, np.arange(-1, 2))
    spread_y = np.tile(along_y.T, (4, 1))
    spread_zx = np.einsum("pc,xd->pxcd", along_z, along_x).reshape((depth + 4) * rows, -1)
    return spread_y.astype(jnp.bfloat16), spread_zx.astype(jnp.bfloat16)


def first_kernel(
    weight_hbm, germs_hbm, panels_hbm, density_hbm, load_hbm,
    partial_ref, density_ref, load_ref,
    weight, germs, panels, sems,
):
    sample = lax.axis_index("sample")
    copies = [
        pltpu.make_async_copy(source, target, sems.at[at])
        for at, (source, target) in enumerate(
            (
                (weight_hbm, weight),
                (germs_hbm, germs),
                (panels_hbm, panels),
                (density_hbm, density_ref),
                (load_hbm, load_ref),
            )
        )
    ]
    for copy in copies:
        copy.start()
    own_modes = panels.shape[0]
    modes = germs.shape[1]
    mode_at = lax.broadcasted_iota(jnp.int32, (modes, own_modes), 0)
    slot_at = lax.broadcasted_iota(jnp.int32, (modes, own_modes), 1)
    pick = jnp.where(mode_at == slot_at + sample * own_modes, 1.0, 0.0).astype(jnp.bfloat16)
    for copy in copies[:3]:
        copy.wait()
    coefficients = (weight[...] * germs[...]).astype(jnp.bfloat16)
    own_coeff = dot32(coefficients, pick).astype(jnp.bfloat16)
    partial = dot32(own_coeff, panels[...])
    for at in range(partial_ref.shape[1]):
        partial_ref[:, at] = partial[:, at * 128 : (at + 1) * 128]
    for copy in copies[3:]:
        copy.wait()


def pack_kernel(parts_ref, density_ref, load_ref, sums_ref, up_ref, down_ref):
    rows = density_ref.shape[1]
    depth = density_ref.shape[0]
    cells = parts_ref.shape[1]
    sums = jnp.sum(parts_ref[...], axis=0)
    sums_ref[...] = sums
    up = [density_ref[depth - 2], density_ref[depth - 1]]
    up += [load_ref[comp, depth - 1] for comp in range(3)]
    down = [density_ref[0], density_ref[1]]
    down += [load_ref[comp, place] for comp in range(3) for place in range(2)]
    for ref, parts in ((up_ref, up), (down_ref, down)):
        for at, part in enumerate(parts):
            ref[at * rows : (at + 1) * rows] = part
        first = len(parts) * rows
        ref[first : first + cells] = sums
        ref[first + cells :] = jnp.zeros((8 - cells, sums.shape[1]), jnp.float32)


def shift_ahead(value, axis, mask):
    return jnp.where(mask, 0.0, pltpu.roll(value, value.shape[axis] - 1, axis))


def shift_back(value, axis, mask):
    return jnp.where(mask, 0.0, pltpu.roll(value, 1, axis))


def store_along_y(target, place, comp, value, last_col):
    ahead = shift_ahead(value, 1, last_col)
    target[place, 2 * comp, 0 : value.shape[0]] = value + ahead
    target[place, 2 * comp + 1, 0 : value.shape[0]] = ahead - value


def load_spread(source, place, chunk):
    parts = []
    for comp in range(3):
        here = [source[place, 2 * comp + mode, pl.ds(chunk * 8, 8)] for mode in range(2)]
        ahead = [source[place, 2 * comp + mode, pl.ds(chunk * 8 + 1, 8)] for mode in range(2)]
        parts += [one + two for one, two in zip(here, ahead)]
        parts += [two - one for one, two in zip(here, ahead)]
    return parts


def element_modes(lower, upper):
    hat = {}
    for comp in range(3):
        for mode_x, mode_y in itertools.product((0, 1), repeat=2):
            at = 4 * comp + 2 * mode_x + mode_y
            if mode_x or mode_y:
                hat[comp, (0, mode_x, mode_y)] = lower[at] + upper[at]
            hat[comp, (1, mode_x, mode_y)] = upper[at] - lower[at]
    return hat


def mode(*axes):
    return tuple(int(axis in axes) for axis in range(3))


def modal_parts(hat):
    shear = {
        (one, two): hat[one, mode(two)] + hat[two, mode(one)] for one, two in ((0, 1), (0, 2), (1, 2))
    }
    trace = hat[0, mode(0)] + hat[1, mode(1)] + hat[2, mode(2)]
    twist = [hat[axis, mode(*(other for other in range(3) if other != axis))] for axis in range(3)]
    bends = {}
    for across in range(3):
        one, two = (axis for axis in range(3) if axis != across)
        bends[across] = (one, two, hat[one, mode(one, across)] + hat[two, mode(two, across)])
    return shear, trace, twist, bends


def modal_forces(hat, weight):
    shear, trace, twist, bends = modal_parts(hat)
    forces = {}
    for (one, two), value in shear.items():
        forces[one, mode(two)] = forces[two, mode(one)] = value * weight
    level = RATIO * trace
    for axis in range(3):
        forces[axis, mode(axis)] = (2.0 * hat[axis, mode(axis)] + level) * weight
    third = (1.0 / 3.0) * weight
    both = twist[0] + twist[1] + twist[2]
    for axis in range(3):
        place = mode(*(other for other in range(3) if other != axis))
        forces[axis, place] = (twist[axis] + both) * third
    for across, (one, two, total) in bends.items():
        extra = (RATIO / 3.0) * total
        for axis in (one, two):
            place = mode(axis, across)
            forces[axis, place] = (hat[axis, place] + extra) * weight
    last = ((RATIO + 4.0) / 9.0) * weight
    for axis in range(3):
        forces[axis, (1, 1, 1)] = hat[axis, (1, 1, 1)] * last
    return forces


def total_of(values):
    values = list(values)
    while len(values) > 1:
        paired = [one + two for one, two in zip(values[::2], values[1::2])]
        values = paired + ([values[-1]] if len(values) % 2 else [])
    return values[0]


def modal_product(left, right):
    return total_of(left[key] * value for key, value in right.items())


def modal_energy(hat):
    shear, trace, twist, bends = modal_parts(hat)

    def squares(values):
        return total_of(value * value for value in values)

    both = twist[0] + twist[1] + twist[2]
    whole = list(shear.values())
    for across, (one, two, _) in bends.items():
        whole += [hat[one, mode(one, across)], hat[two, mode(two, across)]]
    return total_of(
        [
            squares(whole),
            2.0 * squares(hat[axis, mode(axis)] for axis in range(3)),
            RATIO * (trace * trace),
            (1.0 / 3.0) * squares(twist + [both]),
            (RATIO / 3.0) * squares(total for _, _, total in bends.values()),
            ((RATIO + 4.0) / 9.0) * squares(hat[axis, (1, 1, 1)] for axis in range(3)),
        ]
    )


def fold(plane):
    return jnp.sum(plane.reshape(-1, 8, plane.shape[-1]), axis=0)


def middle_kernel(
    sums_ref, density_ref, load_ref, below_ref, above_ref, spread_y_ref, spread_zx_ref,
    z_ref, y_ref, growth_ref, dots_ref,
    elastic, around, inverse, fields, fields_y, near_at, far_at,
):
    slab = lax.axis_index("space")
    slabs = lax.axis_size("space")
    depth, rows, cols = density_ref.shape
    row_at = lax.broadcasted_iota(jnp.int32, (rows, cols), 0)
    col_at = lax.broadcasted_iota(jnp.int32, (rows, cols), 1)
    first_row = row_at == 0
    first_col, last_col = col_at == 0, col_at == cols - 1
    cells = sums_ref.shape[0]
    def from_below(span):
        return below_ref[span]

    def from_above(span):
        return above_ref[span]

    def plane(place):
        return pl.ds(place * rows, rows)

    coarse_x, coarse_y = rows // 4, cols // 4
    fold_x = coarse_x // cells
    line_at = lax.broadcasted_iota(jnp.int32, (coarse_x, cols), 0)
    cell_at = lax.broadcasted_iota(jnp.int32, (coarse_x, cols), 1)
    on_line = cell_at // coarse_y == line_at % fold_x
    lines = []
    for coarse in (from_below(pl.ds(5 * rows, cells)), sums_ref[...], from_above(pl.ds(8 * rows, cells))):
        tall = jnp.zeros((coarse_x, cols), jnp.float32)
        for at in range(cells):
            tall = jnp.where(line_at // fold_x == at, coarse[at : at + 1], tall)
        lines.append(jnp.where(on_line, tall, 0.0))
    lines = jnp.concatenate(lines, axis=0)
    spread_y = spread_y_ref[...]
    high, mid, low = (dot32(part, spread_y) for part in split3(lines))
    along_y = high + (mid + low)
    spread_zx = spread_zx_ref[...]
    high, mid, low = (dot32(spread_zx, part) for part in split3(along_y))
    growth_ref[...] = jnp.exp(high + (mid + low)).reshape(depth + 4, rows, cols)

    def dense_at(place):
        if place < 2:
            return from_below(plane(place))
        return density_ref[place - 2] if place < depth + 2 else from_above(plane(place - depth - 2))

    def load_at(comp, place):
        if place < 2:
            return from_below(plane(2 + comp))
        if place < depth + 2:
            return load_ref[comp, place - 2]
        return from_above(plane(2 + 2 * comp + place - depth - 2))

    zero_rows = jnp.zeros((8, cols), jnp.float32)
    for target, first in ((fields, rows), (fields_y, rows), (far_at, 0)):
        for place, at in itertools.product(range(target.shape[0]), range(6)):
            target[place, at, first : first + 8] = zero_rows

    for place in range(depth + 4):
        dense = dense_at(place)
        modulus = growth_ref[place] * (0.001 + dense * dense * dense)
        if place < 2:
            modulus = modulus * jnp.where(slab == 0, 0.0, UNIT)
        elif place >= depth + 2:
            modulus = modulus * jnp.where(slab == slabs - 1, 0.0, UNIT)
        else:
            modulus = modulus * UNIT
        elastic[place] = modulus
        along = modulus + shift_back(modulus, 1, first_col)
        around[place] = along + shift_back(along, 0, first_row)

    for place in range(1, depth + 4):
        diagonal = (DIAGONAL / UNIT) * (around[place - 1] + around[place])
        if place == 1:
            diagonal = jnp.where(slab == 0, 1.0, diagonal)
        if place == depth + 3:
            diagonal = jnp.where(slab == slabs - 1, 1.0, diagonal)
        inverse_here = 1.0 / diagonal
        inverse[place - 1] = inverse_here
        for comp in range(3):
            value = load_at(comp, place) * inverse_here
            z_ref[comp, place - 1] = value
            store_along_y(fields, place - 1, comp, value, last_col)

    def first_product(chunk, carry):
        lower = load_spread(fields, 0, chunk)
        carried = None
        for place in range(1, depth + 3):
            upper = load_spread(fields, place, chunk)
            forces = modal_forces(element_modes(lower, upper), elastic[place, pl.ds(chunk * 8, 8)])
            passed = []
            for comp in range(3):
                sums = []
                for mode_x, mode_y in itertools.product((0, 1), repeat=2):
                    rise = forces[comp, (1, mode_x, mode_y)]
                    if mode_x or mode_y:
                        level = forces[comp, (0, mode_x, mode_y)]
                        near, far = level - rise, level + rise
                    else:
                        near, far = -rise, rise
                    if carried is not None:
                        sums.append(near + carried[4 * comp + 2 * mode_x + mode_y])
                    passed.append(far)
                if carried is not None:
                    for mode_y in range(2):
                        level, rise = sums[mode_y], sums[2 + mode_y]
                        near_at[place - 2, 2 * comp + mode_y, pl.ds(chunk * 8, 8)] = level - rise
                        far_at[place - 2, 2 * comp + mode_y, pl.ds(chunk * 8 + 8, 8)] = level + rise
            carried = passed
            lower = upper
        return carry

    lax.fori_loop(0, rows // 8, first_product, 0, unroll=2)

    def image_at(place, dots, own):
        dot_load, dot_zz, dot_zy = dots
        scale = inverse[place + 1]
        if not own:
            scale = jnp.where(slab < slabs - 1, scale, 0.0)
        for comp in range(3):
            along = [
                near_at[place, 2 * comp + mode_y] + far_at[place, 2 * comp + mode_y, 7 : rows + 7]
                for mode_y in range(2)
            ]
            image = (along[0] - along[1]) + shift_back(along[0] + along[1], 1, first_col)
            scaled = image * scale
            y_ref[comp, place] = scaled
            if own:
                value = z_ref[comp, place + 1]
                dot_load = dot_load + fold(load_ref[comp, place] * value)
                dot_zz = dot_zz + fold(value * image)
                dot_zy = dot_zy + fold(scaled * image)
            store_along_y(fields_y, place, comp, scaled, last_col)
        return dot_load, dot_zz, dot_zy

    zeros = jnp.zeros((8, cols), jnp.float32)
    dot_load, dot_zz, dot_zy = lax.fori_loop(
        0, depth, lambda place, dots: image_at(place, dots, True), (zeros,) * 3, unroll=True
    )
    image_at(depth, (zeros,) * 3, False)

    def second_product(chunk, dot_yy):
        lower = load_spread(fields_y, 0, chunk)
        for place in range(depth):
            upper = load_spread(fields_y, place + 1, chunk)
            weight = elastic[place + 2, pl.ds(chunk * 8, 8)]
            dot_yy = dot_yy + weight * modal_energy(element_modes(lower, upper))
            lower = upper
        return dot_yy

    dot_yy = lax.fori_loop(0, rows // 8, second_product, zeros, unroll=True)
    lane_at = lax.broadcasted_iota(jnp.int32, (1, cols), 1)
    packed = jnp.zeros((1, cols), jnp.float32)
    for at, part in enumerate((dot_load, dot_zz, dot_zy, dot_yy)):
        packed = jnp.where(lane_at == at, jnp.sum(part, keepdims=True), packed)
    dots_ref[...] = jnp.broadcast_to(packed, dots_ref.shape)


def energy_kernel(z_ref, y_ref, growth_ref, density_ref, quad_ref, fields, fields_y):
    depth, rows, cols = density_ref.shape
    last_col = lax.broadcasted_iota(jnp.int32, (rows, cols), 1) == cols - 1
    zero_rows = jnp.zeros((8, cols), jnp.float32)

    def spread(place, carry):
        for source, first, target in ((z_ref, 1, fields), (y_ref, 0, fields_y)):
            for comp in range(3):
                store_along_y(target, place, comp, source[comp, place + first], last_col)
            for at in range(6):
                target[place, at, rows : rows + 8] = zero_rows
        return carry

    lax.fori_loop(0, depth + 1, spread, 0)

    def products(chunk, carry):
        span = pl.ds(chunk * 8, 8)
        lower, lower_y = load_spread(fields, 0, chunk), load_spread(fields_y, 0, chunk)
        for place in range(depth):
            upper, upper_y = load_spread(fields, place + 1, chunk), load_spread(fields_y, place + 1, chunk)
            hat, hat_y = element_modes(lower, upper), element_modes(lower_y, upper_y)
            dense = density_ref[place, span]
            weight = (-3.0 / 8.0 * UNIT) * dense * dense * growth_ref[place + 2, span]
            forces = modal_forces(hat, weight)
            quad_ref[0, place, span] = modal_product(hat, forces)
            quad_ref[1, place, span] = 2.0 * modal_product(hat_y, forces)
            quad_ref[2, place, span] = weight * modal_energy(hat_y)
            lower, lower_y = upper, upper_y
        return carry

    lax.fori_loop(0, rows // 8, products, 0)


def solve(dots_ref):
    dots = jnp.sum(dots_ref[...], axis=0, keepdims=True)
    lane_at = lax.broadcasted_iota(jnp.int32, dots.shape, 1)
    dot_load, dot_zz, dot_zy, dot_yy = (
        jnp.sum(jnp.where(lane_at == at, dots, 0.0), axis=1, keepdims=True) for at in range(4)
    )
    first = dot_zz / dot_load
    second = dot_zy / dot_load
    third = dot_yy / dot_load
    under = third * first - second * second
    along_z = (third - first * second) / under
    along_y = (first * first - second) / under
    return dot_load * (along_z + along_y * first), along_z, along_y


def terms_kernel(dots_ref, quad_ref, terms_ref):
    _, along_z, along_y = solve(dots_ref)
    squares = (along_z * along_z, along_z * along_y, along_y * along_y)
    samples, depth, share = terms_ref.shape[:3]
    for sample in range(samples):
        span = pl.ds(sample * share, share)
        for place in range(depth):
            terms_ref[sample, place] = sum(squares[at] * quad_ref[at, place, span] for at in range(3))


def last_kernel(
    terms_ref, dots_ref, z_ref, y_ref, displacement_ref, gradient_ref, compliance_ref
):
    compliance, along_z, along_y = solve(dots_ref)
    compliance_ref[...] = compliance
    gradient_ref[...] = jnp.sum(terms_ref[...], axis=0)
    for comp in range(3):
        for place in range(displacement_ref.shape[2]):
            displacement_ref[0, comp, place] = along_z * z_ref[comp, place + 1] + along_y * y_ref[comp, place]


def call(kernel, outs, inputs, scratch=(), in_memory=pltpu.VMEM, out_specs=None):
    return pl.pallas_call(
        kernel,
        out_shape=outs,
        in_specs=[pl.BlockSpec(memory_space=in_memory)] * inputs,
        out_specs=out_specs if out_specs is not None else [vmem_spec()] * len(outs),
        scratch_shapes=scratch,
        compiler_params=pltpu.CompilerParams(vmem_limit_bytes=VMEM_LIMIT),
    )


def per_device(load_field, density, mode_panels, mode_weight, mode_germs):
    depth, rows, cols = density.shape
    slabs = lax.axis_size("space")
    samples = lax.axis_size("sample")
    own_modes, _, cells = mode_panels.shape
    spread_y, spread_zx = weight_tables(depth, rows, cols)

    held_density, held_load = f32(depth, rows, cols), f32(3, depth, rows, cols)
    partial, density, load_field = call(
        first_kernel,
        [f32(samples, cells // 128, 128), held_density, held_load],
        inputs=5,
        scratch=[
            pltpu.VMEM((1, mode_weight.shape[0]), jnp.float32),
            pltpu.VMEM(mode_germs.shape, jnp.float32),
            pltpu.VMEM((own_modes, cells), jnp.bfloat16),
            pltpu.SemaphoreType.DMA((5,)),
        ],
        in_memory=pltpu.HBM,
    )(
        *(
            pltpu.with_memory_space_constraint(value, pltpu.HBM)
            for value in (
                mode_weight.reshape(1, -1),
                mode_germs,
                mode_panels.reshape(own_modes, cells),
                density,
                load_field,
            )
        )
    )
    parts = lax.all_to_all(partial, "sample", 0, 0, tiled=True)

    sums, up, down = call(
        pack_kernel,
        [f32(cells // 128, 128), f32(5 * rows + 8, cols), f32(8 * rows + 8, cols)],
        inputs=3,
    )(parts, density, load_field)
    below = lax.ppermute(up, "space", [(at, at + 1) for at in range(slabs - 1)])
    above = lax.ppermute(down, "space", [(at + 1, at) for at in range(slabs - 1)])

    padded = pltpu.VMEM((depth + 1, 6, rows + 8, cols), jnp.float32)
    planes = pltpu.VMEM((depth + 4, rows, cols), jnp.float32)
    z_vec, y_vec, growth, dots = call(
        middle_kernel,
        [
            f32(3, depth + 3, rows, cols),
            f32(3, depth + 1, rows, cols),
            f32(depth + 4, rows, cols),
            f32(slabs, cols),
        ],
        inputs=7,
        scratch=[
            planes,
            planes,
            pltpu.VMEM((depth + 3, rows, cols), jnp.float32),
            pltpu.VMEM((depth + 3, 6, rows + 8, cols), jnp.float32),
            padded,
            pltpu.VMEM((depth + 1, 6, rows, cols), jnp.float32),
            padded,
        ],
    )(sums, density, load_field, below, above, spread_y, spread_zx)
    dots = lax.all_to_all(dots, "space", 0, 0, tiled=True)
    (quads,) = call(energy_kernel, [f32(3, depth, rows, cols)], inputs=4, scratch=[padded, padded])(
        z_vec, y_vec, growth, density
    )
    (terms,) = call(terms_kernel, [f32(samples, depth, rows // samples, cols)], inputs=2)(dots, quads)
    terms = lax.all_to_all(terms, "sample", 0, 0, tiled=True)
    displacement, gradient, compliance = call(
        last_kernel,
        [f32(1, 3, depth, rows, cols), f32(depth, rows // samples, cols), f32(1, 1)],
        inputs=4,
    )(terms, dots, z_vec, y_vec)
    return displacement, gradient, compliance.reshape(1)


def solution(mesh):
    placed = (
        P(None, "space", None, None),
        P("space", None, None),
        P("sample", "space", None),
        P(),
        P(),
    )
    return jax.shard_map(
        per_device,
        mesh=mesh,
        in_specs=placed,
        out_specs=(P("sample", None, "space", None, None), P("space", "sample", None), P("sample")),
        check_vma=False,
    )
```

```python
import itertools

import jax
import jax.numpy as jnp
import numpy as np
from jax import lax
from jax.experimental import pallas as pl
from jax.experimental.pallas import tpu as pltpu
from jax.sharding import PartitionSpec as P

POISSON = 0.3
LAME = POISSON / ((1.0 + POISSON) * (1.0 - 2.0 * POISSON))
SHEAR = 1.0 / (2.0 * (1.0 + POISSON))
DIAGONAL = (LAME + 2.0 * SHEAR) / 9.0 + 2.0 * SHEAR / 9.0
RATIO = LAME / SHEAR
UNIT = SHEAR / 16.0
VMEM_LIMIT = 48 * 1024 * 1024


def vmem_spec():
    return pl.BlockSpec(memory_space=pltpu.VMEM)


def f32(*shape):
    return jax.ShapeDtypeStruct(shape, jnp.float32)


def split3(value):
    high = value.astype(jnp.bfloat16)
    rest = value - high.astype(jnp.float32)
    mid = rest.astype(jnp.bfloat16)
    low = (rest - mid.astype(jnp.float32)).astype(jnp.bfloat16)
    return high, mid, low


def dot32(left, right):
    return jnp.dot(left, right, preferred_element_type=jnp.float32)


def weight_tables(depth, rows, cols):
    def hat(positions, cells):
        return np.maximum(0.0, 1.0 - np.abs(positions[:, None] - cells[None, :]))

    along_x = hat((np.arange(rows) + 0.5) / 4.0 - 0.5, np.arange(rows // 4))
    along_y = hat((np.arange(cols) + 0.5) / 4.0 - 0.5, np.arange(cols // 4))
    along_z = hat((np.arange(depth + 4) - 2 + 0.5) / 4.0 - 0.5, np.arange(-1, 2))
    spread_y = np.tile(along_y.T, (4, 1))
    spread_zx = np.einsum("pc,xd->pxcd", along_z, along_x).reshape((depth + 4) * rows, -1)
    return spread_y.astype(jnp.bfloat16), spread_zx.astype(jnp.bfloat16)


def first_kernel(
    weight_hbm, germs_hbm, panels_hbm, density_hbm, load_hbm,
    partial_ref, density_ref, load_ref,
    weight, germs, panels, sems,
):
    sample = lax.axis_index("sample")
    copies = [
        pltpu.make_async_copy(source, target, sems.at[at])
        for at, (source, target) in enumerate(
            (
                (weight_hbm, weight),
                (germs_hbm, germs),
                (panels_hbm, panels),
                (density_hbm, density_ref),
                (load_hbm, load_ref),
            )
        )
    ]
    for copy in copies:
        copy.start()
    own_modes = panels.shape[0]
    modes = germs.shape[1]
    mode_at = lax.broadcasted_iota(jnp.int32, (modes, own_modes), 0)
    slot_at = lax.broadcasted_iota(jnp.int32, (modes, own_modes), 1)
    pick = jnp.where(mode_at == slot_at + sample * own_modes, 1.0, 0.0).astype(jnp.bfloat16)
    for copy in copies[:3]:
        copy.wait()
    coefficients = (weight[...] * germs[...]).astype(jnp.bfloat16)
    own_coeff = dot32(coefficients, pick).astype(jnp.bfloat16)
    partial = dot32(own_coeff, panels[...])
    lines = partial_ref.shape[1] // 2
    for target in range(partial_ref.shape[0]):
        for at in range(2 * lines):
            row, line = target // 2 * 2 + at // lines, at % lines
            partial_ref[target, at : at + 1] = partial[row : row + 1, line * 128 : (line + 1) * 128]
    for copy in copies[3:]:
        copy.wait()


def towards_above():
    core, slab = lax.axis_index("sample") % 2, lax.axis_index("space")
    return core == slab % 2


def pack_kernel(parts_ref, density_ref, load_ref, sums_ref, message_ref):
    rows = density_ref.shape[1]
    depth = density_ref.shape[0]
    sums = jnp.sum(parts_ref[...], axis=0)
    sums_ref[...] = sums
    message_ref[message_ref.shape[0] - sums.shape[0] :] = sums

    def fill(parts):
        for at in range(8):
            part = parts[at] if at < len(parts) else jnp.zeros_like(parts[0])
            message_ref[at * rows : (at + 1) * rows] = part

    @pl.when(towards_above())
    def _():
        up = [density_ref[depth - 2], density_ref[depth - 1]]
        fill(up + [load_ref[comp, depth - 1] for comp in range(3)])

    @pl.when(jnp.logical_not(towards_above()))
    def _():
        down = [density_ref[0], density_ref[1]]
        fill(down + [load_ref[comp, place] for comp in range(3) for place in range(2)])


def shift_ahead(value, axis, mask):
    return jnp.where(mask, 0.0, pltpu.roll(value, value.shape[axis] - 1, axis))


def shift_back(value, axis, mask):
    return jnp.where(mask, 0.0, pltpu.roll(value, 1, axis))


def store_along_y(target, place, comp, value, last_col):
    ahead = shift_ahead(value, 1, last_col)
    target[place, 2 * comp, 0 : value.shape[0]] = value + ahead
    target[place, 2 * comp + 1, 0 : value.shape[0]] = ahead - value


def load_spread(source, place, chunk):
    parts = []
    for comp in range(3):
        here = [source[place, 2 * comp + mode, pl.ds(chunk * 8, 8)] for mode in range(2)]
        ahead = [source[place, 2 * comp + mode, pl.ds(chunk * 8 + 1, 8)] for mode in range(2)]
        parts += [one + two for one, two in zip(here, ahead)]
        parts += [two - one for one, two in zip(here, ahead)]
    return parts


def element_modes(lower, upper):
    hat = {}
    for comp in range(3):
        for mode_x, mode_y in itertools.product((0, 1), repeat=2):
            at = 4 * comp + 2 * mode_x + mode_y
            if mode_x or mode_y:
                hat[comp, (0, mode_x, mode_y)] = lower[at] + upper[at]
            hat[comp, (1, mode_x, mode_y)] = upper[at] - lower[at]
    return hat


def mode(*axes):
    return tuple(int(axis in axes) for axis in range(3))


def modal_parts(hat):
    shear = {
        (one, two): hat[one, mode(two)] + hat[two, mode(one)] for one, two in ((0, 1), (0, 2), (1, 2))
    }
    trace = hat[0, mode(0)] + hat[1, mode(1)] + hat[2, mode(2)]
    twist = [hat[axis, mode(*(other for other in range(3) if other != axis))] for axis in range(3)]
    bends = {}
    for across in range(3):
        one, two = (axis for axis in range(3) if axis != across)
        bends[across] = (one, two, hat[one, mode(one, across)] + hat[two, mode(two, across)])
    return shear, trace, twist, bends


def modal_forces(hat, weight):
    shear, trace, twist, bends = modal_parts(hat)
    forces = {}
    for (one, two), value in shear.items():
        forces[one, mode(two)] = forces[two, mode(one)] = value * weight
    level = RATIO * trace
    for axis in range(3):
        forces[axis, mode(axis)] = (2.0 * hat[axis, mode(axis)] + level) * weight
    third = (1.0 / 3.0) * weight
    both = twist[0] + twist[1] + twist[2]
    for axis in range(3):
        place = mode(*(other for other in range(3) if other != axis))
        forces[axis, place] = (twist[axis] + both) * third
    for across, (one, two, total) in bends.items():
        extra = (RATIO / 3.0) * total
        for axis in (one, two):
            place = mode(axis, across)
            forces[axis, place] = (hat[axis, place] + extra) * weight
    last = ((RATIO + 4.0) / 9.0) * weight
    for axis in range(3):
        forces[axis, (1, 1, 1)] = hat[axis, (1, 1, 1)] * last
    return forces


def total_of(values):
    values = list(values)
    while len(values) > 1:
        paired = [one + two for one, two in zip(values[::2], values[1::2])]
        values = paired + ([values[-1]] if len(values) % 2 else [])
    return values[0]


def modal_product(left, right):
    return total_of(left[key] * value for key, value in right.items())


def modal_energy(hat):
    shear, trace, twist, bends = modal_parts(hat)

    def squares(values):
        return total_of(value * value for value in values)

    both = twist[0] + twist[1] + twist[2]
    whole = list(shear.values())
    for across, (one, two, _) in bends.items():
        whole += [hat[one, mode(one, across)], hat[two, mode(two, across)]]
    return total_of(
        [
            squares(whole),
            2.0 * squares(hat[axis, mode(axis)] for axis in range(3)),
            RATIO * (trace * trace),
            (1.0 / 3.0) * squares(twist + [both]),
            (RATIO / 3.0) * squares(total for _, _, total in bends.values()),
            ((RATIO + 4.0) / 9.0) * squares(hat[axis, (1, 1, 1)] for axis in range(3)),
        ]
    )


def fold(plane):
    return jnp.sum(plane.reshape(-1, 8, plane.shape[-1]), axis=0)


def middle_kernel(
    sums_ref, density_ref, load_ref, own_ref, other_ref, spread_y_ref, spread_zx_ref,
    z_ref, y_ref, growth_ref, dots_ref,
    elastic, around, inverse, fields, fields_y, near_at, far_at,
):
    slab = lax.axis_index("space")
    slabs = lax.axis_size("space")
    depth, rows, cols = density_ref.shape
    row_at = lax.broadcasted_iota(jnp.int32, (rows, cols), 0)
    col_at = lax.broadcasted_iota(jnp.int32, (rows, cols), 1)
    first_row = row_at == 0
    first_col, last_col = col_at == 0, col_at == cols - 1
    cells = sums_ref.shape[0] // 2
    core = lax.axis_index("sample") % 2
    extra = own_ref.shape[0] - 2 * cells
    own_above = towards_above()

    def from_below(span):
        return jnp.where(own_above, other_ref[span], own_ref[span])

    def from_above(span):
        return jnp.where(own_above, own_ref[span], other_ref[span])

    def own_sample(lines):
        return jnp.where(core == 0, lines[0:cells], lines[cells:])

    def plane(place):
        return pl.ds(place * rows, rows)

    coarse_x, coarse_y = rows // 4, cols // 4
    fold_x = coarse_x // cells
    line_at = lax.broadcasted_iota(jnp.int32, (coarse_x, cols), 0)
    cell_at = lax.broadcasted_iota(jnp.int32, (coarse_x, cols), 1)
    on_line = cell_at // coarse_y == line_at % fold_x
    lines = []
    last = pl.ds(extra, 2 * cells)
    for both in (from_below(last), sums_ref[...], from_above(last)):
        coarse = own_sample(both)
        tall = jnp.zeros((coarse_x, cols), jnp.float32)
        for at in range(cells):
            tall = jnp.where(line_at // fold_x == at, coarse[at : at + 1], tall)
        lines.append(jnp.where(on_line, tall, 0.0))
    lines = jnp.concatenate(lines, axis=0)
    spread_y = spread_y_ref[...]
    high, mid, low = (dot32(part, spread_y) for part in split3(lines))
    along_y = high + (mid + low)
    spread_zx = spread_zx_ref[...]
    high, mid, low = (dot32(spread_zx, part) for part in split3(along_y))
    growth_ref[...] = jnp.exp(high + (mid + low)).reshape(depth + 4, rows, cols)

    def dense_at(place):
        if place < 2:
            return from_below(plane(place))
        return density_ref[place - 2] if place < depth + 2 else from_above(plane(place - depth - 2))

    def load_at(comp, place):
        if place < 2:
            return from_below(plane(2 + comp))
        if place < depth + 2:
            return load_ref[comp, place - 2]
        return from_above(plane(2 + 2 * comp + place - depth - 2))

    zero_rows = jnp.zeros((8, cols), jnp.float32)
    for target, first in ((fields, rows), (fields_y, rows), (far_at, 0)):
        for place, at in itertools.product(range(target.shape[0]), range(6)):
            target[place, at, first : first + 8] = zero_rows

    for place in range(depth + 4):
        dense = dense_at(place)
        modulus = growth_ref[place] * (0.001 + dense * dense * dense)
        if place < 2:
            modulus = modulus * jnp.where(slab == 0, 0.0, UNIT)
        elif place >= depth + 2:
            modulus = modulus * jnp.where(slab == slabs - 1, 0.0, UNIT)
        else:
            modulus = modulus * UNIT
        elastic[place] = modulus
        along = modulus + shift_back(modulus, 1, first_col)
        around[place] = along + shift_back(along, 0, first_row)

    for place in range(1, depth + 4):
        diagonal = (DIAGONAL / UNIT) * (around[place - 1] + around[place])
        if place == 1:
            diagonal = jnp.where(slab == 0, 1.0, diagonal)
        if place == depth + 3:
            diagonal = jnp.where(slab == slabs - 1, 1.0, diagonal)
        inverse_here = 1.0 / diagonal
        inverse[place - 1] = inverse_here
        for comp in range(3):
            value = load_at(comp, place) * inverse_here
            z_ref[comp, place - 1] = value
            store_along_y(fields, place - 1, comp, value, last_col)

    def first_product(chunk, carry):
        lower = load_spread(fields, 0, chunk)
        carried = None
        for place in range(1, depth + 3):
            upper = load_spread(fields, place, chunk)
            forces = modal_forces(element_modes(lower, upper), elastic[place, pl.ds(chunk * 8, 8)])
            passed = []
            for comp in range(3):
                sums = []
                for mode_x, mode_y in itertools.product((0, 1), repeat=2):
                    rise = forces[comp, (1, mode_x, mode_y)]
                    if mode_x or mode_y:
                        level = forces[comp, (0, mode_x, mode_y)]
                        near, far = level - rise, level + rise
                    else:
                        near, far = -rise, rise
                    if carried is not None:
                        sums.append(near + carried[4 * comp + 2 * mode_x + mode_y])
                    passed.append(far)
                if carried is not None:
                    for mode_y in range(2):
                        level, rise = sums[mode_y], sums[2 + mode_y]
                        near_at[place - 2, 2 * comp + mode_y, pl.ds(chunk * 8, 8)] = level - rise
                        far_at[place - 2, 2 * comp + mode_y, pl.ds(chunk * 8 + 8, 8)] = level + rise
            carried = passed
            lower = upper
        return carry

    lax.fori_loop(0, rows // 8, first_product, 0, unroll=2)

    def image_at(place, dots, own):
        dot_load, dot_zz, dot_zy = dots
        scale = inverse[place + 1]
        if not own:
            scale = jnp.where(slab < slabs - 1, scale, 0.0)
        for comp in range(3):
            along = [
                near_at[place, 2 * comp + mode_y] + far_at[place, 2 * comp + mode_y, 7 : rows + 7]
                for mode_y in range(2)
            ]
            image = (along[0] - along[1]) + shift_back(along[0] + along[1], 1, first_col)
            scaled = image * scale
            y_ref[comp, place] = scaled
            if own:
                value = z_ref[comp, place + 1]
                dot_load = dot_load + fold(load_ref[comp, place] * value)
                dot_zz = dot_zz + fold(value * image)
                dot_zy = dot_zy + fold(scaled * image)
            store_along_y(fields_y, place, comp, scaled, last_col)
        return dot_load, dot_zz, dot_zy

    zeros = jnp.zeros((8, cols), jnp.float32)
    dot_load, dot_zz, dot_zy = lax.fori_loop(
        0, depth, lambda place, dots: image_at(place, dots, True), (zeros,) * 3, unroll=True
    )
    image_at(depth, (zeros,) * 3, False)

    def second_product(chunk, dot_yy):
        lower = load_spread(fields_y, 0, chunk)
        for place in range(depth):
            upper = load_spread(fields_y, place + 1, chunk)
            weight = elastic[place + 2, pl.ds(chunk * 8, 8)]
            dot_yy = dot_yy + weight * modal_energy(element_modes(lower, upper))
            lower = upper
        return dot_yy

    dot_yy = lax.fori_loop(0, rows // 8, second_product, zeros, unroll=True)
    lane_at = lax.broadcasted_iota(jnp.int32, (1, cols), 1)
    packed = jnp.zeros((1, cols), jnp.float32)
    for at, part in enumerate((dot_load, dot_zz, dot_zy, dot_yy)):
        packed = jnp.where(lane_at == at, jnp.sum(part, keepdims=True), packed)
    dots_ref[...] = jnp.broadcast_to(packed, dots_ref.shape)


def energy_kernel(z_ref, y_ref, growth_ref, density_ref, quad_ref, fields, fields_y):
    depth, rows, cols = density_ref.shape
    last_col = lax.broadcasted_iota(jnp.int32, (rows, cols), 1) == cols - 1
    zero_rows = jnp.zeros((8, cols), jnp.float32)

    def spread(place, carry):
        for source, first, target in ((z_ref, 1, fields), (y_ref, 0, fields_y)):
            for comp in range(3):
                store_along_y(target, place, comp, source[comp, place + first], last_col)
            for at in range(6):
                target[place, at, rows : rows + 8] = zero_rows
        return carry

    lax.fori_loop(0, depth + 1, spread, 0)

    def products(chunk, carry):
        span = pl.ds(chunk * 8, 8)
        lower, lower_y = load_spread(fields, 0, chunk), load_spread(fields_y, 0, chunk)
        for place in range(depth):
            upper, upper_y = load_spread(fields, place + 1, chunk), load_spread(fields_y, place + 1, chunk)
            hat, hat_y = element_modes(lower, upper), element_modes(lower_y, upper_y)
            dense = density_ref[place, span]
            weight = (-3.0 / 8.0 * UNIT) * dense * dense * growth_ref[place + 2, span]
            forces = modal_forces(hat, weight)
            quad_ref[0, place, span] = modal_product(hat, forces)
            quad_ref[1, place, span] = 2.0 * modal_product(hat_y, forces)
            quad_ref[2, place, span] = weight * modal_energy(hat_y)
            lower, lower_y = upper, upper_y
        return carry

    lax.fori_loop(0, rows // 8, products, 0)


def solve(dots_ref):
    dots = jnp.sum(dots_ref[...], axis=0, keepdims=True)
    lane_at = lax.broadcasted_iota(jnp.int32, dots.shape, 1)
    dot_load, dot_zz, dot_zy, dot_yy = (
        jnp.sum(jnp.where(lane_at == at, dots, 0.0), axis=1, keepdims=True) for at in range(4)
    )
    first = dot_zz / dot_load
    second = dot_zy / dot_load
    third = dot_yy / dot_load
    under = third * first - second * second
    along_z = (third - first * second) / under
    along_y = (first * first - second) / under
    return dot_load * (along_z + along_y * first), along_z, along_y


def terms_kernel(dots_ref, quad_ref, terms_ref):
    _, along_z, along_y = solve(dots_ref)
    squares = (along_z * along_z, along_z * along_y, along_y * along_y)
    samples, depth, share = terms_ref.shape[:3]
    for sample in range(samples):
        span = pl.ds(sample * share, share)
        for place in range(depth):
            terms_ref[sample, place] = sum(squares[at] * quad_ref[at, place, span] for at in range(3))


def last_kernel(
    terms_ref, dots_ref, z_ref, y_ref, displacement_ref, gradient_ref, compliance_ref
):
    compliance, along_z, along_y = solve(dots_ref)
    compliance_ref[...] = compliance
    gradient_ref[...] = jnp.sum(terms_ref[...], axis=0)
    for comp in range(3):
        for place in range(displacement_ref.shape[2]):
            displacement_ref[0, comp, place] = along_z * z_ref[comp, place + 1] + along_y * y_ref[comp, place]


def call(kernel, outs, inputs, scratch=(), in_memory=pltpu.VMEM, out_specs=None):
    return pl.pallas_call(
        kernel,
        out_shape=outs,
        in_specs=[pl.BlockSpec(memory_space=in_memory)] * inputs,
        out_specs=out_specs if out_specs is not None else [vmem_spec()] * len(outs),
        scratch_shapes=scratch,
        compiler_params=pltpu.CompilerParams(vmem_limit_bytes=VMEM_LIMIT),
    )


def per_device(load_field, density, mode_panels, mode_weight, mode_germs):
    depth, rows, cols = density.shape
    slabs = lax.axis_size("space")
    samples = lax.axis_size("sample")
    own_modes, _, cells = mode_panels.shape
    spread_y, spread_zx = weight_tables(depth, rows, cols)

    held_density, held_load = f32(depth, rows, cols), f32(3, depth, rows, cols)
    partial, density, load_field = call(
        first_kernel,
        [f32(samples, 2 * cells // 128, 128), held_density, held_load],
        inputs=5,
        scratch=[
            pltpu.VMEM((1, mode_weight.shape[0]), jnp.float32),
            pltpu.VMEM(mode_germs.shape, jnp.float32),
            pltpu.VMEM((own_modes, cells), jnp.bfloat16),
            pltpu.SemaphoreType.DMA((5,)),
        ],
        in_memory=pltpu.HBM,
    )(
        *(
            pltpu.with_memory_space_constraint(value, pltpu.HBM)
            for value in (
                mode_weight.reshape(1, -1),
                mode_germs,
                mode_panels.reshape(own_modes, cells),
                density,
                load_field,
            )
        )
    )
    parts = lax.all_to_all(partial, "sample", 0, 0, tiled=True)

    lines = 2 * cells // 128
    sums, message = call(pack_kernel, [f32(lines, 128), f32(8 * rows + lines, cols)], inputs=3)(
        parts, density, load_field
    )
    pairs = []
    for sample in range(samples):
        for slab in range(slabs):
            target = slab + (1 if sample % 2 == slab % 2 else -1)
            if 0 <= target < slabs:
                pairs.append((sample * slabs + slab, sample * slabs + target))
    own = lax.ppermute(message, ("sample", "space"), pairs)
    other = lax.ppermute(own, "sample", [(at, at ^ 1) for at in range(samples)])

    padded = pltpu.VMEM((depth + 1, 6, rows + 8, cols), jnp.float32)
    planes = pltpu.VMEM((depth + 4, rows, cols), jnp.float32)
    z_vec, y_vec, growth, dots = call(
        middle_kernel,
        [
            f32(3, depth + 3, rows, cols),
            f32(3, depth + 1, rows, cols),
            f32(depth + 4, rows, cols),
            f32(slabs, cols),
        ],
        inputs=7,
        scratch=[
            planes,
            planes,
            pltpu.VMEM((depth + 3, rows, cols), jnp.float32),
            pltpu.VMEM((depth + 3, 6, rows + 8, cols), jnp.float32),
            padded,
            pltpu.VMEM((depth + 1, 6, rows, cols), jnp.float32),
            padded,
        ],
    )(sums, density, load_field, own, other, spread_y, spread_zx)
    dots = lax.all_to_all(dots, "space", 0, 0, tiled=True)
    (quads,) = call(energy_kernel, [f32(3, depth, rows, cols)], inputs=4, scratch=[padded, padded])(
        z_vec, y_vec, growth, density
    )
    (terms,) = call(terms_kernel, [f32(samples, depth, rows // samples, cols)], inputs=2)(dots, quads)
    terms = lax.all_to_all(terms, "sample", 0, 0, tiled=True)
    displacement, gradient, compliance = call(
        last_kernel,
        [f32(1, 3, depth, rows, cols), f32(depth, rows // samples, cols), f32(1, 1)],
        inputs=4,
    )(terms, dots, z_vec, y_vec)
    return displacement, gradient, compliance.reshape(1)


def solution(mesh):
    placed = (
        P(None, "space", None, None),
        P("space", None, None),
        P("sample", "space", None),
        P(),
        P(),
    )
    return jax.shard_map(
        per_device,
        mesh=mesh,
        in_specs=placed,
        out_specs=(P("sample", None, "space", None, None), P("space", "sample", None), P("sample")),
        check_vma=False,
    )
```

```python
import itertools

import jax
import jax.numpy as jnp
import numpy as np
from jax import lax
from jax.experimental import pallas as pl
from jax.experimental.pallas import tpu as pltpu
from jax.sharding import PartitionSpec as P

POISSON = 0.3
LAME = POISSON / ((1.0 + POISSON) * (1.0 - 2.0 * POISSON))
SHEAR = 1.0 / (2.0 * (1.0 + POISSON))
DIAGONAL = (LAME + 2.0 * SHEAR) / 9.0 + 2.0 * SHEAR / 9.0
RATIO = LAME / SHEAR
UNIT = SHEAR / 16.0
VMEM_LIMIT = 48 * 1024 * 1024


def vmem_spec():
    return pl.BlockSpec(memory_space=pltpu.VMEM)


def f32(*shape):
    return jax.ShapeDtypeStruct(shape, jnp.float32)


def split3(value):
    high = value.astype(jnp.bfloat16)
    rest = value - high.astype(jnp.float32)
    mid = rest.astype(jnp.bfloat16)
    low = (rest - mid.astype(jnp.float32)).astype(jnp.bfloat16)
    return high, mid, low


def dot32(left, right):
    return jnp.dot(left, right, preferred_element_type=jnp.float32)


def weight_tables(depth, rows, cols):
    def hat(positions, cells):
        return np.maximum(0.0, 1.0 - np.abs(positions[:, None] - cells[None, :]))

    along_x = hat((np.arange(rows) + 0.5) / 4.0 - 0.5, np.arange(rows // 4))
    along_y = hat((np.arange(cols) + 0.5) / 4.0 - 0.5, np.arange(cols // 4))
    along_z = hat((np.arange(depth + 4) - 2 + 0.5) / 4.0 - 0.5, np.arange(-1, 2))
    spread_y = np.tile(along_y.T, (4, 1))
    spread_zx = np.einsum("pc,xd->pxcd", along_z, along_x).reshape((depth + 4) * rows, -1)
    return spread_y.astype(jnp.bfloat16), spread_zx.astype(jnp.bfloat16)


def first_kernel(
    weight_hbm, germs_hbm, panels_hbm, density_hbm, load_hbm,
    partial_ref, density_ref, load_ref,
    weight, germs, panels, sems,
):
    sample = lax.axis_index("sample")
    copies = [
        pltpu.make_async_copy(source, target, sems.at[at])
        for at, (source, target) in enumerate(
            (
                (weight_hbm, weight),
                (germs_hbm, germs),
                (panels_hbm, panels),
                (density_hbm, density_ref),
                (load_hbm, load_ref),
            )
        )
    ]
    for copy in copies:
        copy.start()
    own_modes = panels.shape[0]
    modes = germs.shape[1]
    mode_at = lax.broadcasted_iota(jnp.int32, (modes, own_modes), 0)
    slot_at = lax.broadcasted_iota(jnp.int32, (modes, own_modes), 1)
    pick = jnp.where(mode_at == slot_at + sample * own_modes, 1.0, 0.0).astype(jnp.bfloat16)
    for copy in copies[:3]:
        copy.wait()
    coefficients = (weight[...] * germs[...]).astype(jnp.bfloat16)
    own_coeff = dot32(coefficients, pick).astype(jnp.bfloat16)
    partial = dot32(own_coeff, panels[...])
    lines = partial_ref.shape[1] // 2
    for target in range(partial_ref.shape[0]):
        for at in range(2 * lines):
            row, line = target // 2 * 2 + at // lines, at % lines
            partial_ref[target, at : at + 1] = partial[row : row + 1, line * 128 : (line + 1) * 128]
    for copy in copies[3:]:
        copy.wait()


def towards_above():
    core, slab = lax.axis_index("sample") % 2, lax.axis_index("space")
    return core == slab % 2


def pack_kernel(parts_ref, density_ref, load_ref, sums_ref, message_ref):
    rows = density_ref.shape[1]
    depth = density_ref.shape[0]
    sums = jnp.sum(parts_ref[...], axis=0)
    sums_ref[...] = sums
    message_ref[message_ref.shape[0] - sums.shape[0] :] = sums

    def fill(parts):
        for at in range(8):
            part = parts[at] if at < len(parts) else jnp.zeros_like(parts[0])
            message_ref[at * rows : (at + 1) * rows] = part

    @pl.when(towards_above())
    def _():
        up = [density_ref[depth - 2], density_ref[depth - 1]]
        fill(up + [load_ref[comp, depth - 1] for comp in range(3)])

    @pl.when(jnp.logical_not(towards_above()))
    def _():
        down = [density_ref[0], density_ref[1]]
        fill(down + [load_ref[comp, place] for comp in range(3) for place in range(2)])


def shift_ahead(value, axis, mask):
    return jnp.where(mask, 0.0, pltpu.roll(value, value.shape[axis] - 1, axis))


def shift_back(value, axis, mask):
    return jnp.where(mask, 0.0, pltpu.roll(value, 1, axis))


def store_along_y(target, place, comp, value, last_col):
    ahead = shift_ahead(value, 1, last_col)
    target[place, 2 * comp, 0 : value.shape[0]] = value + ahead
    target[place, 2 * comp + 1, 0 : value.shape[0]] = ahead - value


def load_spread(source, place, chunk):
    parts = []
    for comp in range(3):
        here = [source[place, 2 * comp + mode, pl.ds(chunk * 8, 8)] for mode in range(2)]
        ahead = [source[place, 2 * comp + mode, pl.ds(chunk * 8 + 1, 8)] for mode in range(2)]
        parts += [one + two for one, two in zip(here, ahead)]
        parts += [two - one for one, two in zip(here, ahead)]
    return parts


def element_modes(lower, upper):
    hat = {}
    for comp in range(3):
        for mode_x, mode_y in itertools.product((0, 1), repeat=2):
            at = 4 * comp + 2 * mode_x + mode_y
            if mode_x or mode_y:
                hat[comp, (0, mode_x, mode_y)] = lower[at] + upper[at]
            hat[comp, (1, mode_x, mode_y)] = upper[at] - lower[at]
    return hat


def mode(*axes):
    return tuple(int(axis in axes) for axis in range(3))


def modal_parts(hat):
    shear = {
        (one, two): hat[one, mode(two)] + hat[two, mode(one)] for one, two in ((0, 1), (0, 2), (1, 2))
    }
    trace = hat[0, mode(0)] + hat[1, mode(1)] + hat[2, mode(2)]
    twist = [hat[axis, mode(*(other for other in range(3) if other != axis))] for axis in range(3)]
    bends = {}
    for across in range(3):
        one, two = (axis for axis in range(3) if axis != across)
        bends[across] = (one, two, hat[one, mode(one, across)] + hat[two, mode(two, across)])
    return shear, trace, twist, bends


def modal_forces(hat, weight):
    shear, trace, twist, bends = modal_parts(hat)
    forces = {}
    for (one, two), value in shear.items():
        forces[one, mode(two)] = forces[two, mode(one)] = value * weight
    level = RATIO * trace
    for axis in range(3):
        forces[axis, mode(axis)] = (2.0 * hat[axis, mode(axis)] + level) * weight
    third = (1.0 / 3.0) * weight
    both = twist[0] + twist[1] + twist[2]
    for axis in range(3):
        place = mode(*(other for other in range(3) if other != axis))
        forces[axis, place] = (twist[axis] + both) * third
    for across, (one, two, total) in bends.items():
        extra = (RATIO / 3.0) * total
        for axis in (one, two):
            place = mode(axis, across)
            forces[axis, place] = (hat[axis, place] + extra) * weight
    last = ((RATIO + 4.0) / 9.0) * weight
    for axis in range(3):
        forces[axis, (1, 1, 1)] = hat[axis, (1, 1, 1)] * last
    return forces


def total_of(values):
    values = list(values)
    while len(values) > 1:
        paired = [one + two for one, two in zip(values[::2], values[1::2])]
        values = paired + ([values[-1]] if len(values) % 2 else [])
    return values[0]


def modal_product(left, right):
    return total_of(left[key] * value for key, value in right.items())


def modal_energy(hat):
    shear, trace, twist, bends = modal_parts(hat)

    def squares(values):
        return total_of(value * value for value in values)

    both = twist[0] + twist[1] + twist[2]
    whole = list(shear.values())
    for across, (one, two, _) in bends.items():
        whole += [hat[one, mode(one, across)], hat[two, mode(two, across)]]
    return total_of(
        [
            squares(whole),
            2.0 * squares(hat[axis, mode(axis)] for axis in range(3)),
            RATIO * (trace * trace),
            (1.0 / 3.0) * squares(twist + [both]),
            (RATIO / 3.0) * squares(total for _, _, total in bends.values()),
            ((RATIO + 4.0) / 9.0) * squares(hat[axis, (1, 1, 1)] for axis in range(3)),
        ]
    )


def fold(plane):
    return jnp.sum(plane.reshape(-1, 8, plane.shape[-1]), axis=0)


def middle_kernel(
    sums_ref, density_ref, load_ref, own_ref, other_ref, spread_y_ref, spread_zx_ref,
    z_ref, y_ref, growth_ref, dots_ref,
    elastic, around, inverse, fields, fields_y, near_at, far_at,
):
    slab = lax.axis_index("space")
    slabs = lax.axis_size("space")
    depth, rows, cols = density_ref.shape
    row_at = lax.broadcasted_iota(jnp.int32, (rows, cols), 0)
    col_at = lax.broadcasted_iota(jnp.int32, (rows, cols), 1)
    first_row = row_at == 0
    first_col, last_col = col_at == 0, col_at == cols - 1
    cells = sums_ref.shape[0] // 2
    core = lax.axis_index("sample") % 2
    extra = own_ref.shape[0] - 2 * cells
    own_above = towards_above()

    def from_below(span):
        return jnp.where(own_above, other_ref[span], own_ref[span])

    def from_above(span):
        return jnp.where(own_above, own_ref[span], other_ref[span])

    def own_sample(lines):
        return jnp.where(core == 0, lines[0:cells], lines[cells:])

    def plane(place):
        return pl.ds(place * rows, rows)

    coarse_x, coarse_y = rows // 4, cols // 4
    fold_x = coarse_x // cells
    line_at = lax.broadcasted_iota(jnp.int32, (coarse_x, cols), 0)
    cell_at = lax.broadcasted_iota(jnp.int32, (coarse_x, cols), 1)
    on_line = cell_at // coarse_y == line_at % fold_x
    lines = []
    last = pl.ds(extra, 2 * cells)
    for both in (from_below(last), sums_ref[...], from_above(last)):
        coarse = own_sample(both)
        tall = jnp.zeros((coarse_x, cols), jnp.float32)
        for at in range(cells):
            tall = jnp.where(line_at // fold_x == at, coarse[at : at + 1], tall)
        lines.append(jnp.where(on_line, tall, 0.0))
    lines = jnp.concatenate(lines, axis=0)
    spread_y = spread_y_ref[...]
    high, mid, low = (dot32(part, spread_y) for part in split3(lines))
    along_y = high + (mid + low)
    spread_zx = spread_zx_ref[...]
    high, mid, low = (dot32(spread_zx, part) for part in split3(along_y))
    growth_ref[...] = jnp.exp(high + (mid + low)).reshape(depth + 4, rows, cols)

    def dense_at(place):
        if place < 2:
            return from_below(plane(place))
        return density_ref[place - 2] if place < depth + 2 else from_above(plane(place - depth - 2))

    def load_at(comp, place):
        if place < 2:
            return from_below(plane(2 + comp))
        if place < depth + 2:
            return load_ref[comp, place - 2]
        return from_above(plane(2 + 2 * comp + place - depth - 2))

    zero_rows = jnp.zeros((8, cols), jnp.float32)
    for target, first in ((fields, rows), (fields_y, rows), (far_at, 0)):
        for place, at in itertools.product(range(target.shape[0]), range(6)):
            target[place, at, first : first + 8] = zero_rows

    for place in range(depth + 4):
        dense = dense_at(place)
        modulus = growth_ref[place] * (0.001 + dense * dense * dense)
        if place < 2:
            modulus = modulus * jnp.where(slab == 0, 0.0, UNIT)
        elif place >= depth + 2:
            modulus = modulus * jnp.where(slab == slabs - 1, 0.0, UNIT)
        else:
            modulus = modulus * UNIT
        elastic[place] = modulus
        along = modulus + shift_back(modulus, 1, first_col)
        around[place] = along + shift_back(along, 0, first_row)

    for place in range(1, depth + 4):
        diagonal = (DIAGONAL / UNIT) * (around[place - 1] + around[place])
        if place == 1:
            diagonal = jnp.where(slab == 0, 1.0, diagonal)
        if place == depth + 3:
            diagonal = jnp.where(slab == slabs - 1, 1.0, diagonal)
        inverse_here = 1.0 / diagonal
        inverse[place - 1] = inverse_here
        for comp in range(3):
            value = load_at(comp, place) * inverse_here
            z_ref[comp, place - 1] = value
            store_along_y(fields, place - 1, comp, value, last_col)

    def first_product(chunk, carry):
        lower = load_spread(fields, 0, chunk)
        carried = None
        for place in range(1, depth + 3):
            upper = load_spread(fields, place, chunk)
            forces = modal_forces(element_modes(lower, upper), elastic[place, pl.ds(chunk * 8, 8)])
            passed = []
            for comp in range(3):
                sums = []
                for mode_x, mode_y in itertools.product((0, 1), repeat=2):
                    rise = forces[comp, (1, mode_x, mode_y)]
                    if mode_x or mode_y:
                        level = forces[comp, (0, mode_x, mode_y)]
                        near, far = level - rise, level + rise
                    else:
                        near, far = -rise, rise
                    if carried is not None:
                        sums.append(near + carried[4 * comp + 2 * mode_x + mode_y])
                    passed.append(far)
                if carried is not None:
                    for mode_y in range(2):
                        level, rise = sums[mode_y], sums[2 + mode_y]
                        near_at[place - 2, 2 * comp + mode_y, pl.ds(chunk * 8, 8)] = level - rise
                        far_at[place - 2, 2 * comp + mode_y, pl.ds(chunk * 8 + 8, 8)] = level + rise
            carried = passed
            lower = upper
        return carry

    lax.fori_loop(0, rows // 8, first_product, 0, unroll=2)

    def image_at(place, dots, own):
        dot_load, dot_zz, dot_zy = dots
        scale = inverse[place + 1]
        if not own:
            scale = jnp.where(slab < slabs - 1, scale, 0.0)
        for comp in range(3):
            along = [
                near_at[place, 2 * comp + mode_y] + far_at[place, 2 * comp + mode_y, 7 : rows + 7]
                for mode_y in range(2)
            ]
            image = (along[0] - along[1]) + shift_back(along[0] + along[1], 1, first_col)
            scaled = image * scale
            y_ref[comp, place] = scaled
            if own:
                value = z_ref[comp, place + 1]
                dot_load = dot_load + fold(load_ref[comp, place] * value)
                dot_zz = dot_zz + fold(value * image)
                dot_zy = dot_zy + fold(scaled * image)
            store_along_y(fields_y, place, comp, scaled, last_col)
        return dot_load, dot_zz, dot_zy

    zeros = jnp.zeros((8, cols), jnp.float32)
    dot_load, dot_zz, dot_zy = lax.fori_loop(
        0, depth, lambda place, dots: image_at(place, dots, True), (zeros,) * 3, unroll=True
    )
    image_at(depth, (zeros,) * 3, False)

    def second_product(chunk, dot_yy):
        lower = load_spread(fields_y, 0, chunk)
        for place in range(depth):
            upper = load_spread(fields_y, place + 1, chunk)
            weight = elastic[place + 2, pl.ds(chunk * 8, 8)]
            dot_yy = dot_yy + weight * modal_energy(element_modes(lower, upper))
            lower = upper
        return dot_yy

    dot_yy = lax.fori_loop(0, rows // 8, second_product, zeros, unroll=True)
    lane_at = lax.broadcasted_iota(jnp.int32, (1, cols), 1)
    packed = jnp.zeros((1, cols), jnp.float32)
    for at, part in enumerate((dot_load, dot_zz, dot_zy, dot_yy)):
        packed = jnp.where(lane_at == at, jnp.sum(part, keepdims=True), packed)
    dots_ref[...] = jnp.broadcast_to(packed, dots_ref.shape)


def solve(dots_ref):
    dots = jnp.sum(dots_ref[...], axis=0, keepdims=True)
    lane_at = lax.broadcasted_iota(jnp.int32, dots.shape, 1)
    dot_load, dot_zz, dot_zy, dot_yy = (
        jnp.sum(jnp.where(lane_at == at, dots, 0.0), axis=1, keepdims=True) for at in range(4)
    )
    first = dot_zz / dot_load
    second = dot_zy / dot_load
    third = dot_yy / dot_load
    under = third * first - second * second
    along_z = (third - first * second) / under
    along_y = (first * first - second) / under
    return dot_load * (along_z + along_y * first), along_z, along_y


def terms_kernel(dots_ref, z_ref, y_ref, growth_ref, density_ref, terms_ref, fields):
    _, along_z, along_y = solve(dots_ref)
    depth, rows, cols = density_ref.shape
    last_col = lax.broadcasted_iota(jnp.int32, (rows, cols), 1) == cols - 1
    zero_rows = jnp.zeros((8, cols), jnp.float32)
    for place in range(depth + 1):
        for comp in range(3):
            value = along_z * z_ref[comp, place + 1] + along_y * y_ref[comp, place]
            store_along_y(fields, place, comp, value, last_col)
        for at in range(6):
            fields[place, at, rows : rows + 8] = zero_rows
    for chunk in range(rows // 8):
        span = pl.ds(chunk * 8, 8)
        lower = load_spread(fields, 0, chunk)
        for place in range(depth):
            upper = load_spread(fields, place + 1, chunk)
            dense = density_ref[place, span]
            share = (-3.0 / 8.0 * UNIT) * dense * dense * growth_ref[place + 2, span]
            terms_ref[chunk, place] = share * modal_energy(element_modes(lower, upper))
            lower = upper


def last_kernel(
    terms_ref, dots_ref, z_ref, y_ref, displacement_ref, gradient_ref, compliance_ref
):
    compliance, along_z, along_y = solve(dots_ref)
    compliance_ref[...] = compliance
    gradient_ref[...] = jnp.sum(terms_ref[...], axis=0)
    for comp in range(3):
        for place in range(displacement_ref.shape[2]):
            displacement_ref[0, comp, place] = along_z * z_ref[comp, place + 1] + along_y * y_ref[comp, place]


def call(kernel, outs, inputs, scratch=(), in_memory=pltpu.VMEM, out_specs=None):
    return pl.pallas_call(
        kernel,
        out_shape=outs,
        in_specs=[pl.BlockSpec(memory_space=in_memory)] * inputs,
        out_specs=out_specs if out_specs is not None else [vmem_spec()] * len(outs),
        scratch_shapes=scratch,
        compiler_params=pltpu.CompilerParams(vmem_limit_bytes=VMEM_LIMIT),
    )


def per_device(load_field, density, mode_panels, mode_weight, mode_germs):
    depth, rows, cols = density.shape
    slabs = lax.axis_size("space")
    samples = lax.axis_size("sample")
    own_modes, _, cells = mode_panels.shape
    spread_y, spread_zx = weight_tables(depth, rows, cols)

    held_density, held_load = f32(depth, rows, cols), f32(3, depth, rows, cols)
    partial, density, load_field = call(
        first_kernel,
        [f32(samples, 2 * cells // 128, 128), held_density, held_load],
        inputs=5,
        scratch=[
            pltpu.VMEM((1, mode_weight.shape[0]), jnp.float32),
            pltpu.VMEM(mode_germs.shape, jnp.float32),
            pltpu.VMEM((own_modes, cells), jnp.bfloat16),
            pltpu.SemaphoreType.DMA((5,)),
        ],
        in_memory=pltpu.HBM,
    )(
        *(
            pltpu.with_memory_space_constraint(value, pltpu.HBM)
            for value in (
                mode_weight.reshape(1, -1),
                mode_germs,
                mode_panels.reshape(own_modes, cells),
                density,
                load_field,
            )
        )
    )
    parts = lax.all_to_all(partial, "sample", 0, 0, tiled=True)

    lines = 2 * cells // 128
    sums, message = call(pack_kernel, [f32(lines, 128), f32(8 * rows + lines, cols)], inputs=3)(
        parts, density, load_field
    )
    pairs = []
    for sample in range(samples):
        for slab in range(slabs):
            target = slab + (1 if sample % 2 == slab % 2 else -1)
            if 0 <= target < slabs:
                pairs.append((sample * slabs + slab, sample * slabs + target))
    own = lax.ppermute(message, ("sample", "space"), pairs)
    other = lax.ppermute(own, "sample", [(at, at ^ 1) for at in range(samples)])

    padded = pltpu.VMEM((depth + 1, 6, rows + 8, cols), jnp.float32)
    planes = pltpu.VMEM((depth + 4, rows, cols), jnp.float32)
    z_vec, y_vec, growth, dots = call(
        middle_kernel,
        [
            f32(3, depth + 3, rows, cols),
            f32(3, depth + 1, rows, cols),
            f32(depth + 4, rows, cols),
            f32(slabs, cols),
        ],
        inputs=7,
        scratch=[
            planes,
            planes,
            pltpu.VMEM((depth + 3, rows, cols), jnp.float32),
            pltpu.VMEM((depth + 3, 6, rows + 8, cols), jnp.float32),
            padded,
            pltpu.VMEM((depth + 1, 6, rows, cols), jnp.float32),
            padded,
        ],
    )(sums, density, load_field, own, other, spread_y, spread_zx)
    dots = lax.all_to_all(dots, "space", 0, 0, tiled=True)
    (terms,) = call(
        terms_kernel, [f32(samples, depth, rows // samples, cols)], inputs=5, scratch=[padded]
    )(dots, z_vec, y_vec, growth, density)
    terms = lax.all_to_all(terms, "sample", 0, 0, tiled=True)
    displacement, gradient, compliance = call(
        last_kernel,
        [f32(1, 3, depth, rows, cols), f32(depth, rows // samples, cols), f32(1, 1)],
        inputs=4,
    )(terms, dots, z_vec, y_vec)
    return displacement, gradient, compliance.reshape(1)


def solution(mesh):
    placed = (
        P(None, "space", None, None),
        P("space", None, None),
        P("sample", "space", None),
        P(),
        P(),
    )
    return jax.shard_map(
        per_device,
        mesh=mesh,
        in_specs=placed,
        out_specs=(P("sample", None, "space", None, None), P("space", "sample", None), P("sample")),
        check_vma=False,
    )
```

```python
import itertools

import jax
import jax.numpy as jnp
import numpy as np
from jax import lax
from jax.experimental import pallas as pl
from jax.experimental.pallas import tpu as pltpu
from jax.sharding import PartitionSpec as P

POISSON = 0.3
LAME = POISSON / ((1.0 + POISSON) * (1.0 - 2.0 * POISSON))
SHEAR = 1.0 / (2.0 * (1.0 + POISSON))
DIAGONAL = (LAME + 2.0 * SHEAR) / 9.0 + 2.0 * SHEAR / 9.0
RATIO = LAME / SHEAR
UNIT = SHEAR / 16.0
VMEM_LIMIT = 48 * 1024 * 1024


def vmem_spec():
    return pl.BlockSpec(memory_space=pltpu.VMEM)


def f32(*shape):
    return jax.ShapeDtypeStruct(shape, jnp.float32)


def split3(value):
    high = value.astype(jnp.bfloat16)
    rest = value - high.astype(jnp.float32)
    mid = rest.astype(jnp.bfloat16)
    low = (rest - mid.astype(jnp.float32)).astype(jnp.bfloat16)
    return high, mid, low


def dot32(left, right):
    return jnp.dot(left, right, preferred_element_type=jnp.float32)


def weight_tables(depth, rows, cols):
    def hat(positions, cells):
        return np.maximum(0.0, 1.0 - np.abs(positions[:, None] - cells[None, :]))

    along_x = hat((np.arange(rows) + 0.5) / 4.0 - 0.5, np.arange(rows // 4))
    along_y = hat((np.arange(cols) + 0.5) / 4.0 - 0.5, np.arange(cols // 4))
    along_z = hat((np.arange(depth + 4) - 2 + 0.5) / 4.0 - 0.5, np.arange(-1, 2))
    spread_y = np.tile(along_y.T, (4, 1))
    spread_zx = np.einsum("pc,xd->pxcd", along_z, along_x).reshape((depth + 4) * rows, -1)
    return spread_y.astype(jnp.bfloat16), spread_zx.astype(jnp.bfloat16)


def first_kernel(
    weight_hbm, germs_hbm, panels_hbm, density_hbm, load_hbm,
    partial_ref, density_ref, load_ref,
    weight, germs, panels, sems,
):
    sample = lax.axis_index("sample")
    copies = [
        pltpu.make_async_copy(source, target, sems.at[at])
        for at, (source, target) in enumerate(
            (
                (weight_hbm, weight),
                (germs_hbm, germs),
                (panels_hbm, panels),
                (density_hbm, density_ref),
                (load_hbm, load_ref),
            )
        )
    ]
    for copy in copies:
        copy.start()
    own_modes = panels.shape[0]
    modes = germs.shape[1]
    mode_at = lax.broadcasted_iota(jnp.int32, (modes, own_modes), 0)
    slot_at = lax.broadcasted_iota(jnp.int32, (modes, own_modes), 1)
    pick = jnp.where(mode_at == slot_at + sample * own_modes, 1.0, 0.0).astype(jnp.bfloat16)
    for copy in copies[:3]:
        copy.wait()
    coefficients = (weight[...] * germs[...]).astype(jnp.bfloat16)
    own_coeff = dot32(coefficients, pick).astype(jnp.bfloat16)
    partial = dot32(own_coeff, panels[...])
    lines = partial_ref.shape[1] // 2
    for target in range(partial_ref.shape[0]):
        for at in range(2 * lines):
            row, line = target // 2 * 2 + at // lines, at % lines
            partial_ref[target, at : at + 1] = partial[row : row + 1, line * 128 : (line + 1) * 128]
    for copy in copies[3:]:
        copy.wait()


def towards_above():
    core, slab = lax.axis_index("sample") % 2, lax.axis_index("space")
    return core == slab % 2


def pack_kernel(parts_ref, density_ref, load_ref, sums_ref, message_ref):
    rows = density_ref.shape[1]
    depth = density_ref.shape[0]
    sums = jnp.sum(parts_ref[...], axis=0)
    sums_ref[...] = sums
    message_ref[message_ref.shape[0] - sums.shape[0] :] = sums

    def fill(parts):
        for at in range(8):
            part = parts[at] if at < len(parts) else jnp.zeros_like(parts[0])
            message_ref[at * rows : (at + 1) * rows] = part

    @pl.when(towards_above())
    def _():
        up = [density_ref[depth - 2], density_ref[depth - 1]]
        fill(up + [load_ref[comp, depth - 1] for comp in range(3)])

    @pl.when(jnp.logical_not(towards_above()))
    def _():
        down = [density_ref[0], density_ref[1]]
        fill(down + [load_ref[comp, place] for comp in range(3) for place in range(2)])


def shift_ahead(value, axis, mask):
    return jnp.where(mask, 0.0, pltpu.roll(value, value.shape[axis] - 1, axis))


def shift_back(value, axis, mask):
    return jnp.where(mask, 0.0, pltpu.roll(value, 1, axis))


def store_along_y(target, place, comp, value, last_col):
    ahead = shift_ahead(value, 1, last_col)
    target[place, 2 * comp, 0 : value.shape[0]] = value + ahead
    target[place, 2 * comp + 1, 0 : value.shape[0]] = ahead - value


def load_spread(source, place, chunk):
    parts = []
    for comp in range(3):
        here = [source[place, 2 * comp + mode, pl.ds(chunk * 8, 8)] for mode in range(2)]
        ahead = [source[place, 2 * comp + mode, pl.ds(chunk * 8 + 1, 8)] for mode in range(2)]
        parts += [one + two for one, two in zip(here, ahead)]
        parts += [two - one for one, two in zip(here, ahead)]
    return parts


def element_modes(lower, upper):
    hat = {}
    for comp in range(3):
        for mode_x, mode_y in itertools.product((0, 1), repeat=2):
            at = 4 * comp + 2 * mode_x + mode_y
            if mode_x or mode_y:
                hat[comp, (0, mode_x, mode_y)] = lower[at] + upper[at]
            hat[comp, (1, mode_x, mode_y)] = upper[at] - lower[at]
    return hat


def mode(*axes):
    return tuple(int(axis in axes) for axis in range(3))


def modal_parts(hat):
    shear = {
        (one, two): hat[one, mode(two)] + hat[two, mode(one)] for one, two in ((0, 1), (0, 2), (1, 2))
    }
    trace = hat[0, mode(0)] + hat[1, mode(1)] + hat[2, mode(2)]
    twist = [hat[axis, mode(*(other for other in range(3) if other != axis))] for axis in range(3)]
    bends = {}
    for across in range(3):
        one, two = (axis for axis in range(3) if axis != across)
        bends[across] = (one, two, hat[one, mode(one, across)] + hat[two, mode(two, across)])
    return shear, trace, twist, bends


def modal_forces(hat, weight):
    shear, trace, twist, bends = modal_parts(hat)
    forces = {}
    for (one, two), value in shear.items():
        forces[one, mode(two)] = forces[two, mode(one)] = value * weight
    level = RATIO * trace
    for axis in range(3):
        forces[axis, mode(axis)] = (2.0 * hat[axis, mode(axis)] + level) * weight
    third = (1.0 / 3.0) * weight
    both = twist[0] + twist[1] + twist[2]
    for axis in range(3):
        place = mode(*(other for other in range(3) if other != axis))
        forces[axis, place] = (twist[axis] + both) * third
    for across, (one, two, total) in bends.items():
        extra = (RATIO / 3.0) * total
        for axis in (one, two):
            place = mode(axis, across)
            forces[axis, place] = (hat[axis, place] + extra) * weight
    last = ((RATIO + 4.0) / 9.0) * weight
    for axis in range(3):
        forces[axis, (1, 1, 1)] = hat[axis, (1, 1, 1)] * last
    return forces


def total_of(values):
    values = list(values)
    while len(values) > 1:
        paired = [one + two for one, two in zip(values[::2], values[1::2])]
        values = paired + ([values[-1]] if len(values) % 2 else [])
    return values[0]


def modal_product(left, right):
    return total_of(left[key] * value for key, value in right.items())


def modal_energy(hat):
    shear, trace, twist, bends = modal_parts(hat)

    def squares(values):
        return total_of(value * value for value in values)

    both = twist[0] + twist[1] + twist[2]
    whole = list(shear.values())
    for across, (one, two, _) in bends.items():
        whole += [hat[one, mode(one, across)], hat[two, mode(two, across)]]
    return total_of(
        [
            squares(whole),
            2.0 * squares(hat[axis, mode(axis)] for axis in range(3)),
            RATIO * (trace * trace),
            (1.0 / 3.0) * squares(twist + [both]),
            (RATIO / 3.0) * squares(total for _, _, total in bends.values()),
            ((RATIO + 4.0) / 9.0) * squares(hat[axis, (1, 1, 1)] for axis in range(3)),
        ]
    )


def fold(plane):
    return jnp.sum(plane.reshape(-1, 8, plane.shape[-1]), axis=0)


def middle_kernel(
    sums_ref, density_ref, load_ref, own_ref, other_ref, spread_y_ref, spread_zx_ref,
    z_ref, y_ref, growth_ref, dots_ref,
    elastic, around, inverse, fields, fields_y, near_at, far_at,
):
    slab = lax.axis_index("space")
    slabs = lax.axis_size("space")
    depth, rows, cols = density_ref.shape
    row_at = lax.broadcasted_iota(jnp.int32, (rows, cols), 0)
    col_at = lax.broadcasted_iota(jnp.int32, (rows, cols), 1)
    first_row = row_at == 0
    first_col, last_col = col_at == 0, col_at == cols - 1
    cells = sums_ref.shape[0] // 2
    core = lax.axis_index("sample") % 2
    extra = own_ref.shape[0] - 2 * cells
    own_above = towards_above()

    def from_below(span):
        return jnp.where(own_above, other_ref[span], own_ref[span])

    def from_above(span):
        return jnp.where(own_above, own_ref[span], other_ref[span])

    def own_sample(lines):
        return jnp.where(core == 0, lines[0:cells], lines[cells:])

    def plane(place):
        return pl.ds(place * rows, rows)

    coarse_x, coarse_y = rows // 4, cols // 4
    fold_x = coarse_x // cells
    line_at = lax.broadcasted_iota(jnp.int32, (coarse_x, cols), 0)
    cell_at = lax.broadcasted_iota(jnp.int32, (coarse_x, cols), 1)
    on_line = cell_at // coarse_y == line_at % fold_x
    lines = []
    last = pl.ds(extra, 2 * cells)
    for both in (from_below(last), sums_ref[...], from_above(last)):
        coarse = own_sample(both)
        tall = jnp.zeros((coarse_x, cols), jnp.float32)
        for at in range(cells):
            tall = jnp.where(line_at // fold_x == at, coarse[at : at + 1], tall)
        lines.append(jnp.where(on_line, tall, 0.0))
    lines = jnp.concatenate(lines, axis=0)
    spread_y = spread_y_ref[...]
    high, mid, low = (dot32(part, spread_y) for part in split3(lines))
    along_y = high + (mid + low)
    spread_zx = spread_zx_ref[...]
    high, mid, low = (dot32(spread_zx, part) for part in split3(along_y))
    growth_ref[...] = jnp.exp(high + (mid + low)).reshape(depth + 4, rows, cols)

    def dense_at(place):
        if place < 2:
            return from_below(plane(place))
        return density_ref[place - 2] if place < depth + 2 else from_above(plane(place - depth - 2))

    def load_at(comp, place):
        if place < 2:
            return from_below(plane(2 + comp))
        if place < depth + 2:
            return load_ref[comp, place - 2]
        return from_above(plane(2 + 2 * comp + place - depth - 2))

    zero_rows = jnp.zeros((8, cols), jnp.float32)
    for target, first in ((fields, rows), (fields_y, rows), (far_at, 0)):
        for place, at in itertools.product(range(target.shape[0]), range(6)):
            target[place, at, first : first + 8] = zero_rows

    for place in range(depth + 4):
        dense = dense_at(place)
        modulus = growth_ref[place] * (0.001 + dense * dense * dense)
        if place < 2:
            modulus = modulus * jnp.where(slab == 0, 0.0, UNIT)
        elif place >= depth + 2:
            modulus = modulus * jnp.where(slab == slabs - 1, 0.0, UNIT)
        else:
            modulus = modulus * UNIT
        elastic[place] = modulus
        along = modulus + shift_back(modulus, 1, first_col)
        around[place] = along + shift_back(along, 0, first_row)

    for place in range(1, depth + 4):
        diagonal = (DIAGONAL / UNIT) * (around[place - 1] + around[place])
        if place == 1:
            diagonal = jnp.where(slab == 0, 1.0, diagonal)
        if place == depth + 3:
            diagonal = jnp.where(slab == slabs - 1, 1.0, diagonal)
        inverse_here = 1.0 / diagonal
        inverse[place - 1] = inverse_here
        for comp in range(3):
            value = load_at(comp, place) * inverse_here
            z_ref[comp, place - 1] = value
            store_along_y(fields, place - 1, comp, value, last_col)

    def first_product(chunk, carry):
        lower = load_spread(fields, 0, chunk)
        carried = None
        for place in range(1, depth + 3):
            upper = load_spread(fields, place, chunk)
            forces = modal_forces(element_modes(lower, upper), elastic[place, pl.ds(chunk * 8, 8)])
            passed = []
            for comp in range(3):
                sums = []
                for mode_x, mode_y in itertools.product((0, 1), repeat=2):
                    rise = forces[comp, (1, mode_x, mode_y)]
                    if mode_x or mode_y:
                        level = forces[comp, (0, mode_x, mode_y)]
                        near, far = level - rise, level + rise
                    else:
                        near, far = -rise, rise
                    if carried is not None:
                        sums.append(near + carried[4 * comp + 2 * mode_x + mode_y])
                    passed.append(far)
                if carried is not None:
                    for mode_y in range(2):
                        level, rise = sums[mode_y], sums[2 + mode_y]
                        near_at[place - 2, 2 * comp + mode_y, pl.ds(chunk * 8, 8)] = level - rise
                        far_at[place - 2, 2 * comp + mode_y, pl.ds(chunk * 8 + 8, 8)] = level + rise
            carried = passed
            lower = upper
        return carry

    lax.fori_loop(0, rows // 8, first_product, 0, unroll=2)

    def image_at(place, dots, own):
        dot_load, dot_zz, dot_zy = dots
        scale = inverse[place + 1]
        if not own:
            scale = jnp.where(slab < slabs - 1, scale, 0.0)
        for comp in range(3):
            along = [
                near_at[place, 2 * comp + mode_y] + far_at[place, 2 * comp + mode_y, 7 : rows + 7]
                for mode_y in range(2)
            ]
            image = (along[0] - along[1]) + shift_back(along[0] + along[1], 1, first_col)
            scaled = image * scale
            y_ref[comp, place] = scaled
            if own:
                value = z_ref[comp, place + 1]
                dot_load = dot_load + fold(load_ref[comp, place] * value)
                dot_zz = dot_zz + fold(value * image)
                dot_zy = dot_zy + fold(scaled * image)
            store_along_y(fields_y, place, comp, scaled, last_col)
        return dot_load, dot_zz, dot_zy

    zeros = jnp.zeros((8, cols), jnp.float32)
    dot_load, dot_zz, dot_zy = lax.fori_loop(
        0, depth, lambda place, dots: image_at(place, dots, True), (zeros,) * 3, unroll=True
    )
    image_at(depth, (zeros,) * 3, False)

    def second_product(chunk, dot_yy):
        lower = load_spread(fields_y, 0, chunk)
        for place in range(depth):
            upper = load_spread(fields_y, place + 1, chunk)
            weight = elastic[place + 2, pl.ds(chunk * 8, 8)]
            dot_yy = dot_yy + weight * modal_energy(element_modes(lower, upper))
            lower = upper
        return dot_yy

    dot_yy = lax.fori_loop(0, rows // 8, second_product, zeros, unroll=True)
    lane_at = lax.broadcasted_iota(jnp.int32, (1, cols), 1)
    packed = jnp.zeros((1, cols), jnp.float32)
    for at, part in enumerate((dot_load, dot_zz, dot_zy, dot_yy)):
        packed = jnp.where(lane_at == at, jnp.sum(part, keepdims=True), packed)
    dots_ref[...] = jnp.broadcast_to(packed, dots_ref.shape)


def solve(dots_ref):
    dots = jnp.sum(dots_ref[...], axis=0, keepdims=True)
    lane_at = lax.broadcasted_iota(jnp.int32, dots.shape, 1)
    dot_load, dot_zz, dot_zy, dot_yy = (
        jnp.sum(jnp.where(lane_at == at, dots, 0.0), axis=1, keepdims=True) for at in range(4)
    )
    first = dot_zz / dot_load
    second = dot_zy / dot_load
    third = dot_yy / dot_load
    under = third * first - second * second
    along_z = (third - first * second) / under
    along_y = (first * first - second) / under
    return dot_load * (along_z + along_y * first), along_z, along_y


def terms_kernel(
    dots_ref, z_ref, y_ref, growth_ref, density_ref, terms_ref, displacement_hbm, fields, held, sem
):
    _, along_z, along_y = solve(dots_ref)
    depth, rows, cols = density_ref.shape
    last_col = lax.broadcasted_iota(jnp.int32, (rows, cols), 1) == cols - 1
    zero_rows = jnp.zeros((8, cols), jnp.float32)
    for place in range(depth + 1):
        for comp in range(3):
            value = along_z * z_ref[comp, place + 1] + along_y * y_ref[comp, place]
            store_along_y(fields, place, comp, value, last_col)
            if place < depth:
                held[comp, place] = value
        for at in range(6):
            fields[place, at, rows : rows + 8] = zero_rows
    copy = pltpu.make_async_copy(held, displacement_hbm.at[0], sem)
    copy.start()
    for chunk in range(rows // 8):
        span = pl.ds(chunk * 8, 8)
        lower = load_spread(fields, 0, chunk)
        for place in range(depth):
            upper = load_spread(fields, place + 1, chunk)
            dense = density_ref[place, span]
            share = (-3.0 / 8.0 * UNIT) * dense * dense * growth_ref[place + 2, span]
            terms_ref[chunk, place] = share * modal_energy(element_modes(lower, upper))
            lower = upper
    copy.wait()


def last_kernel(terms_ref, dots_ref, gradient_ref, compliance_ref):
    gradient_ref[...] = jnp.sum(terms_ref[...], axis=0)
    compliance_ref[...] = solve(dots_ref)[0]


def call(kernel, outs, inputs, scratch=(), in_memory=pltpu.VMEM, out_specs=None):
    return pl.pallas_call(
        kernel,
        out_shape=outs,
        in_specs=[pl.BlockSpec(memory_space=in_memory)] * inputs,
        out_specs=out_specs if out_specs is not None else [vmem_spec()] * len(outs),
        scratch_shapes=scratch,
        compiler_params=pltpu.CompilerParams(vmem_limit_bytes=VMEM_LIMIT),
    )


def per_device(load_field, density, mode_panels, mode_weight, mode_germs):
    depth, rows, cols = density.shape
    slabs = lax.axis_size("space")
    samples = lax.axis_size("sample")
    own_modes, _, cells = mode_panels.shape
    spread_y, spread_zx = weight_tables(depth, rows, cols)

    held_density, held_load = f32(depth, rows, cols), f32(3, depth, rows, cols)
    partial, density, load_field = call(
        first_kernel,
        [f32(samples, 2 * cells // 128, 128), held_density, held_load],
        inputs=5,
        scratch=[
            pltpu.VMEM((1, mode_weight.shape[0]), jnp.float32),
            pltpu.VMEM(mode_germs.shape, jnp.float32),
            pltpu.VMEM((own_modes, cells), jnp.bfloat16),
            pltpu.SemaphoreType.DMA((5,)),
        ],
        in_memory=pltpu.HBM,
    )(
        *(
            pltpu.with_memory_space_constraint(value, pltpu.HBM)
            for value in (
                mode_weight.reshape(1, -1),
                mode_germs,
                mode_panels.reshape(own_modes, cells),
                density,
                load_field,
            )
        )
    )
    parts = lax.all_to_all(partial, "sample", 0, 0, tiled=True)

    lines = 2 * cells // 128
    sums, message = call(pack_kernel, [f32(lines, 128), f32(8 * rows + lines, cols)], inputs=3)(
        parts, density, load_field
    )
    pairs = []
    for sample in range(samples):
        for slab in range(slabs):
            target = slab + (1 if sample % 2 == slab % 2 else -1)
            if 0 <= target < slabs:
                pairs.append((sample * slabs + slab, sample * slabs + target))
    own = lax.ppermute(message, ("sample", "space"), pairs)
    other = lax.ppermute(own, "sample", [(at, at ^ 1) for at in range(samples)])

    padded = pltpu.VMEM((depth + 1, 6, rows + 8, cols), jnp.float32)
    planes = pltpu.VMEM((depth + 4, rows, cols), jnp.float32)
    z_vec, y_vec, growth, dots = call(
        middle_kernel,
        [
            f32(3, depth + 3, rows, cols),
            f32(3, depth + 1, rows, cols),
            f32(depth + 4, rows, cols),
            f32(slabs, cols),
        ],
        inputs=7,
        scratch=[
            planes,
            planes,
            pltpu.VMEM((depth + 3, rows, cols), jnp.float32),
            pltpu.VMEM((depth + 3, 6, rows + 8, cols), jnp.float32),
            padded,
            pltpu.VMEM((depth + 1, 6, rows, cols), jnp.float32),
            padded,
        ],
    )(sums, density, load_field, own, other, spread_y, spread_zx)
    dots = lax.all_to_all(dots, "space", 0, 0, tiled=True)
    terms, displacement = call(
        terms_kernel,
        [f32(samples, depth, rows // samples, cols), f32(1, 3, depth, rows, cols)],
        inputs=5,
        scratch=[
            padded,
            pltpu.VMEM((3, depth, rows, cols), jnp.float32),
            pltpu.SemaphoreType.DMA,
        ],
        out_specs=[vmem_spec(), pl.BlockSpec(memory_space=pl.ANY)],
    )(dots, z_vec, y_vec, growth, density)
    terms = lax.all_to_all(terms, "sample", 0, 0, tiled=True)
    gradient, compliance = call(
        last_kernel, [f32(depth, rows // samples, cols), f32(1, 1)], inputs=2
    )(terms, dots)
    return displacement, gradient, compliance.reshape(1)


def solution(mesh):
    placed = (
        P(None, "space", None, None),
        P("space", None, None),
        P("sample", "space", None),
        P(),
        P(),
    )
    return jax.shard_map(
        per_device,
        mesh=mesh,
        in_specs=placed,
        out_specs=(P("sample", None, "space", None, None), P("space", "sample", None), P("sample")),
        check_vma=False,
    )
```

```python
import itertools

import jax
import jax.numpy as jnp
import numpy as np
from jax import lax
from jax.experimental import pallas as pl
from jax.experimental.pallas import tpu as pltpu
from jax.sharding import PartitionSpec as P

POISSON = 0.3
LAME = POISSON / ((1.0 + POISSON) * (1.0 - 2.0 * POISSON))
SHEAR = 1.0 / (2.0 * (1.0 + POISSON))
DIAGONAL = (LAME + 2.0 * SHEAR) / 9.0 + 2.0 * SHEAR / 9.0
RATIO = LAME / SHEAR
UNIT = SHEAR / 16.0
VMEM_LIMIT = 48 * 1024 * 1024


def vmem_spec():
    return pl.BlockSpec(memory_space=pltpu.VMEM)


def f32(*shape):
    return jax.ShapeDtypeStruct(shape, jnp.float32)


def split3(value):
    high = value.astype(jnp.bfloat16)
    rest = value - high.astype(jnp.float32)
    mid = rest.astype(jnp.bfloat16)
    low = (rest - mid.astype(jnp.float32)).astype(jnp.bfloat16)
    return high, mid, low


def dot32(left, right):
    return jnp.dot(left, right, preferred_element_type=jnp.float32)


def weight_tables(depth, rows, cols):
    def hat(positions, cells):
        return np.maximum(0.0, 1.0 - np.abs(positions[:, None] - cells[None, :]))

    along_x = hat((np.arange(rows) + 0.5) / 4.0 - 0.5, np.arange(rows // 4))
    along_y = hat((np.arange(cols) + 0.5) / 4.0 - 0.5, np.arange(cols // 4))
    along_z = hat((np.arange(depth + 4) - 2 + 0.5) / 4.0 - 0.5, np.arange(-1, 2))
    spread_y = np.tile(along_y.T, (4, 1))
    spread_zx = np.einsum("pc,xd->pxcd", along_z, along_x).reshape((depth + 4) * rows, -1)
    return spread_y.astype(jnp.bfloat16), spread_zx.astype(jnp.bfloat16)


def first_kernel(
    weight_hbm, germs_hbm, panels_hbm, density_hbm, load_hbm,
    partial_ref, density_ref, load_ref,
    weight, germs, panels, sems,
):
    sample = lax.axis_index("sample")
    copies = [
        pltpu.make_async_copy(source, target, sems.at[at])
        for at, (source, target) in enumerate(
            (
                (weight_hbm, weight),
                (germs_hbm, germs),
                (panels_hbm, panels),
                (density_hbm, density_ref),
                (load_hbm, load_ref),
            )
        )
    ]
    for copy in copies:
        copy.start()
    own_modes = panels.shape[0]
    modes = germs.shape[1]
    mode_at = lax.broadcasted_iota(jnp.int32, (modes, own_modes), 0)
    slot_at = lax.broadcasted_iota(jnp.int32, (modes, own_modes), 1)
    pick = jnp.where(mode_at == slot_at + sample * own_modes, 1.0, 0.0).astype(jnp.bfloat16)
    for copy in copies[:3]:
        copy.wait()
    coefficients = (weight[...] * germs[...]).astype(jnp.bfloat16)
    own_coeff = dot32(coefficients, pick).astype(jnp.bfloat16)
    partial = dot32(own_coeff, panels[...])
    lines = partial_ref.shape[1] // 2
    for target in range(partial_ref.shape[0]):
        for at in range(2 * lines):
            row, line = target // 2 * 2 + at // lines, at % lines
            partial_ref[target, at : at + 1] = partial[row : row + 1, line * 128 : (line + 1) * 128]
    for copy in copies[3:]:
        copy.wait()


def towards_above():
    core, slab = lax.axis_index("sample") % 2, lax.axis_index("space")
    return core == slab % 2


def pack_kernel(parts_ref, density_ref, load_ref, sums_ref, message_ref):
    rows = density_ref.shape[1]
    depth = density_ref.shape[0]
    sums = jnp.sum(parts_ref[...], axis=0)
    sums_ref[...] = sums
    message_ref[message_ref.shape[0] - sums.shape[0] :] = sums

    def fill(parts):
        for at in range(8):
            part = parts[at] if at < len(parts) else jnp.zeros_like(parts[0])
            message_ref[at * rows : (at + 1) * rows] = part

    @pl.when(towards_above())
    def _():
        up = [density_ref[depth - 2], density_ref[depth - 1]]
        fill(up + [load_ref[comp, depth - 1] for comp in range(3)])

    @pl.when(jnp.logical_not(towards_above()))
    def _():
        down = [density_ref[0], density_ref[1]]
        fill(down + [load_ref[comp, place] for comp in range(3) for place in range(2)])


def shift_ahead(value, axis, mask):
    return jnp.where(mask, 0.0, pltpu.roll(value, value.shape[axis] - 1, axis))


def shift_back(value, axis, mask):
    return jnp.where(mask, 0.0, pltpu.roll(value, 1, axis))


def store_along_y(target, place, comp, value, last_col):
    ahead = shift_ahead(value, 1, last_col)
    target[place, 2 * comp, 0 : value.shape[0]] = value + ahead
    target[place, 2 * comp + 1, 0 : value.shape[0]] = ahead - value


def load_spread(source, place, chunk):
    parts = []
    for comp in range(3):
        here = [source[place, 2 * comp + mode, pl.ds(chunk * 8, 8)] for mode in range(2)]
        ahead = [source[place, 2 * comp + mode, pl.ds(chunk * 8 + 1, 8)] for mode in range(2)]
        parts += [one + two for one, two in zip(here, ahead)]
        parts += [two - one for one, two in zip(here, ahead)]
    return parts


def element_modes(lower, upper):
    hat = {}
    for comp in range(3):
        for mode_x, mode_y in itertools.product((0, 1), repeat=2):
            at = 4 * comp + 2 * mode_x + mode_y
            if mode_x or mode_y:
                hat[comp, (0, mode_x, mode_y)] = lower[at] + upper[at]
            hat[comp, (1, mode_x, mode_y)] = upper[at] - lower[at]
    return hat


def mode(*axes):
    return tuple(int(axis in axes) for axis in range(3))


def modal_parts(hat):
    shear = {
        (one, two): hat[one, mode(two)] + hat[two, mode(one)] for one, two in ((0, 1), (0, 2), (1, 2))
    }
    trace = hat[0, mode(0)] + hat[1, mode(1)] + hat[2, mode(2)]
    twist = [hat[axis, mode(*(other for other in range(3) if other != axis))] for axis in range(3)]
    bends = {}
    for across in range(3):
        one, two = (axis for axis in range(3) if axis != across)
        bends[across] = (one, two, hat[one, mode(one, across)] + hat[two, mode(two, across)])
    return shear, trace, twist, bends


def modal_forces(hat, weight):
    shear, trace, twist, bends = modal_parts(hat)
    forces = {}
    for (one, two), value in shear.items():
        forces[one, mode(two)] = forces[two, mode(one)] = value * weight
    level = RATIO * trace
    for axis in range(3):
        forces[axis, mode(axis)] = (2.0 * hat[axis, mode(axis)] + level) * weight
    third = (1.0 / 3.0) * weight
    both = twist[0] + twist[1] + twist[2]
    for axis in range(3):
        place = mode(*(other for other in range(3) if other != axis))
        forces[axis, place] = (twist[axis] + both) * third
    for across, (one, two, total) in bends.items():
        extra = (RATIO / 3.0) * total
        for axis in (one, two):
            place = mode(axis, across)
            forces[axis, place] = (hat[axis, place] + extra) * weight
    last = ((RATIO + 4.0) / 9.0) * weight
    for axis in range(3):
        forces[axis, (1, 1, 1)] = hat[axis, (1, 1, 1)] * last
    return forces


def total_of(values):
    values = list(values)
    while len(values) > 1:
        paired = [one + two for one, two in zip(values[::2], values[1::2])]
        values = paired + ([values[-1]] if len(values) % 2 else [])
    return values[0]


def modal_product(left, right):
    return total_of(left[key] * value for key, value in right.items())


def modal_energy(hat):
    shear, trace, twist, bends = modal_parts(hat)

    def squares(values):
        return total_of(value * value for value in values)

    both = twist[0] + twist[1] + twist[2]
    whole = list(shear.values())
    for across, (one, two, _) in bends.items():
        whole += [hat[one, mode(one, across)], hat[two, mode(two, across)]]
    return total_of(
        [
            squares(whole),
            2.0 * squares(hat[axis, mode(axis)] for axis in range(3)),
            RATIO * (trace * trace),
            (1.0 / 3.0) * squares(twist + [both]),
            (RATIO / 3.0) * squares(total for _, _, total in bends.values()),
            ((RATIO + 4.0) / 9.0) * squares(hat[axis, (1, 1, 1)] for axis in range(3)),
        ]
    )


def fold(plane):
    return jnp.sum(plane.reshape(-1, 8, plane.shape[-1]), axis=0)


def middle_kernel(
    sums_ref, density_ref, load_ref, own_ref, other_ref, spread_y_ref, spread_zx_ref,
    z_ref, y_ref, growth_ref, dots_ref,
    elastic, around, inverse, fields, fields_y, near_at, far_at,
):
    slab = lax.axis_index("space")
    slabs = lax.axis_size("space")
    depth, rows, cols = density_ref.shape
    row_at = lax.broadcasted_iota(jnp.int32, (rows, cols), 0)
    col_at = lax.broadcasted_iota(jnp.int32, (rows, cols), 1)
    first_row = row_at == 0
    first_col, last_col = col_at == 0, col_at == cols - 1
    cells = sums_ref.shape[0] // 2
    core = lax.axis_index("sample") % 2
    extra = own_ref.shape[0] - 2 * cells
    own_above = towards_above()

    def from_below(span):
        return jnp.where(own_above, other_ref[span], own_ref[span])

    def from_above(span):
        return jnp.where(own_above, own_ref[span], other_ref[span])

    def own_sample(lines):
        return jnp.where(core == 0, lines[0:cells], lines[cells:])

    def plane(place):
        return pl.ds(place * rows, rows)

    coarse_x, coarse_y = rows // 4, cols // 4
    fold_x = coarse_x // cells
    line_at = lax.broadcasted_iota(jnp.int32, (coarse_x, cols), 0)
    cell_at = lax.broadcasted_iota(jnp.int32, (coarse_x, cols), 1)
    on_line = cell_at // coarse_y == line_at % fold_x
    lines = []
    last = pl.ds(extra, 2 * cells)
    for both in (from_below(last), sums_ref[...], from_above(last)):
        coarse = own_sample(both)
        tall = jnp.zeros((coarse_x, cols), jnp.float32)
        for at in range(cells):
            tall = jnp.where(line_at // fold_x == at, coarse[at : at + 1], tall)
        lines.append(jnp.where(on_line, tall, 0.0))
    lines = jnp.concatenate(lines, axis=0)
    spread_y = spread_y_ref[...]
    high, mid, low = (dot32(part, spread_y) for part in split3(lines))
    along_y = high + (mid + low)
    spread_zx = spread_zx_ref[...]
    high, mid, low = (dot32(spread_zx, part) for part in split3(along_y))
    growth_ref[...] = jnp.exp(high + (mid + low)).reshape(depth + 4, rows, cols)

    def dense_at(place):
        if place < 2:
            return from_below(plane(place))
        return density_ref[place - 2] if place < depth + 2 else from_above(plane(place - depth - 2))

    def load_at(comp, place):
        if place < 2:
            return from_below(plane(2 + comp))
        if place < depth + 2:
            return load_ref[comp, place - 2]
        return from_above(plane(2 + 2 * comp + place - depth - 2))

    zero_rows = jnp.zeros((8, cols), jnp.float32)
    for target, first in ((fields, rows), (fields_y, rows), (far_at, 0)):
        for place, at in itertools.product(range(target.shape[0]), range(6)):
            target[place, at, first : first + 8] = zero_rows

    for place in range(depth + 4):
        dense = dense_at(place)
        modulus = growth_ref[place] * (0.001 + dense * dense * dense)
        if place < 2:
            modulus = modulus * jnp.where(slab == 0, 0.0, UNIT)
        elif place >= depth + 2:
            modulus = modulus * jnp.where(slab == slabs - 1, 0.0, UNIT)
        else:
            modulus = modulus * UNIT
        elastic[place] = modulus
        along = modulus + shift_back(modulus, 1, first_col)
        around[place] = along + shift_back(along, 0, first_row)

    for place in range(1, depth + 4):
        diagonal = (DIAGONAL / UNIT) * (around[place - 1] + around[place])
        if place == 1:
            diagonal = jnp.where(slab == 0, 1.0, diagonal)
        if place == depth + 3:
            diagonal = jnp.where(slab == slabs - 1, 1.0, diagonal)
        inverse_here = 1.0 / diagonal
        inverse[place - 1] = inverse_here
        for comp in range(3):
            value = load_at(comp, place) * inverse_here
            z_ref[comp, place - 1] = value
            store_along_y(fields, place - 1, comp, value, last_col)

    def first_product(chunk, carry):
        lower = load_spread(fields, 0, chunk)
        carried = None
        for place in range(1, depth + 3):
            upper = load_spread(fields, place, chunk)
            forces = modal_forces(element_modes(lower, upper), elastic[place, pl.ds(chunk * 8, 8)])
            passed = []
            for comp in range(3):
                sums = []
                for mode_x, mode_y in itertools.product((0, 1), repeat=2):
                    rise = forces[comp, (1, mode_x, mode_y)]
                    if mode_x or mode_y:
                        level = forces[comp, (0, mode_x, mode_y)]
                        near, far = level - rise, level + rise
                    else:
                        near, far = -rise, rise
                    if carried is not None:
                        sums.append(near + carried[4 * comp + 2 * mode_x + mode_y])
                    passed.append(far)
                if carried is not None:
                    for mode_y in range(2):
                        level, rise = sums[mode_y], sums[2 + mode_y]
                        near_at[place - 2, 2 * comp + mode_y, pl.ds(chunk * 8, 8)] = level - rise
                        far_at[place - 2, 2 * comp + mode_y, pl.ds(chunk * 8 + 8, 8)] = level + rise
            carried = passed
            lower = upper
        return carry

    lax.fori_loop(0, rows // 8, first_product, 0, unroll=2)

    def image_at(place, dots, own):
        dot_load, dot_zz, dot_zy = dots
        scale = inverse[place + 1]
        if not own:
            scale = jnp.where(slab < slabs - 1, scale, 0.0)
        for comp in range(3):
            along = [
                near_at[place, 2 * comp + mode_y] + far_at[place, 2 * comp + mode_y, 7 : rows + 7]
                for mode_y in range(2)
            ]
            image = (along[0] - along[1]) + shift_back(along[0] + along[1], 1, first_col)
            scaled = image * scale
            y_ref[comp, place] = scaled
            if own:
                value = z_ref[comp, place + 1]
                dot_load = dot_load + fold(load_ref[comp, place] * value)
                dot_zz = dot_zz + fold(value * image)
                dot_zy = dot_zy + fold(scaled * image)
            store_along_y(fields_y, place, comp, scaled, last_col)
        return dot_load, dot_zz, dot_zy

    zeros = jnp.zeros((8, cols), jnp.float32)
    dot_load, dot_zz, dot_zy = lax.fori_loop(
        0, depth, lambda place, dots: image_at(place, dots, True), (zeros,) * 3, unroll=True
    )
    image_at(depth, (zeros,) * 3, False)

    def second_product(chunk, dot_yy):
        lower = load_spread(fields_y, 0, chunk)
        for place in range(depth):
            upper = load_spread(fields_y, place + 1, chunk)
            weight = elastic[place + 2, pl.ds(chunk * 8, 8)]
            dot_yy = dot_yy + weight * modal_energy(element_modes(lower, upper))
            lower = upper
        return dot_yy

    dot_yy = lax.fori_loop(0, rows // 8, second_product, zeros, unroll=True)
    lane_at = lax.broadcasted_iota(jnp.int32, (1, cols), 1)
    packed = jnp.zeros((1, cols), jnp.float32)
    for at, part in enumerate((dot_load, dot_zz, dot_zy, dot_yy)):
        packed = jnp.where(lane_at == at, jnp.sum(part, keepdims=True), packed)
    dots_ref[...] = jnp.broadcast_to(packed, dots_ref.shape)


def solve(dots_ref):
    dots = jnp.sum(dots_ref[...], axis=0, keepdims=True)
    lane_at = lax.broadcasted_iota(jnp.int32, dots.shape, 1)
    dot_load, dot_zz, dot_zy, dot_yy = (
        jnp.sum(jnp.where(lane_at == at, dots, 0.0), axis=1, keepdims=True) for at in range(4)
    )
    first = dot_zz / dot_load
    second = dot_zy / dot_load
    third = dot_yy / dot_load
    under = third * first - second * second
    along_z = (third - first * second) / under
    along_y = (first * first - second) / under
    return dot_load * (along_z + along_y * first), along_z, along_y


def terms_kernel(
    dots_ref, z_ref, y_ref, growth_ref, density_ref, terms_ref, displacement_hbm, fields, held, sems
):
    _, along_z, along_y = solve(dots_ref)
    depth, rows, cols = density_ref.shape
    last_col = lax.broadcasted_iota(jnp.int32, (rows, cols), 1) == cols - 1
    zero_rows = jnp.zeros((8, cols), jnp.float32)
    copies = []
    for comp in range(3):
        for place in range(depth + 1):
            value = along_z * z_ref[comp, place + 1] + along_y * y_ref[comp, place]
            store_along_y(fields, place, comp, value, last_col)
            if place < depth:
                held[comp, place] = value
        copies.append(
            pltpu.make_async_copy(held.at[comp], displacement_hbm.at[0, comp], sems.at[comp])
        )
        copies[-1].start()
    for place in range(depth + 1):
        for at in range(6):
            fields[place, at, rows : rows + 8] = zero_rows
    for chunk in range(rows // 8):
        span = pl.ds(chunk * 8, 8)
        lower = load_spread(fields, 0, chunk)
        for place in range(depth):
            upper = load_spread(fields, place + 1, chunk)
            dense = density_ref[place, span]
            share = (-3.0 / 8.0 * UNIT) * dense * dense * growth_ref[place + 2, span]
            terms_ref[chunk, place] = share * modal_energy(element_modes(lower, upper))
            lower = upper
    for copy in copies:
        copy.wait()


def last_kernel(terms_ref, dots_ref, gradient_ref, compliance_ref):
    gradient_ref[...] = jnp.sum(terms_ref[...], axis=0)
    compliance_ref[...] = solve(dots_ref)[0]


def call(kernel, outs, inputs, scratch=(), in_memory=pltpu.VMEM, out_specs=None):
    return pl.pallas_call(
        kernel,
        out_shape=outs,
        in_specs=[pl.BlockSpec(memory_space=in_memory)] * inputs,
        out_specs=out_specs if out_specs is not None else [vmem_spec()] * len(outs),
        scratch_shapes=scratch,
        compiler_params=pltpu.CompilerParams(vmem_limit_bytes=VMEM_LIMIT),
    )


def per_device(load_field, density, mode_panels, mode_weight, mode_germs):
    depth, rows, cols = density.shape
    slabs = lax.axis_size("space")
    samples = lax.axis_size("sample")
    own_modes, _, cells = mode_panels.shape
    spread_y, spread_zx = weight_tables(depth, rows, cols)

    held_density, held_load = f32(depth, rows, cols), f32(3, depth, rows, cols)
    partial, density, load_field = call(
        first_kernel,
        [f32(samples, 2 * cells // 128, 128), held_density, held_load],
        inputs=5,
        scratch=[
            pltpu.VMEM((1, mode_weight.shape[0]), jnp.float32),
            pltpu.VMEM(mode_germs.shape, jnp.float32),
            pltpu.VMEM((own_modes, cells), jnp.bfloat16),
            pltpu.SemaphoreType.DMA((5,)),
        ],
        in_memory=pltpu.HBM,
    )(
        *(
            pltpu.with_memory_space_constraint(value, pltpu.HBM)
            for value in (
                mode_weight.reshape(1, -1),
                mode_germs,
                mode_panels.reshape(own_modes, cells),
                density,
                load_field,
            )
        )
    )
    parts = lax.all_to_all(partial, "sample", 0, 0, tiled=True)

    lines = 2 * cells // 128
    sums, message = call(pack_kernel, [f32(lines, 128), f32(8 * rows + lines, cols)], inputs=3)(
        parts, density, load_field
    )
    pairs = []
    for sample in range(samples):
        for slab in range(slabs):
            target = slab + (1 if sample % 2 == slab % 2 else -1)
            if 0 <= target < slabs:
                pairs.append((sample * slabs + slab, sample * slabs + target))
    own = lax.ppermute(message, ("sample", "space"), pairs)
    other = lax.ppermute(own, "sample", [(at, at ^ 1) for at in range(samples)])

    padded = pltpu.VMEM((depth + 1, 6, rows + 8, cols), jnp.float32)
    planes = pltpu.VMEM((depth + 4, rows, cols), jnp.float32)
    z_vec, y_vec, growth, dots = call(
        middle_kernel,
        [
            f32(3, depth + 3, rows, cols),
            f32(3, depth + 1, rows, cols),
            f32(depth + 4, rows, cols),
            f32(slabs, cols),
        ],
        inputs=7,
        scratch=[
            planes,
            planes,
            pltpu.VMEM((depth + 3, rows, cols), jnp.float32),
            pltpu.VMEM((depth + 3, 6, rows + 8, cols), jnp.float32),
            padded,
            pltpu.VMEM((depth + 1, 6, rows, cols), jnp.float32),
            padded,
        ],
    )(sums, density, load_field, own, other, spread_y, spread_zx)
    dots = lax.all_to_all(dots, "space", 0, 0, tiled=True)
    terms, displacement = call(
        terms_kernel,
        [f32(samples, depth, rows // samples, cols), f32(1, 3, depth, rows, cols)],
        inputs=5,
        scratch=[
            padded,
            pltpu.VMEM((3, depth, rows, cols), jnp.float32),
            pltpu.SemaphoreType.DMA((3,)),
        ],
        out_specs=[vmem_spec(), pl.BlockSpec(memory_space=pl.ANY)],
    )(dots, z_vec, y_vec, growth, density)
    terms = lax.all_to_all(terms, "sample", 0, 0, tiled=True)
    gradient, compliance = call(
        last_kernel, [f32(depth, rows // samples, cols), f32(1, 1)], inputs=2
    )(terms, dots)
    return displacement, gradient, compliance.reshape(1)


def solution(mesh):
    placed = (
        P(None, "space", None, None),
        P("space", None, None),
        P("sample", "space", None),
        P(),
        P(),
    )
    return jax.shard_map(
        per_device,
        mesh=mesh,
        in_specs=placed,
        out_specs=(P("sample", None, "space", None, None), P("space", "sample", None), P("sample")),
        check_vma=False,
    )
```
